32 devices in a mesh: dp: 8 (over z, y), tensor: 4 (over x, core).
Axes of the slice: x: 2, y: 2, z: 4, core: 2. Of those that a mesh axis runs over, the one named last changes fastest.
Arguments:
- layer_input: bfloat16 [8192, 2048], P(('dp', 'tensor')), may hold values from -6 to 6
- cotangent: bfloat16 [8192, 2048], P(('dp', 'tensor')), may hold values from -6 to 6
- starts: int32 [8, 2], P('dp'), may hold values from 0 to 768, as said below
- pieces: int32 [8192], P('dp'), may hold values from -1 to 1, as said below
- norm_attn: float32 [2048], replicated, may hold values from 0.5 to 1.5
- w_query: bfloat16 [2048, 2048], P(None, 'tensor'), may hold values from -0.125 to 0.125
- w_key: bfloat16 [2048, 256], P(None, 'tensor'), may hold values from -0.125 to 0.125
- w_value: bfloat16 [2048, 256], P(None, 'tensor'), may hold values from -0.125 to 0.125
- w_out: bfloat16 [2048, 2048], P('tensor'), may hold values from -0.75 to 0.75
- norm_mlp: float32 [2048], replicated, may hold values from 0.5 to 1.5
- w_gate: bfloat16 [2048, 5632], P(None, 'tensor'), may hold values from -0.125 to 0.125
- w_up: bfloat16 [2048, 5632], P(None, 'tensor'), may hold values from -0.125 to 0.125
- w_down: bfloat16 [5632, 2048], P('tensor'), may hold values from -0.078125 to 0.078125
Outputs:
- block_out: bfloat16 [8192, 2048], P(('dp', 'tensor'))
- x_grad: float32 [8192, 2048], P(('dp', 'tensor'))
- norm_attn_grad: float32 [2048], P(('dp', 'tensor'))
- w_query_grad: float32 [2048, 2048], P('dp', 'tensor')
- w_key_grad: float32 [2048, 256], P('dp', 'tensor')
- w_value_grad: float32 [2048, 256], P('dp', 'tensor')
- w_out_grad: float32 [2048, 2048], P('tensor', 'dp')
- norm_mlp_grad: float32 [2048], P(('dp', 'tensor'))
- w_gate_grad: float32 [2048, 5632], P('dp', 'tensor')
- w_up_grad: float32 [2048, 5632], P('dp', 'tensor')
- w_down_grad: float32 [5632, 2048], P('tensor', 'dp')
The draws below stay inside these ranges and needn't reach their ends.
Inputs may be any that keep to these rules, and one draw needn't show every extreme that they name: `starts`: pictures of a sequence don't intersect and lie inside it. pieces of a token is the k with starts[its sequence, k] <= its position < starts[its sequence, k] + 256, or -1 outside every picture.
All inputs are finite; a program needn't handle non-finite values.
Results may differ from the reference program's by a relative error of at most 0.02.
Values may be sent and summed in bfloat16 or wider, within the bound.
No kernel may reach another device: no remote copies, remote signals or barrier semaphores. Data moves between devices by JAX's collectives and lax.ppermute only.
A program may use at most 384 MiB of HBM per device.

```python
import math
import jax
import jax.numpy as jnp
from jax import lax

D = 2048
H = 32
KV = 4
HD = 64
FF = 5632
SEQ = 1024
PIECE = 256
PICS = 2
NSEQS = 8
TOKENS = 8192


def picture_starts(key):
    region = SEQ // PICS
    offsets = jax.random.randint(jax.random.fold_in(key, 7), (NSEQS, PICS), 0, region - PIECE + 1)
    return (offsets + jnp.arange(PICS, dtype=jnp.int32)[None, :] * region).astype(jnp.int32)


def draw_starts(key, part):
    return picture_starts(key)


def draw_pieces(key, part):
    begins = picture_starts(key)
    positions = jnp.arange(SEQ, dtype=jnp.int32)
    inside = (positions[None, None, :] >= begins[:, :, None]) & (positions[None, None, :] < begins[:, :, None] + PIECE)
    numbers = jnp.arange(PICS, dtype=jnp.int32)[None, :, None]
    found = jnp.sum(jnp.where(inside, numbers + 1, 0), axis=1).astype(jnp.int32)
    return (found - 1).reshape(NSEQS * SEQ).astype(jnp.int32)


def raised(array, key, source, target, parts, factor):
    def block_of(axis_at):
        return (jnp.arange(array.shape[axis_at]) // (array.shape[axis_at] // parts)).reshape((-1,) + (1,) * (array.ndim - 1 - axis_at))

    near = jax.random.permutation(key, parts)[block_of(target)]
    second = (block_of(target) + parts // 2) % parts
    return jnp.where((block_of(source) == near) | (block_of(source) == second), factor * array, array)


def level_of(key, shape, shards, low, largest):
    factor_of, own = 1.0, jax.random.fold_in(key, 6)
    for dim, shards_of in shards:
        draws = jnp.exp(jax.random.uniform(jax.random.fold_in(own, dim), (shards_of,), jnp.float32, low / len(shards), largest / len(shards)))
        factor_of = factor_of * jnp.repeat(draws, shape[dim] // shards_of).reshape([-1 if axis == dim else 1 for axis in range(len(shape))])
    return factor_of


def scatter_about(rng, extent, width, reach, shards=(), held_as=jnp.bfloat16):
    values = width * jax.random.normal(rng, extent, jnp.float32)
    if shards:
        values = values * level_of(rng, extent, shards, -0.22, 0.18)
    return jnp.clip(values, -reach, reach).astype(held_as)


def bell_draw_with(rng, dims, deviation, most, cuts, heavy, kind=jnp.bfloat16):
    entries = deviation * jax.random.normal(rng, dims, jnp.float32)
    if cuts:
        entries = entries * level_of(rng, dims, cuts, -0.22, 0.18)
    return jnp.clip(raised(entries, jax.random.fold_in(rng, 3), *heavy), -most, most).astype(kind)


def setup_inputs(seed: int = 0) -> dict:
    arg_keys = jax.random.split(jax.random.key(seed), 14)
    return {
        "layer_input": scatter_about(arg_keys[0], (TOKENS, D), 1.0, 6.0, ((0, 32),)),
        "cotangent": bell_draw_with(arg_keys[1], (TOKENS, D), 1.0, 6.0, ((0, 32),), (0, 1, 32, 2.75)),
        "starts": draw_starts(jax.random.fold_in(arg_keys[13], 71), 0),
        "pieces": draw_pieces(jax.random.fold_in(arg_keys[13], 71), 0),
        "norm_attn": jnp.clip(1.0 + 0.1 * jax.random.normal(arg_keys[4], (D,), jnp.float32), 0.5, 1.5),
        "w_query": scatter_about(arg_keys[5], (D, H * HD), D ** -0.5, 0.125, ((1, 4),)),
        "w_key": scatter_about(arg_keys[6], (D, KV * HD), D ** -0.5, 0.125, ((1, 4),)),
        "w_value": scatter_about(arg_keys[7], (D, KV * HD), D ** -0.5, 0.125, ((1, 4),)),
        "w_out": scatter_about(arg_keys[8], (H * HD, D), (H * HD // 32) ** -0.5, 0.75, ((0, 4),)),
        "norm_mlp": jnp.clip(1.0 + 0.1 * jax.random.normal(arg_keys[9], (D,), jnp.float32), 0.5, 1.5),
        "w_gate": scatter_about(arg_keys[10], (D, FF), D ** -0.5, 0.125, ((1, 4),)),
        "w_up": scatter_about(arg_keys[11], (D, FF), D ** -0.5, 0.125, ((1, 4),)),
        "w_down": scatter_about(arg_keys[12], (FF, D), FF ** -0.5, 0.078125, ((0, 4),)),
    }


@jax.custom_vjp
def low(v):
    return lax.optimization_barrier(v.astype(jnp.bfloat16)).astype(jnp.float32)

@jax.custom_vjp
def low_back(v):
    return v

def low_keep(v):
    return (low(v), None)

def low_pass(kept, grad):
    return (grad,)

def back_keep(v):
    return (v, None)

def back_low(kept, grad):
    return (low(grad),)
low.defvjp(low_keep, low_pass)
low_back.defvjp(back_keep, back_low)
EPSILON = 1e-05
ROPE_BASE = 10000.0
MASKED = -1e+30

def matmul(left, right):
    return jnp.dot(left, right, precision=lax.Precision.HIGHEST, preferred_element_type=jnp.float32)

def rope_tables(count, head_dim, seq_len):
    half_dim = head_dim // 2
    positions = (jnp.arange(count, dtype=jnp.int32) % seq_len).astype(jnp.float32)
    inverse = jnp.power(ROPE_BASE, -(jnp.arange(half_dim).astype(jnp.float32) * 2.0) / head_dim)
    angles = positions[:, None] * inverse[None, :]
    return (jnp.cos(angles)[:, None, :], jnp.sin(angles)[:, None, :])

def rotate(value, cos_tab, sin_tab):
    half_dim = value.shape[-1] // 2
    first = value[..., :half_dim]
    second = value[..., half_dim:]
    return jnp.concatenate([first * cos_tab - second * sin_tab, second * cos_tab + first * sin_tab], axis=-1)

def visible(row_pos, row_piece, seq_starts, length, piece_len):
    numbers = jnp.arange(seq_starts.shape[0], dtype=jnp.int32)
    hit = row_piece[:, None] == numbers[None, :]
    begin = lax.optimization_barrier(jnp.sum(jnp.where(hit, seq_starts[None, :], 0), axis=1)).astype(jnp.int32)
    inside = row_piece >= 0
    low_end = jnp.where(inside, begin, 0)
    high_end = jnp.where(inside, begin + piece_len, 0)
    columns = jnp.arange(length, dtype=jnp.int32)
    return (columns[None, :] <= row_pos[:, None]) | (columns[None, :] >= low_end[:, None]) & (columns[None, :] < high_end[:, None])

def attend_sequence(q_seq, k_seq, v_seq, piece_seq, starts_seq):
    block = min(512, SEQ)
    count = SEQ // block
    ratio = H // KV
    q_blocks = q_seq.reshape(count, block, KV, ratio, HD)
    piece_blocks = piece_seq.reshape(count, block)
    pos_blocks = jnp.arange(SEQ, dtype=jnp.int32).reshape(count, block)

    def one_block(items):
        q_blk, row_piece, row_pos = items
        mask = visible(row_pos, row_piece, starts_seq, SEQ, PIECE)
        scores = low_back(jnp.einsum('qkrd,skd->krqs', q_blk, k_seq, precision=lax.Precision.HIGHEST))
        masked = jnp.where(mask[None, None], scores, MASKED)
        row_max = lax.optimization_barrier(jnp.max(masked, axis=-1, keepdims=True))
        exp_terms = jnp.exp(masked - row_max)
        probs = low(exp_terms / lax.optimization_barrier(jnp.sum(exp_terms, axis=-1, keepdims=True)))
        return jnp.einsum('krqs,skd->qkrd', probs, v_seq, precision=lax.Precision.HIGHEST)
    outs = lax.map(jax.checkpoint(one_block), (q_blocks, piece_blocks, pos_blocks))
    return outs.reshape(SEQ, H * HD)

def forward(params, x_group, piece_group, starts_group):
    norm_attn, w_query, w_key, w_value, w_out, norm_mlp, w_gate, w_up, w_down = params
    count = x_group.shape[0]
    seq_count = starts_group.shape[0]
    cos_tab, sin_tab = rope_tables(count, HD, SEQ)
    inv_attn = lax.rsqrt(lax.optimization_barrier(jnp.mean(x_group * x_group, axis=-1, keepdims=True)) + EPSILON)
    normed_attn = low(x_group * inv_attn * norm_attn)
    query = low_back(matmul(normed_attn, w_query)).reshape(count, H, HD)
    key = low_back(matmul(normed_attn, w_key)).reshape(count, KV, HD)
    value = low(low_back(matmul(normed_attn, w_value))).reshape(count, KV, HD)
    q_low = low(rotate(query, cos_tab, sin_tab) * HD ** (-0.5))
    k_low = low(rotate(key, cos_tab, sin_tab))
    attn = jax.vmap(attend_sequence)(q_low.reshape(seq_count, SEQ, H, HD), k_low.reshape(seq_count, SEQ, KV, HD), value.reshape(seq_count, SEQ, KV, HD), piece_group.reshape(seq_count, SEQ), starts_group)
    attn_low = low(low_back(attn.reshape(count, H * HD)))
    resid_mid = x_group + low_back(matmul(attn_low, w_out))
    inv_mlp = lax.rsqrt(lax.optimization_barrier(jnp.mean(resid_mid * resid_mid, axis=-1, keepdims=True)) + EPSILON)
    normed_mlp = low(resid_mid * inv_mlp * norm_mlp)
    gate_val = low_back(matmul(normed_mlp, w_gate))
    up_val = low_back(matmul(normed_mlp, w_up))
    hidden = low(gate_val * jax.nn.sigmoid(gate_val) * up_val)
    return resid_mid + low_back(matmul(hidden, w_down))

def reference(layer_input, cotangent, starts, pieces, norm_attn, w_query, w_key, w_value, w_out, norm_mlp, w_gate, w_up, w_down):
    params = tuple((item.astype(jnp.float32) for item in (norm_attn, w_query, w_key, w_value, w_out, norm_mlp, w_gate, w_up, w_down)))
    group = math.gcd(NSEQS, max(1, 4096 // SEQ))
    rounds = NSEQS // group
    x_steps = layer_input.astype(jnp.float32).reshape(rounds, group * SEQ, D)
    cot_steps = cotangent.astype(jnp.float32).reshape(rounds, group * SEQ, D)
    piece_steps = pieces.reshape(rounds, group * SEQ)
    start_steps = starts.reshape(rounds, group, PICS)

    def one_step(totals, items):
        x_group, cot_group, piece_group, starts_group = items
        output, pull = jax.vjp(lambda prm, xin: forward(prm, xin, piece_group, starts_group), params, x_group)
        grad_params, grad_x = pull(cot_group)
        totals = jax.tree.map(lambda left, right: left + right, totals, grad_params)
        return (totals, (output.astype(jnp.bfloat16), grad_x))
    zeros = tuple((jnp.zeros_like(item) for item in params))
    totals, (outputs, grads) = lax.scan(one_step, zeros, (x_steps, cot_steps, piece_steps, start_steps))
    return (outputs.reshape(TOKENS, D), grads.reshape(TOKENS, D), totals[0], totals[1], totals[2], totals[3], totals[4], totals[5], totals[6], totals[7], totals[8])
```

```python
import functools

import jax
import jax.numpy as jnp
from jax import lax
from jax.experimental import pallas as pl
from jax.experimental.pallas import tpu as pltpu
from jax.sharding import PartitionSpec as P

HD = 64
SEQ = 1024
PIECE = 256
QB = 256


EPSILON = 1e-05
ROPE_BASE = 10000.0
MASKED = -1e30
VMEM_LIMIT = 48 * 2**20
NT = (((1,), (1,)), ((), ()))
TN = (((0,), (0,)), ((), ()))


def dot(left, right):
    return jnp.dot(left, right, preferred_element_type=jnp.float32)


def contract_rows(left, right):
    return lax.dot_general(left, right, TN, preferred_element_type=jnp.float32)


def contract_cols(left, right):
    return lax.dot_general(left, right, NT, preferred_element_type=jnp.float32)


def rms_inverse(resid):
    return lax.rsqrt(jnp.mean(resid * resid, axis=-1, keepdims=True) + EPSILON)


def norm_back(d_norm, resid, inverse, gain):
    scaled = d_norm * gain
    return inverse * scaled - resid * (inverse * inverse * inverse) * jnp.mean(
        scaled * resid, axis=-1, keepdims=True
    )


def rope_tables(positions):
    half_dim = HD // 2
    inverse = jnp.power(ROPE_BASE, -(jnp.arange(half_dim).astype(jnp.float32) * 2.0) / HD)
    angles = positions.astype(jnp.float32)[:, None] * inverse[None, :]
    cos, sin = jnp.cos(angles), jnp.sin(angles)
    return jnp.concatenate([cos] * 4, axis=1), jnp.concatenate([-sin, sin] * 2, axis=1)


def swap_halves(pair):
    lane = lax.broadcasted_iota(jnp.int32, pair.shape, 1)
    up = pltpu.roll(pair, 2 * HD - HD // 2, 1)
    down = pltpu.roll(pair, HD // 2, 1)
    return jnp.where(lane % HD < HD // 2, up, down)


def rotate_rows(grad, cos_tab, sin_tab):
    half = HD // 2
    swapped = jnp.concatenate([grad[:, half:], grad[:, :half]], axis=1)
    return grad * cos_tab[:, :HD] - swapped * sin_tab[:, :HD]


def project_kernel(x_ref, gain_ref, wq_ref, wkv_ref, cos_ref, sin_ref, n_ref, q_ref, k_ref, v_ref):
    resid = x_ref[...].astype(jnp.float32)
    normed = (resid * rms_inverse(resid) * gain_ref[...]).astype(jnp.bfloat16)
    n_ref[...] = normed
    cos, sin = cos_ref[...], sin_ref[...]
    query = dot(normed, wq_ref[...])
    for first in range(0, query.shape[1], 2 * HD):
        pair = query[:, first : first + 2 * HD]
        turned = (pair * cos + swap_halves(pair) * sin) * HD ** (-0.5)
        q_ref[:, first : first + 2 * HD] = turned.astype(jnp.bfloat16)
    key_value = dot(normed, wkv_ref[...])
    turned = key_value * cos + swap_halves(key_value) * sin
    k_ref[...] = turned[:, :HD].astype(jnp.bfloat16)
    v_ref[...] = key_value[:, HD:].astype(jnp.bfloat16)


def project(x, gain, w_query, w_kv, cos_tab, sin_tab):
    rows, width = x.shape
    queries = w_query.shape[1]

    def tall(cols):
        return pl.BlockSpec((QB, cols), lambda i: (i, 0))

    def whole(array):
        return pl.BlockSpec(array.shape, lambda i: (0, 0))

    return pl.pallas_call(
        project_kernel,
        grid=(rows // QB,),
        in_specs=[
            tall(width),
            pl.BlockSpec((1, width), lambda i: (0, 0)),
            whole(w_query),
            whole(w_kv),
            tall(2 * HD),
            tall(2 * HD),
        ],
        out_specs=[tall(width), tall(queries), tall(HD), tall(HD)],
        out_shape=[
            jax.ShapeDtypeStruct((rows, width), jnp.bfloat16),
            jax.ShapeDtypeStruct((rows, queries), jnp.bfloat16),
            jax.ShapeDtypeStruct((rows, HD), jnp.bfloat16),
            jax.ShapeDtypeStruct((rows, HD), jnp.bfloat16),
        ],
        compiler_params=pltpu.CompilerParams(vmem_limit_bytes=VMEM_LIMIT),
        cost_estimate=pl.CostEstimate(
            flops=2 * rows * width * (queries + 2 * HD),
            bytes_accessed=4 * rows * width + 2 * width * (queries + 2 * HD),
            transcendentals=0,
        ),
        name="project",
    )(x, gain[None, :], w_query, w_kv, cos_tab, sin_tab)


def see(qpos, kpos, starts_ref, pics):
    mask = kpos <= qpos
    for pic in range(pics):
        begin = starts_ref[pic]
        mask = mask | (
            (qpos >= begin) & (qpos < begin + PIECE) & (kpos >= begin) & (kpos < begin + PIECE)
        )
    return mask


def key_blocks(starts_ref, pics, first):
    edge = first + QB
    crossed = jnp.bool_(False)
    for pic in range(pics):
        begin = starts_ref[pic]
        crossed = crossed | ((begin < edge) & (begin + PIECE > edge))
    return edge // QB + jnp.where(crossed, 1, 0)


def forward_kernel(
    pos_ref, starts_ref, q_ref, k_ref, v_ref, o_ref, lse_ref, bias, *, heads, pics, seq
):
    first = pos_ref[pl.program_id(0)]
    count = key_blocks(starts_ref, pics, first)
    for blocks in range(1, seq // QB + 1):

        @pl.when(count == blocks)
        def _():
            ext = blocks * QB
            low = max(0, ext - 2 * QB)
            wide = ext - low
            qpos = lax.broadcasted_iota(jnp.int32, (QB, wide), 0) + first
            kpos = lax.broadcasted_iota(jnp.int32, (QB, wide), 1) + low
            bias[:, :wide] = jnp.where(see(qpos, kpos, starts_ref, pics), 0.0, MASKED)
            outs, stats = [], []
            values = jnp.concatenate([v_ref[:ext, :], jnp.ones((ext, HD), jnp.bfloat16)], axis=1)
            for head in range(heads):
                queries = q_ref[:, head * HD : (head + 1) * HD]
                scores = contract_cols(queries, k_ref[:ext, :])
                if low:
                    scores = jnp.concatenate(
                        [scores[:, :low], scores[:, low:] + bias[:, :wide]], axis=1
                    )
                else:
                    scores = scores + bias[:, :wide]
                row_max = jnp.max(scores, axis=1, keepdims=True)
                terms = jnp.exp(scores - row_max).astype(jnp.bfloat16)
                summed = dot(terms, values)
                row_sum = summed[:, HD : HD + 1]
                outs.append(summed[:, :HD] / row_sum)
                stats.append(row_max + jnp.log(row_sum))
            o_ref[...] = jnp.concatenate(outs, axis=1).astype(jnp.bfloat16)
            lse_ref[...] = jnp.concatenate(stats, axis=1)


def attend_forward(q_low, k_low, v_low, starts, positions):
    rows, width = q_low.shape
    heads, seq, pics = width // HD, k_low.shape[0], starts.shape[0]
    tall = pl.BlockSpec((QB, width), lambda i, *_: (i, 0))
    keys = pl.BlockSpec((seq, HD), lambda i, *_: (0, 0))
    return pl.pallas_call(
        functools.partial(forward_kernel, heads=heads, pics=pics, seq=seq),
        grid_spec=pltpu.PrefetchScalarGridSpec(
            num_scalar_prefetch=2,
            grid=(rows // QB,),
            in_specs=[tall, keys, keys],
            out_specs=[tall, pl.BlockSpec((QB, heads), lambda i, *_: (i, 0))],
            scratch_shapes=[pltpu.VMEM((QB, 2 * QB), jnp.float32)],
        ),
        out_shape=[
            jax.ShapeDtypeStruct((rows, width), jnp.bfloat16),
            jax.ShapeDtypeStruct((rows, heads), jnp.float32),
        ],
        compiler_params=pltpu.CompilerParams(vmem_limit_bytes=VMEM_LIMIT),
        cost_estimate=pl.CostEstimate(
            flops=16 * rows * seq * width, bytes_accessed=4 * rows * width, transcendentals=0
        ),
        name="attend_forward",
    )(positions, starts, q_low, k_low, v_low)


def in_three(value):
    top = value.astype(jnp.bfloat16)
    rest = value - top.astype(jnp.float32)
    middle = rest.astype(jnp.bfloat16)
    last = (rest - middle.astype(jnp.float32)).astype(jnp.bfloat16)
    return [top, middle, last]


def backward_kernel(
    pos_ref, starts_ref, q_ref, do_ref, o_ref, lse_ref, k_ref, v_ref, cos_ref, sin_ref,
    dq_ref, dk_ref, dv_ref, bias, *, heads, pics, seq
):
    first = pos_ref[pl.program_id(0)]
    count = key_blocks(starts_ref, pics, first)

    @pl.when(pl.program_id(0) == 0)
    def _():
        dk_ref[...] = jnp.zeros_like(dk_ref)
        dv_ref[...] = jnp.zeros_like(dv_ref)

    for blocks in range(1, seq // QB + 1):

        @pl.when(count == blocks)
        def _():
            ext = blocks * QB
            low = max(0, ext - 2 * QB)
            wide = ext - low
            kpos = lax.broadcasted_iota(jnp.int32, (wide, QB), 0) + low
            qpos = lax.broadcasted_iota(jnp.int32, (wide, QB), 1) + first
            bias[:wide, :] = jnp.where(see(qpos, kpos, starts_ref, pics), 0.0, MASKED)
            ones = jnp.ones((ext, HD), jnp.bfloat16)
            keys = jnp.concatenate([k_ref[:ext, :], ones], axis=1)
            values = jnp.concatenate([v_ref[:ext, :], ones], axis=1)
            zeros = jnp.zeros((QB, HD - 3), jnp.bfloat16)
            d_key = jnp.zeros((ext, HD), jnp.float32)
            d_val = jnp.zeros((ext, HD), jnp.float32)
            for pair in range(heads // 2):
                parts = []
                for head in (2 * pair, 2 * pair + 1):
                    cols = slice(head * HD, (head + 1) * HD)
                    queries, d_out = q_ref[:, cols], do_ref[:, cols]
                    delta = jnp.sum(
                        d_out.astype(jnp.float32) * o_ref[:, cols].astype(jnp.float32),
                        axis=1,
                        keepdims=True,
                    )
                    queries_ext = jnp.concatenate(
                        [queries] + in_three(-lse_ref[:, head : head + 1]) + [zeros], axis=1
                    )
                    d_out_ext = jnp.concatenate([d_out] + in_three(-delta) + [zeros], axis=1)
                    scores = contract_cols(keys, queries_ext)
                    if low:
                        scores = jnp.concatenate(
                            [scores[:low], scores[low:] + bias[:wide, :]], axis=0
                        )
                    else:
                        scores = scores + bias[:wide, :]
                    probs = jnp.exp(scores)
                    d_probs = contract_cols(values, d_out_ext)
                    d_scores = (probs * d_probs).astype(jnp.bfloat16)
                    d_val += dot(probs.astype(jnp.bfloat16), d_out)
                    d_key += dot(d_scores, queries)
                    parts.append(contract_rows(d_scores, k_ref[:ext, :]))
                both = jnp.concatenate(parts, axis=1) * HD ** (-0.5)
                turned = both * cos_ref[...] - swap_halves(both) * sin_ref[...]
                dq_ref[:, 2 * pair * HD : 2 * (pair + 1) * HD] = turned.astype(jnp.bfloat16)
            dk_ref[:ext, :] += d_key
            dv_ref[:ext, :] += d_val


def attend_backward(q_low, d_attn, attn_low, lse, k_low, v_low, cos_tab, sin_tab, starts, positions):
    rows, width = q_low.shape
    heads, seq, pics = width // HD, k_low.shape[0], starts.shape[0]
    tall = pl.BlockSpec((QB, width), lambda i, *_: (i, 0))
    table = pl.BlockSpec((QB, 2 * HD), lambda i, *_: (i, 0))
    keys = pl.BlockSpec((seq, HD), lambda i, *_: (0, 0))
    return pl.pallas_call(
        functools.partial(backward_kernel, heads=heads, pics=pics, seq=seq),
        grid_spec=pltpu.PrefetchScalarGridSpec(
            num_scalar_prefetch=2,
            grid=(rows // QB,),
            in_specs=[
                tall, tall, tall, pl.BlockSpec((QB, heads), lambda i, *_: (i, 0)), keys, keys, table, table
            ],
            out_specs=[tall, keys, keys],
            scratch_shapes=[pltpu.VMEM((2 * QB, QB), jnp.float32)],
        ),
        out_shape=[
            jax.ShapeDtypeStruct((rows, width), jnp.bfloat16),
            jax.ShapeDtypeStruct((seq, HD), jnp.float32),
            jax.ShapeDtypeStruct((seq, HD), jnp.float32),
        ],
        compiler_params=pltpu.CompilerParams(vmem_limit_bytes=VMEM_LIMIT),
        cost_estimate=pl.CostEstimate(
            flops=32 * rows * seq * width, bytes_accessed=8 * rows * width, transcendentals=0
        ),
        name="attend_backward",
    )(positions, starts, q_low, d_attn, attn_low, lse, k_low, v_low, cos_tab, sin_tab)


def swap_core(value):
    return lax.ppermute(value, "tensor", [(i, i ^ 1) for i in range(4)])


def swap_chip(value):
    return lax.ppermute(value, "tensor", [(i, i ^ 2) for i in range(4)])


def gather_near(own):
    return jnp.concatenate([own, swap_core(own)], axis=0)


def gather_far(own):
    far = swap_chip(own)
    return jnp.concatenate([far, swap_core(far)], axis=0)


def send_far(part):
    rows = part.shape[0] // 2
    low = part.astype(jnp.bfloat16)
    chip_sum = low[:rows].astype(jnp.float32) + swap_core(low[rows:]).astype(jnp.float32)
    return swap_chip(chip_sum.astype(jnp.bfloat16)).astype(jnp.float32)


def sum_near(part):
    rows = part.shape[0] // 2
    return part[:rows] + swap_core(part[rows:].astype(jnp.bfloat16)).astype(jnp.float32)


def block_order(bits):
    order = [0]
    for bit in reversed(bits):
        order = [item ^ bit for item in order] + order
    return order


def permuted_features(value, index, bits):
    order = block_order(bits)
    width = value.shape[1] // len(order)
    return jnp.concatenate(
        [lax.dynamic_slice_in_dim(value, (index ^ item) * width, width, 1) for item in order], axis=1
    )


def reduce(make, total, axis, bits, size):
    half = total // 2
    sent = make(0, half).astype(jnp.bfloat16)
    kept = make(half, total).astype(jnp.bfloat16)
    for step, bit in enumerate(bits):
        came = lax.ppermute(sent, "dp", [(i, i ^ bit) for i in range(size)])
        added = kept.astype(jnp.float32) + came.astype(jnp.float32)
        if step == len(bits) - 1:
            return added
        added = added.astype(jnp.bfloat16)
        half = added.shape[axis] // 2
        sent = lax.slice_in_dim(added, 0, half, axis=axis)
        kept = lax.slice_in_dim(added, half, 2 * half, axis=axis)


def per_device(
    dp_size,
    layer_input,
    cotangent,
    starts,
    pieces,
    norm_attn,
    w_query,
    w_key,
    w_value,
    w_out,
    norm_mlp,
    w_gate,
    w_up,
    w_down,
):
    rows = layer_input.shape[0]
    width = layer_input.shape[1]
    place = lax.axis_index("tensor")
    index = lax.axis_index("dp")
    bits = [1 << i for i in range(dp_size.bit_length() - 1)]
    late_bits = bits[1:] + bits[:1]
    begins = starts[0]

    block_pos = jnp.stack([(place ^ m) * rows for m in range(4)]).astype(jnp.int32)
    near_pos, far_pos = block_pos[:2], block_pos[2:]
    row_pos = (block_pos[:, None] + jnp.arange(rows, dtype=jnp.int32)[None, :]).reshape(-1)
    cos_tab, sin_tab = rope_tables(row_pos)
    w_kv = jnp.concatenate([w_key, w_value], axis=1)

    def in_sequence(value):
        return jnp.concatenate(
            [lax.dynamic_slice_in_dim(value, (place ^ b) * rows, rows, 0) for b in range(4)], axis=0
        )

    near, far = slice(0, 2 * rows), slice(2 * rows, 4 * rows)
    x_near, x_far = gather_near(layer_input), gather_far(layer_input)
    cot_near, cot_far = gather_near(cotangent), gather_far(cotangent)
    normed_n, q_n, k_n, v_n = project(x_near, norm_attn, w_query, w_kv, cos_tab[near], sin_tab[near])
    normed_f, q_f, k_f, v_f = project(x_far, norm_attn, w_query, w_kv, cos_tab[far], sin_tab[far])
    k_low = in_sequence(jnp.concatenate([k_n, k_f], axis=0))
    v_low = in_sequence(jnp.concatenate([v_n, v_f], axis=0))
    attn_f, lse_f = attend_forward(q_f, k_low, v_low, begins, far_pos)
    attn_sent = send_far(dot(attn_f, w_out))
    attn_n, lse_n = attend_forward(q_n, k_low, v_low, begins, near_pos)
    attn_total = sum_near(dot(attn_n, w_out)) + attn_sent

    resid_in = layer_input.astype(jnp.float32)
    resid_mid = resid_in + attn_total
    inv_mlp = rms_inverse(resid_mid)
    normed_own = (resid_mid * inv_mlp * norm_mlp).astype(jnp.bfloat16)

    def feed_forward(normed, cot):
        gate_val, up_val = dot(normed, w_gate), dot(normed, w_up)
        gate_sig = jax.nn.sigmoid(gate_val)
        hidden = (gate_val * gate_sig * up_val).astype(jnp.bfloat16)
        d_hidden = contract_cols(cot, w_down)
        d_gate = d_hidden * up_val * (gate_sig * (1.0 + gate_val * (1.0 - gate_sig)))
        d_up = d_hidden * gate_val * gate_sig
        return hidden, d_gate.astype(jnp.bfloat16), d_up.astype(jnp.bfloat16)

    mlp_n, mlp_f = gather_near(normed_own), gather_far(normed_own)
    hidden_n, d_gate_n, d_up_n = feed_forward(mlp_n, cot_near)
    hidden_f, d_gate_f, d_up_f = feed_forward(mlp_f, cot_far)

    def norm_part(d_gate, d_up):
        return contract_cols(d_gate, w_gate) + contract_cols(d_up, w_up)

    d_norm_sent = send_far(norm_part(d_gate_f, d_up_f))
    d_norm_mid = sum_near(norm_part(d_gate_n, d_up_n)) + d_norm_sent

    def rows_of(one, two):
        return jnp.concatenate([one, two], axis=0)

    hidden, d_gate, d_up = (
        rows_of(hidden_n, hidden_f),
        rows_of(d_gate_n, d_gate_f),
        rows_of(d_up_n, d_up_f),
    )
    cot_blocks = permuted_features(rows_of(cot_near, cot_far), index, bits)
    mlp_blocks = permuted_features(rows_of(mlp_n, mlp_f), index, bits)
    grad_down = reduce(
        lambda a, b: contract_rows(hidden, cot_blocks[:, a:b]), width, 1, bits, dp_size
    )
    grad_gate = reduce(
        lambda a, b: contract_rows(mlp_blocks[:, a:b], d_gate), width, 0, bits, dp_size
    )
    grad_up = reduce(lambda a, b: contract_rows(mlp_blocks[:, a:b], d_up), width, 0, bits, dp_size)

    mlp_sent = send_far(dot(hidden_f, w_down))
    mlp_total = sum_near(dot(hidden_n, w_down)) + mlp_sent
    block_out = (resid_mid + mlp_total).astype(jnp.bfloat16)

    d_mid = cotangent.astype(jnp.float32) + norm_back(d_norm_mid, resid_mid, inv_mlp, norm_mlp)
    d_out_own = d_mid.astype(jnp.bfloat16)
    d_out_n, d_out_f = gather_near(d_out_own), gather_far(d_out_own)
    d_attn_n = contract_cols(d_out_n, w_out).astype(jnp.bfloat16)
    d_attn_f = contract_cols(d_out_f, w_out).astype(jnp.bfloat16)
    dq_n, dk_n, dv_n = attend_backward(
        q_n, d_attn_n, attn_n, lse_n, k_low, v_low, cos_tab[near], sin_tab[near], begins, near_pos
    )
    dq_f, dk_f, dv_f = attend_backward(
        q_f, d_attn_f, attn_f, lse_f, k_low, v_low, cos_tab[far], sin_tab[far], begins, far_pos
    )
    d_key = rotate_rows(in_sequence(dk_n + dk_f), cos_tab, sin_tab)
    d_value = in_sequence(dv_n + dv_f)
    d_kv = jnp.concatenate([d_key, d_value], axis=1).astype(jnp.bfloat16)
    d_norm_in_sent = send_far(contract_cols(dq_f, w_query) + contract_cols(d_kv[far], w_kv))
    d_norm_in = (
        sum_near(contract_cols(dq_n, w_query) + contract_cols(d_kv[near], w_kv)) + d_norm_in_sent
    )
    d_out_blocks = permuted_features(rows_of(d_out_n, d_out_f), index, late_bits)
    attn_low = rows_of(attn_n, attn_f)
    grad_out = reduce(
        lambda a, b: contract_rows(attn_low, d_out_blocks[:, a:b]), width, 1, late_bits, dp_size
    )
    normed_blocks = permuted_features(rows_of(normed_n, normed_f), index, late_bits)
    d_qkv = jnp.concatenate([rows_of(dq_n, dq_f), d_kv], axis=1)
    grad_qkv = reduce(
        lambda a, b: contract_rows(normed_blocks[:, a:b], d_qkv), width, 0, late_bits, dp_size
    )
    queries = w_query.shape[1]
    grad_query = grad_qkv[:, :queries]
    grad_key = grad_qkv[:, queries : queries + HD]
    grad_value = grad_qkv[:, queries + HD :]

    x_grad = d_mid + norm_back(d_norm_in, resid_in, rms_inverse(resid_in), norm_attn)

    share = width // dp_size

    def own_features(value):
        return lax.dynamic_slice_in_dim(value, index * share, share, 0).astype(jnp.float32)

    gain_attn = (
        jnp.sum(own_features(w_query) * grad_query, axis=1)
        + jnp.sum(own_features(w_kv) * grad_qkv[:, queries:], axis=1)
    ) / own_features(norm_attn)
    gain_mlp = jnp.sum(
        own_features(w_gate) * grad_gate + own_features(w_up) * grad_up, axis=1
    ) / own_features(norm_mlp)
    gains = jnp.stack([gain_attn, gain_mlp]).reshape(2, 4, share // 4)
    gains = jnp.stack([lax.dynamic_index_in_dim(gains, place ^ m, 1, False) for m in range(4)])
    gains = gains[:2] + swap_chip(gains[2:])
    gains = gains[0] + swap_core(gains[1])

    return (
        block_out,
        x_grad,
        gains[0],
        grad_query,
        grad_key,
        grad_value,
        grad_out,
        gains[1],
        grad_gate,
        grad_up,
        grad_down,
    )


def solution(mesh):
    in_specs = (
        P(("dp", "tensor"), None),
        P(("dp", "tensor"), None),
        P("dp", None),
        P("dp"),
        P(),
        P(None, "tensor"),
        P(None, "tensor"),
        P(None, "tensor"),
        P("tensor", None),
        P(),
        P(None, "tensor"),
        P(None, "tensor"),
        P("tensor", None),
    )
    out_specs = (
        P(("dp", "tensor"), None),
        P(("dp", "tensor"), None),
        P(("dp", "tensor")),
        P("dp", "tensor"),
        P("dp", "tensor"),
        P("dp", "tensor"),
        P("tensor", "dp"),
        P(("dp", "tensor")),
        P("dp", "tensor"),
        P("dp", "tensor"),
        P("tensor", "dp"),
    )
    return jax.shard_map(
        functools.partial(per_device, mesh.shape["dp"]),
        mesh=mesh,
        in_specs=in_specs,
        out_specs=out_specs,
        check_vma=False,
    )
```

```python
import functools

import jax
import jax.numpy as jnp
from jax import lax
from jax.experimental import pallas as pl
from jax.experimental.pallas import tpu as pltpu
from jax.sharding import PartitionSpec as P

HD = 64
SEQ = 1024
PIECE = 256
QB = 256


EPSILON = 1e-05
ROPE_BASE = 10000.0
MASKED = -1e30
VMEM_LIMIT = 48 * 2**20
PARTS = 1
PAIR = 2
NT = (((1,), (1,)), ((), ()))
TN = (((0,), (0,)), ((), ()))


def dot(left, right):
    return jnp.dot(left, right, preferred_element_type=jnp.float32)


def contract_rows(left, right):
    return lax.dot_general(left, right, TN, preferred_element_type=jnp.float32)


def contract_cols(left, right):
    return lax.dot_general(left, right, NT, preferred_element_type=jnp.float32)


def rms_inverse(resid):
    return lax.rsqrt(jnp.mean(resid * resid, axis=-1, keepdims=True) + EPSILON)


def norm_back(d_norm, resid, inverse, gain):
    scaled = d_norm * gain
    return inverse * scaled - resid * (inverse * inverse * inverse) * jnp.mean(
        scaled * resid, axis=-1, keepdims=True
    )


def rope_tables(positions):
    half_dim = HD // 2
    inverse = jnp.power(ROPE_BASE, -(jnp.arange(half_dim).astype(jnp.float32) * 2.0) / HD)
    angles = positions.astype(jnp.float32)[:, None] * inverse[None, :]
    cos, sin = jnp.cos(angles), jnp.sin(angles)
    return jnp.concatenate([cos] * 4, axis=1), jnp.concatenate([-sin, sin] * 2, axis=1)


def swap_halves(pair):
    lane = lax.broadcasted_iota(jnp.int32, pair.shape, 1)
    up = pltpu.roll(pair, 2 * HD - HD // 2, 1)
    down = pltpu.roll(pair, HD // 2, 1)
    return jnp.where(lane % HD < HD // 2, up, down)


def rotate_rows(grad, cos_tab, sin_tab):
    half = HD // 2
    swapped = jnp.concatenate([grad[:, half:], grad[:, :half]], axis=1)
    return grad * cos_tab[:, :HD] - swapped * sin_tab[:, :HD]


def either(near_refs):
    half = len(near_refs) // 2
    own, core = (
        jnp.concatenate([ref[...] for ref in refs], axis=0)
        for refs in (near_refs[:half], near_refs[half:])
    )
    return jnp.where(pl.program_id(0) == 0, own, core)


def project_kernel(*refs):
    x_refs = refs[:-9]
    gain_ref, wq_ref, wkv_ref, cos_ref, sin_ref, n_ref, q_ref, k_ref, v_ref = refs[-9:]
    resid = either(x_refs).astype(jnp.float32)
    normed = (resid * rms_inverse(resid) * gain_ref[...]).astype(jnp.bfloat16)
    n_ref[...] = normed
    cos, sin = cos_ref[...], sin_ref[...]
    query = dot(normed, wq_ref[...])
    for first in range(0, query.shape[1], 2 * HD):
        pair = query[:, first : first + 2 * HD]
        turned = (pair * cos + swap_halves(pair) * sin) * HD ** (-0.5)
        q_ref[:, first : first + 2 * HD] = turned.astype(jnp.bfloat16)
    key_value = dot(normed, wkv_ref[...])
    turned = key_value * cos + swap_halves(key_value) * sin
    k_ref[...] = turned[:, :HD].astype(jnp.bfloat16)
    v_ref[...] = key_value[:, HD:].astype(jnp.bfloat16)


def whole(array):
    return pl.BlockSpec(array.shape, lambda *_: (0,) * len(array.shape))


def params():
    return {
        "compiler_params": pltpu.CompilerParams(vmem_limit_bytes=VMEM_LIMIT),
        "cost_estimate": pl.CostEstimate(flops=1, bytes_accessed=1, transcendentals=0),
    }


def project(parts, gain, w_query, w_kv, cos_tab, sin_tab):
    rows, width = sum(part.shape[0] for part in parts) // 2, parts[0].shape[1]
    queries = w_query.shape[1]

    def tall(cols):
        return pl.BlockSpec((rows, cols), lambda i: (i, 0))

    gain = gain[None, :]
    return pl.pallas_call(
        project_kernel,
        grid=(2,),
        in_specs=[
            *(whole(item) for item in (*parts, gain, w_query, w_kv)), tall(2 * HD), tall(2 * HD)
        ],
        out_specs=[tall(width), tall(queries), tall(HD), tall(HD)],
        out_shape=[
            jax.ShapeDtypeStruct((2 * rows, width), jnp.bfloat16),
            jax.ShapeDtypeStruct((2 * rows, queries), jnp.bfloat16),
            jax.ShapeDtypeStruct((2 * rows, HD), jnp.bfloat16),
            jax.ShapeDtypeStruct((2 * rows, HD), jnp.bfloat16),
        ],
        name="project",
        **params(),
    )(*parts, gain, w_query, w_kv, cos_tab, sin_tab)


def by_rows(function, ins, consts, outs):
    flat, counts = [], []
    for item in ins:
        item = item if isinstance(item, tuple) else (item,)
        counts.append([len(flat) + sum(one is not None for one in item[:i]) if part is not None else None
                       for i, part in enumerate(item)])
        flat.extend(part for part in item if part is not None)
    rows, width = sum(flat[at].shape[0] for at in counts[0]), flat[0].shape[1]
    out_counts = [PARTS if isinstance(item, tuple) else 1 for item in outs]
    dtypes = [item[0] if isinstance(item, tuple) else item for item in outs]
    starts = [sum(out_counts[:i]) for i in range(len(outs))]
    out_places = [range(first, first + count) for first, count in zip(starts, out_counts)]
    step = 32

    def kernel(*refs):
        given = [ref[...] for ref in refs[len(flat) : len(flat) + len(consts)]]

        def views(part_refs, places, part):
            found = []
            for place in places:
                each = PARTS // len(place)
                at = place[part // each]
                ref = None if at is None else part_refs[at]
                found.append((ref, part % each * (rows // PARTS)))
            return found

        for part in range(PARTS):
            sources = views(refs, counts, part)
            targets = views(refs[len(flat) + len(consts) :], out_places, part)

            def chunk(i, _):
                def at(base):
                    return pl.ds(pl.multiple_of(base + i * step, step), step)

                values = [
                    0.0 if ref is None else ref[at(base), :].astype(jnp.float32)
                    for ref, base in sources
                ]
                for (ref, base), value in zip(targets, function(*values, *given)):
                    ref[at(base), :] = value.astype(ref.dtype)
                return 0

            lax.fori_loop(0, rows // PARTS // step, chunk, 0)

    consts = [item[None, :] for item in consts]
    shapes = []
    for count, dtype in zip(out_counts, dtypes):
        shapes.extend([jax.ShapeDtypeStruct((rows // count, width), dtype)] * count)
    results = pl.pallas_call(kernel, out_shape=shapes, name="by_rows", **params())(*flat, *consts)
    grouped, at = [], 0
    for count, item in zip(out_counts, outs):
        grouped.append(tuple(results[at : at + count]) if isinstance(item, tuple) else results[at])
        at += count
    return grouped


def see(qpos, kpos, starts_ref, pics):
    mask = kpos <= qpos
    for pic in range(pics):
        begin = starts_ref[pic]
        mask = mask | (
            (qpos >= begin) & (qpos < begin + PIECE) & (kpos >= begin) & (kpos < begin + PIECE)
        )
    return mask


def key_blocks(starts_ref, pics, first):
    edge = first + QB
    crossed = jnp.bool_(False)
    for pic in range(pics):
        begin = starts_ref[pic]
        crossed = crossed | ((begin < edge) & (begin + PIECE > edge))
    return edge // QB + jnp.where(crossed, 1, 0)


def forward_kernel(
    pos_ref, starts_ref, q_ref, k_ref, v_ref, out_ref, o_ref, lse_ref, kept_ref, *rest, heads, pics, seq
):
    *sent_refs, bias = rest
    first = pos_ref[pl.program_id(0)]
    count = key_blocks(starts_ref, pics, first)
    for blocks in range(1, seq // QB + 1):

        @pl.when(count == blocks)
        def _():
            ext = blocks * QB
            low = max(0, ext - 2 * QB)
            wide = ext - low
            qpos = lax.broadcasted_iota(jnp.int32, (QB, wide), 0) + first
            kpos = lax.broadcasted_iota(jnp.int32, (QB, wide), 1) + low
            bias[:, :wide] = jnp.where(see(qpos, kpos, starts_ref, pics), 0.0, MASKED)
            values = jnp.concatenate([v_ref[:ext, :], jnp.ones((ext, HD), jnp.bfloat16)], axis=1)
            lane = lax.broadcasted_iota(jnp.int32, (QB, heads), 1)

            def one_pair(pair, stats):
                at = pl.ds(pl.multiple_of(pair * 2 * HD, 2 * HD), 2 * HD)
                both = q_ref[:, at]
                outs = []
                for side in range(2):
                    scores = contract_cols(both[:, side * HD : (side + 1) * HD], k_ref[:ext, :])
                    if low:
                        scores = jnp.concatenate(
                            [scores[:, :low], scores[:, low:] + bias[:, :wide]], axis=1
                        )
                    else:
                        scores = scores + bias[:, :wide]
                    row_max = jnp.max(scores, axis=1, keepdims=True)
                    terms = jnp.exp(scores - row_max).astype(jnp.bfloat16)
                    summed = dot(terms, values)
                    row_sum = summed[:, HD : HD + 1]
                    outs.append(summed[:, :HD] / row_sum)
                    stats = jnp.where(lane == 2 * pair + side, row_max + jnp.log(row_sum), stats)
                o_ref[:, at] = jnp.concatenate(outs, axis=1).astype(jnp.bfloat16)
                return stats

            lse_ref[...] = lax.fori_loop(
                0, heads // 2, one_pair, jnp.zeros((QB, heads), jnp.float32)
            )

    part = dot(o_ref[...], out_ref[...]).astype(jnp.bfloat16)

    @pl.when(pl.program_id(0) == 0)
    def _():
        kept_ref[...] = part

    @pl.when(pl.program_id(0) == 1)
    def _():
        for i, ref in enumerate(sent_refs):
            ref[...] = part[i * ref.shape[0] : (i + 1) * ref.shape[0]]


def attend_forward(q_low, k_low, v_low, w_out, starts, positions):
    rows, width = q_low.shape
    heads, seq, pics = width // HD, k_low.shape[0], starts.shape[0]
    tall = pl.BlockSpec((QB, width), lambda i, *_: (i, 0))
    parts = [(QB, w_out.shape[1])] + [(QB // PARTS, w_out.shape[1])] * PARTS
    keys = pl.BlockSpec((seq, HD), lambda i, *_: (0, 0))
    return pl.pallas_call(
        functools.partial(forward_kernel, heads=heads, pics=pics, seq=seq),
        grid_spec=pltpu.PrefetchScalarGridSpec(
            num_scalar_prefetch=2,
            grid=(rows // QB,),
            in_specs=[tall, keys, keys, whole(w_out)],
            out_specs=[
                tall,
                pl.BlockSpec((QB, heads), lambda i, *_: (i, 0)),
                *(pl.BlockSpec(part, lambda i, *_: (0, 0)) for part in parts),
            ],
            scratch_shapes=[pltpu.VMEM((QB, 2 * QB), jnp.float32)],
        ),
        out_shape=[
            jax.ShapeDtypeStruct((rows, width), jnp.bfloat16),
            jax.ShapeDtypeStruct((rows, heads), jnp.float32),
            *(jax.ShapeDtypeStruct(part, jnp.bfloat16) for part in parts),
        ],
        name="attend_forward",
        **params(),
    )(positions, starts, q_low, k_low, v_low, w_out)


def in_three(value):
    top = value.astype(jnp.bfloat16)
    rest = value - top.astype(jnp.float32)
    middle = rest.astype(jnp.bfloat16)
    last = (rest - middle.astype(jnp.float32)).astype(jnp.bfloat16)
    return [top, middle, last]


def backward_kernel(
    pos_ref, starts_ref, q_ref, out_ref, o_ref, lse_ref, k_ref, v_ref, cos_ref, sin_ref,
    *rest, heads, pics, seq
):
    *d_refs, dq_ref, dk_ref, dv_ref, bias, do_ref = rest
    first = pos_ref[pl.program_id(0)]
    count = key_blocks(starts_ref, pics, first)

    @pl.when(pl.program_id(0) == 0)
    def _():
        dk_ref[...] = jnp.zeros_like(dk_ref)
        dv_ref[...] = jnp.zeros_like(dv_ref)

    do_ref[...] = contract_cols(either(d_refs), out_ref[...]).astype(jnp.bfloat16)

    for blocks in range(1, seq // QB + 1):

        @pl.when(count == blocks)
        def _():
            ext = blocks * QB
            low = max(0, ext - 2 * QB)
            wide = ext - low
            kpos = lax.broadcasted_iota(jnp.int32, (wide, QB), 0) + low
            qpos = lax.broadcasted_iota(jnp.int32, (wide, QB), 1) + first
            bias[:wide, :] = jnp.where(see(qpos, kpos, starts_ref, pics), 0.0, MASKED)
            ones = jnp.ones((ext, HD), jnp.bfloat16)
            keys = jnp.concatenate([k_ref[:ext, :], ones], axis=1)
            values = jnp.concatenate([v_ref[:ext, :], ones], axis=1)
            zeros = jnp.zeros((QB, HD - 3), jnp.bfloat16)
            lane = lax.broadcasted_iota(jnp.int32, (QB, heads), 1)

            def one_pair(pair, _):
                at = pl.ds(pl.multiple_of(pair * 2 * HD, 2 * HD), 2 * HD)
                q_both, d_both, o_both = q_ref[:, at], do_ref[:, at], o_ref[:, at]
                stats = lse_ref[...]
                d_query, d_key, d_val = [], 0.0, 0.0
                for side in range(2):
                    cols = slice(side * HD, (side + 1) * HD)
                    queries, d_out = q_both[:, cols], d_both[:, cols]
                    delta = jnp.sum(
                        d_out.astype(jnp.float32) * o_both[:, cols].astype(jnp.float32),
                        axis=1,
                        keepdims=True,
                    )
                    lse = jnp.sum(
                        jnp.where(lane == 2 * pair + side, stats, 0.0), axis=1, keepdims=True
                    )
                    queries_ext = jnp.concatenate([queries] + in_three(-lse) + [zeros], axis=1)
                    d_out_ext = jnp.concatenate([d_out] + in_three(-delta) + [zeros], axis=1)
                    scores = contract_cols(keys, queries_ext)
                    if low:
                        scores = jnp.concatenate(
                            [scores[:low], scores[low:] + bias[:wide, :]], axis=0
                        )
                    else:
                        scores = scores + bias[:wide, :]
                    probs = jnp.exp(scores)
                    d_probs = contract_cols(values, d_out_ext)
                    d_scores = (probs * d_probs).astype(jnp.bfloat16)
                    d_val += dot(probs.astype(jnp.bfloat16), d_out)
                    d_key += dot(d_scores, queries)
                    d_query.append(contract_rows(d_scores, k_ref[:ext, :]))
                dk_ref[:ext, :] += d_key
                dv_ref[:ext, :] += d_val
                turned = jnp.concatenate(d_query, axis=1) * HD ** (-0.5)
                turned = turned * cos_ref[...] - swap_halves(turned) * sin_ref[...]
                dq_ref[:, at] = turned.astype(jnp.bfloat16)
                return 0

            lax.fori_loop(0, heads // 2, one_pair, 0)


def attend_backward(
    q_low, d_parts, w_out, attn_low, lse, k_low, v_low, cos_tab, sin_tab, starts, positions
):
    rows, width = q_low.shape
    heads, seq, pics = width // HD, k_low.shape[0], starts.shape[0]
    tall = pl.BlockSpec((QB, width), lambda i, *_: (i, 0))
    table = pl.BlockSpec((QB, 2 * HD), lambda i, *_: (i, 0))
    stats = pl.BlockSpec((QB, heads), lambda i, *_: (i, 0))
    keys = whole(k_low)
    return pl.pallas_call(
        functools.partial(backward_kernel, heads=heads, pics=pics, seq=seq),
        grid_spec=pltpu.PrefetchScalarGridSpec(
            num_scalar_prefetch=2,
            grid=(rows // QB,),
            in_specs=[
                tall, whole(w_out), tall, stats, keys, keys, table, table,
                *(whole(part) for part in d_parts),
            ],
            out_specs=[tall, keys, keys],
            scratch_shapes=[
                pltpu.VMEM((2 * QB, QB), jnp.float32),
                pltpu.VMEM((QB, width), jnp.bfloat16),
            ],
        ),
        out_shape=[
            jax.ShapeDtypeStruct((rows, width), jnp.bfloat16),
            jax.ShapeDtypeStruct((seq, HD), jnp.float32),
            jax.ShapeDtypeStruct((seq, HD), jnp.float32),
        ],
        name="attend_backward",
        **params(),
    )(
        positions, starts, q_low, w_out, attn_low, lse, k_low, v_low, cos_tab, sin_tab, *d_parts
    )


def feed_kernel(*refs, counts):
    gate_ref, up_ref, down_ref, hidden_ref, d_gate_ref, d_up_ref, normed, cots = refs[sum(counts) :]

    @pl.when(pl.program_id(0) == 0)
    def _():
        for target, sources in ((normed, refs[: counts[0]]), (cots, refs[counts[0] : sum(counts)])):
            at = 0
            for ref in sources:
                target[at : at + ref.shape[0], :] = ref[...]
                at += ref.shape[0]

    gate_val, up_val = dot(normed[...], gate_ref[...]), dot(normed[...], up_ref[...])
    d_hidden = contract_cols(cots[...], down_ref[...])
    gate_sig = jax.nn.sigmoid(gate_val)
    swish = gate_val * gate_sig
    hidden_ref[...] = (swish * up_val).astype(jnp.bfloat16)
    d_gate = d_hidden * up_val * (gate_sig + swish * (1.0 - gate_sig))
    d_gate_ref[...] = d_gate.astype(jnp.bfloat16)
    d_up_ref[...] = (d_hidden * swish).astype(jnp.bfloat16)


def feed_forward(normed, cots, w_gate, w_up, w_down):
    rows, width = sum(item.shape[0] for item in normed), normed[0].shape[1]
    units, tile = w_gate.shape[1], 256
    cols = pl.BlockSpec((width, tile), lambda j: (0, j))
    out = pl.BlockSpec((rows, tile), lambda j: (0, j))
    return pl.pallas_call(
        functools.partial(feed_kernel, counts=(len(normed), len(cots))),
        grid=(pl.cdiv(units, tile),),
        in_specs=[
            *(whole(item) for item in (*normed, *cots)),
            cols,
            cols,
            pl.BlockSpec((tile, width), lambda j: (j, 0)),
        ],
        out_specs=[out] * 3,
        out_shape=[jax.ShapeDtypeStruct((rows, units), jnp.bfloat16)] * 3,
        scratch_shapes=[pltpu.VMEM((rows, width), jnp.bfloat16)] * 2,
        name="feed_forward",
        **params(),
    )(*normed, *cots, w_gate, w_up, w_down)


def share_kernel(*refs, transposed):
    count = (len(refs) - 1 - PARTS) // 2
    kept_ref, *sent_refs = refs[2 * count :]
    multiply = contract_cols if transposed else dot
    part = multiply(refs[0][...], refs[count][...])
    for left, right in zip(refs[1:count], refs[count + 1 : 2 * count]):
        part = part + multiply(left[...], right[...])
    rows = kept_ref.shape[0]
    kept_ref[...] = part[:rows].astype(jnp.bfloat16)
    for i, ref in enumerate(sent_refs):
        at = rows + i * ref.shape[0]
        ref[...] = part[at : at + ref.shape[0]].astype(jnp.bfloat16)


def row_shares(lefts, rights, transposed, rows, block):
    rows //= 2
    width, tile = rights[0].shape[0 if transposed else 1], 512

    def right_spec(item):
        if transposed:
            return pl.BlockSpec((tile, item.shape[1]), lambda j: (j, 0))
        return pl.BlockSpec((item.shape[0], tile), lambda j: (0, j))

    sizes = [rows] + [rows // PARTS] * PARTS
    return pl.pallas_call(
        functools.partial(share_kernel, transposed=transposed),
        grid=(width // tile,),
        in_specs=[
            *(pl.BlockSpec((2 * rows, item.shape[1]), lambda j: (block, 0)) for item in lefts),
            *(right_spec(item) for item in rights),
        ],
        out_specs=[pl.BlockSpec((size, tile), lambda j: (0, j)) for size in sizes],
        out_shape=[jax.ShapeDtypeStruct((size, width), jnp.bfloat16) for size in sizes],
        name="row_shares",
        **params(),
    )(*lefts, *rights)


def outer_kernel(order_ref, *refs, shape):
    refs, sent_ref, kept_ref = list(refs[:-2]), refs[-2], refs[-1]
    totals = None
    for lefts, rights in shape:
        rows = jnp.concatenate([refs.pop(0)[...] for _ in range(lefts)], axis=0)
        parts = [contract_rows(rows, refs.pop(0)[...]) for _ in range(rights)]
        totals = parts if totals is None else [a + b for a, b in zip(totals, parts)]
    total = jnp.concatenate(totals, axis=1).astype(jnp.bfloat16)
    step = pl.program_id(0)
    half = pl.num_programs(0) // 2

    @pl.when(step < half)
    def _():
        sent_ref[...] = total

    @pl.when(step >= half)
    def _():
        kept_ref[...] = total


def outer(sections, index, bits):
    width = sections[0][0][0].shape[1]
    share = width // (1 << len(bits))
    tile = 256
    if share == tile:
        blocks = jnp.stack([index ^ item for item in block_order(bits)]).astype(jnp.int32)
    else:
        blocks = jnp.arange(width // tile, dtype=jnp.int32)
        sections = [
            ([permuted_features(item, index, bits) for item in lefts], rights)
            for lefts, rights in sections
        ]
    count = width // tile
    size = sum(item.shape[1] for item in sections[0][1])
    specs, arrays = [], []
    for lefts, rights in sections:
        specs.extend(pl.BlockSpec((item.shape[0], tile), lambda j, b: (0, b[j])) for item in lefts)
        specs.extend(whole(item) for item in rights)
        arrays.extend((*lefts, *rights))
    return pl.pallas_call(
        functools.partial(
            outer_kernel, shape=[(len(lefts), len(rights)) for lefts, rights in sections]
        ),
        grid_spec=pltpu.PrefetchScalarGridSpec(
            num_scalar_prefetch=1,
            grid=(count,),
            in_specs=specs,
            out_specs=[
                pl.BlockSpec((tile, size), lambda j, _: (jnp.minimum(j, count // 2 - 1), 0)),
                pl.BlockSpec((tile, size), lambda j, _: (jnp.maximum(j - count // 2, 0), 0)),
            ],
        ),
        out_shape=[jax.ShapeDtypeStruct((width // 2, size), jnp.bfloat16)] * 2,
        name="outer",
        **params(),
    )(blocks, *arrays)


def halves_kernel(kept_a, kept_b, came_a, came_b, sent_ref, kept_ref):
    sent_ref[...] = added(kept_a[...], came_a[...])
    kept_ref[...] = added(kept_b[...], came_b[...])


def add_halves(kept, came):
    half, columns = kept.shape[0] // 2, kept.shape[1]
    block = min(256, half)
    first = pl.BlockSpec((block, columns), lambda i: (i, 0))
    second = pl.BlockSpec((block, columns), lambda i: (i + half // block, 0))
    return pl.pallas_call(
        halves_kernel,
        grid=(half // block,),
        in_specs=[first, second, first, second],
        out_specs=[first, first],
        out_shape=[jax.ShapeDtypeStruct((half, columns), jnp.bfloat16)] * 2,
        name="add_halves",
        **params(),
    )(kept, kept, came, came)


def total_kernel(kept_ref, came_ref, out_ref):
    out_ref[...] = kept_ref[...].astype(jnp.float32) + came_ref[...].astype(jnp.float32)


def add_total(kept, came):
    return pl.pallas_call(
        total_kernel,
        out_shape=jax.ShapeDtypeStruct(kept.shape, jnp.float32),
        name="add_total",
        **params(),
    )(kept, came)


def key_value_kernel(
    at_ref, dkn_ref, dkf_ref, dvn_ref, dvf_ref, cos_ref, sin_ref, near_ref, far_ref
):
    rows = dkn_ref.shape[0] // 4
    for m in range(4):
        at = pl.ds(pl.multiple_of(at_ref[m], rows), rows)
        mine = slice(m * rows, (m + 1) * rows)
        d_key = dkn_ref[at, :] + dkf_ref[at, :]
        d_val = dvn_ref[at, :] + dvf_ref[at, :]
        both = jnp.concatenate([d_key, d_val], axis=1)
        turned = both * cos_ref[mine, :] - swap_halves(both) * sin_ref[mine, :]
        both = jnp.concatenate([turned[:, :HD], d_val], axis=1).astype(jnp.bfloat16)
        target = near_ref if m < 2 else far_ref
        target[m % 2 * rows : (m % 2 + 1) * rows, :] = both


def key_value_rows(dk_n, dk_f, dv_n, dv_f, cos_tab, sin_tab, block_pos):
    shape = jax.ShapeDtypeStruct((dk_n.shape[0] // 2, 2 * HD), jnp.bfloat16)
    arrays = (dk_n, dk_f, dv_n, dv_f, cos_tab, sin_tab)
    return pl.pallas_call(
        key_value_kernel,
        grid_spec=pltpu.PrefetchScalarGridSpec(
            num_scalar_prefetch=1,
            grid=(1,),
            in_specs=[whole(item) for item in arrays],
            out_specs=[whole(shape), whole(shape)],
        ),
        out_shape=[shape, shape],
        name="key_value_rows",
        **params(),
    )(block_pos, *arrays)


def swapped(parts, flip):
    pairs = [(i, i ^ flip) for i in range(4)]
    return tuple(lax.ppermute(part, "tensor", pairs) for part in parts)


def swap_core(parts):
    return swapped(parts, 1)


def swap_chip(parts):
    return swapped(parts, 2)


def swap_pair(parts, size):
    return tuple(exchange(part, PAIR, size) for part in parts)


class Order:
    def __init__(self):
        self.last = ()

    def after(self, *values):
        tied = lax.optimization_barrier(values + (self.last,))[: len(values)]
        self.last = tied
        return tied if len(values) > 1 else tied[0]

    def done(self, *values):
        values = lax.optimization_barrier(values + (self.last,))[: len(values)]
        self.last = values
        return values if len(values) > 1 else values[0]


def wait_for(value, *others):
    return lax.optimization_barrier((value,) + others)[0]


def rows_of(one, two):
    return jnp.concatenate([one, two], axis=0)


def block_order(bits):
    order = [0]
    for bit in reversed(bits):
        order = [item ^ bit for item in order] + order
    return order


def permuted_features(value, index, bits):
    order = block_order(bits)
    width = value.shape[1] // len(order)
    return jnp.concatenate(
        [lax.dynamic_slice_in_dim(value, (index ^ item) * width, width, 1) for item in order], axis=1
    )


def rows_and_cols(one, two):
    return jnp.concatenate([one, two], axis=1)


def exchange(value, bit, size):
    return lax.ppermute(value, "dp", [(i, i ^ bit) for i in range(size)])


class Reduction:
    def __init__(self, order, sent, kept, bits, size, assemble=None):
        self.order, self.sent, self.kept, self.assemble = order, sent, kept, assemble
        self.bits, self.size, self.step = bits, size, 0
        self.total = None

    def send(self, *others):
        sent = wait_for(self.sent, *others) if others else self.sent
        self.came = exchange(sent, self.bits[self.step], self.size)
        return self

    def receive(self):
        self.came = self.order.after(self.came)
        return self

    def add(self):
        kept, came = self.kept, self.came
        self.step += 1
        if self.step == len(self.bits):
            self.total = self.order.done((self.assemble or add_total)(kept, came))
        else:
            self.sent, self.kept = self.order.done(*add_halves(kept, came))
        return self

    def advance(self):
        self.receive().add()
        if self.total is None:
            self.send()

    def finish(self):
        while self.total is None:
            self.advance()
        return self.total


def added(one, two):
    return (one.astype(jnp.float32) + two.astype(jnp.float32)).astype(jnp.bfloat16)


def per_device(
    dp_size,
    layer_input,
    cotangent,
    starts,
    pieces,
    norm_attn,
    w_query,
    w_key,
    w_value,
    w_out,
    norm_mlp,
    w_gate,
    w_up,
    w_down,
):
    rows = layer_input.shape[0]
    width = layer_input.shape[1]
    place = lax.axis_index("tensor")
    index = lax.axis_index("dp")
    bits = [1 << i for i in range(dp_size.bit_length() - 1)]
    late_bits = bits[1:] + bits[:1]
    begins = starts[0]

    block_pos = jnp.stack([(place ^ m) * rows for m in range(4)]).astype(jnp.int32)
    near_pos, far_pos = block_pos[:2], block_pos[2:]
    row_pos = (block_pos[:, None] + jnp.arange(rows, dtype=jnp.int32)[None, :]).reshape(-1)
    cos_tab, sin_tab = rope_tables(row_pos)
    w_kv = jnp.concatenate([w_key, w_value], axis=1)

    def in_sequence(value):
        return jnp.concatenate(
            [lax.dynamic_slice_in_dim(value, (place ^ b) * rows, rows, 0) for b in range(4)], axis=0
        )

    def in_two(value):
        return tuple(jnp.split(value, PARTS, axis=0))

    order = Order()
    near, far = slice(0, 2 * rows), slice(2 * rows, 4 * rows)

    def chip_sum(kept, came):
        came = order.after(came)
        return order.done(*by_rows(lambda a, b: (a + b,), (kept, came), (), ((jnp.bfloat16,),)))

    x_own, cot_own = in_two(layer_input), in_two(cotangent)
    x_chip, x_core = swap_chip(x_own), swap_core(x_own)

    side = index // PAIR % 2
    units, queries = w_gate.shape[1], w_query.shape[1]
    window = -(-units // 256) * 128
    overlap = 2 * window - units
    mine = (jnp.arange(window) >= overlap) | (side == 0)
    gate_half = lax.dynamic_slice_in_dim(w_gate, side * (units - window), window, 1)
    up_half = lax.dynamic_slice_in_dim(w_up, side * (units - window), window, 1)
    up_half = jnp.where(mine[None, :], up_half, 0).astype(jnp.bfloat16)
    down_half = lax.dynamic_slice_in_dim(w_down, side * (units - window), window, 0)
    down_half = jnp.where(mine[:, None], down_half, 0).astype(jnp.bfloat16)
    gate_half, up_half, down_half, w_kv, cos_tab, sin_tab = order.done(
        gate_half, up_half, down_half, w_kv, cos_tab, sin_tab
    )
    normed_n, q_n, k_n, v_n = order.done(
        *project((*x_own, *x_core), norm_attn, w_query, w_kv, cos_tab[near], sin_tab[near])
    )
    x_chip = order.after(x_chip)
    cot_own_ = wait_for(cot_own, x_chip)
    cot_chip, cot_core, cot_pair = (
        swap_chip(cot_own_), swap_core(cot_own_), swap_pair(cot_own_, dp_size)
    )
    normed_f, q_f, k_f, v_f = order.done(
        *project((*x_chip, *swap_core(x_chip)), norm_attn, w_query, w_kv, cos_tab[far], sin_tab[far])
    )
    k_low = in_sequence(rows_of(k_n, k_f))
    v_low = in_sequence(rows_of(v_n, v_f))
    attn_f, lse_f, kept, *sent = order.done(
        *attend_forward(q_f, k_low, v_low, w_out, begins, far_pos)
    )
    came = swap_core(sent)
    cot_chip, cot_pair = order.after(cot_chip, cot_pair)
    cot_diag, cot_other, cot_pcore = (
        swap_pair(cot_chip, dp_size), swap_core(cot_chip), swap_core(cot_pair)
    )
    attn_came = swap_chip(chip_sum(kept, came))
    cot_core, cot_other, cot_pcore, q_n = order.after(cot_core, cot_other, cot_pcore, q_n)
    attn_n, lse_n, kept, *sent = order.done(
        *attend_forward(q_n, k_low, v_low, w_out, begins, near_pos)
    )
    sum_came = swap_core(sent)
    cot_diag = order.after(cot_diag)
    cot_dcore = swap_core(cot_diag)
    attn_came = order.after(attn_came)
    sum_came, cot_dcore = order.after(sum_came, cot_dcore)

    def norm_mid(x, kept, core, chip, gain):
        resid = x + (kept + core + chip)
        return resid, resid * rms_inverse(resid) * gain

    resid_mid, mlp_own = order.done(
        *by_rows(
            norm_mid, (x_own, kept, sum_came, attn_came), (norm_mlp,), (jnp.float32, (jnp.bfloat16,))
        )
    )
    mlp_core, mlp_chip, mlp_pair = swap_core(mlp_own), swap_chip(mlp_own), swap_pair(mlp_own, dp_size)
    mlp_core = order.after(mlp_core)

    def feed(normed, cots):
        return order.done(*feed_forward(normed, cots, gate_half, up_half, down_half))

    near_hidden = feed((*mlp_own, *mlp_core), (*cot_own, *cot_core))
    mlp_chip, mlp_pair = order.after(mlp_chip, mlp_pair)
    half = rows // 2
    mlp_diag = (
        *swap_chip((mlp_pair[0][:half],)), *swap_pair((mlp_chip[0][half:],), dp_size)
    )
    mlp_other, mlp_pcore = order.after(swap_core(mlp_chip), swap_core(mlp_pair))
    side_hidden = feed(
        (*mlp_chip, *mlp_other, *mlp_pair, *mlp_pcore),
        (*cot_chip, *cot_other, *cot_pair, *cot_pcore),
    )
    mlp_diag = order.after(mlp_diag)
    mlp_dcore = order.after(swap_core(mlp_diag))
    diag_hidden = feed((*mlp_diag, *mlp_dcore), (*cot_diag, *cot_dcore))
    hiddens = (near_hidden, side_hidden, diag_hidden)

    def in_window(kept, came):
        first = jnp.where(side == 0, kept, came)
        second = jnp.where(side == 0, came, kept)
        return jnp.concatenate([first, second[:, overlap:]], axis=1).astype(jnp.float32)

    pair_bits = [bit for bit in bits if bit != PAIR] + [PAIR]
    always = begins[0] >= 0

    def fence(step):
        def inside():
            outer_last, order.last = order.last, ()
            try:
                return step()
            finally:
                order.last = outer_last

        shapes = jax.eval_shape(inside)
        taken = order.after(always)
        results = lax.cond(
            taken,
            inside,
            lambda: jax.tree.map(lambda item: jnp.zeros(item.shape, item.dtype), shapes),
        )
        leaves, tree = jax.tree.flatten(results)
        return jax.tree.unflatten(tree, order.done(tuple(leaves)))

    def gradient(sections, order_bits):
        lefts, rights = order.after([item[0] for item in sections], [item[1] for item in sections])
        return order.done(*outer(list(zip(lefts, rights)), index, order_bits))

    cots = (
        (*cot_own, *cot_core),
        (*cot_chip, *cot_other, *cot_pair, *cot_pcore),
        (*cot_diag, *cot_dcore),
    )
    mlps = (
        (*mlp_own, *mlp_core),
        (*mlp_chip, *mlp_other, *mlp_pair, *mlp_pcore),
        (*mlp_diag, *mlp_dcore),
    )

    def mlp_gradient(lefts, which):
        sections = [(left, (right[which],)) for left, right in zip(lefts, hiddens)]
        return gradient(sections, pair_bits)

    def reduction(sent_kept, order_bits, assemble=None):
        return Reduction(order, *sent_kept, order_bits, dp_size, assemble)

    def shares(lefts, rights, transposed=True, block=0):
        kept, *sent = order.done(
            *row_shares(order.after(lefts), rights, transposed, 2 * rows, block)
        )
        return kept, swap_core(sent)

    def total(*items):
        return order.done(*by_rows(lambda *values: (sum(values),), items, (), ((jnp.bfloat16,),)))

    class GroupSum:
        def __init__(self, which, rights, transposed):
            self.rest = rights, transposed
            self.near, self.sides, self.diag = (tuple(item[i] for i in which) for item in hiddens)

        def diag_sum(self):
            return chip_sum(*shares(self.diag, *self.rest))

        def side_shares(self):
            chip, chip_came = shares(self.sides, *self.rest, 0)
            pair, pair_came = shares(self.sides, *self.rest, 1)
            return (chip, *order.after(chip_came)), (pair, *order.after(pair_came))

        def own(self):
            kept, core = shares(self.near, *self.rest)
            return kept, order.after(core)

    d_norm = GroupSum((1, 2), (gate_half, up_half), True)
    block_sum = GroupSum((0,), (down_half,), False)

    down = reduction(mlp_gradient(cots, 0), pair_bits, in_window)
    down.send()
    to_pair = swap_pair(fence(d_norm.diag_sum), dp_size)
    gate, (chip_shares, pair_shares) = fence(
        lambda: (mlp_gradient(mlps, 1), d_norm.side_shares())
    )
    gate = reduction(gate, pair_bits, in_window)
    came_p = swap_pair(total(*pair_shares), dp_size)
    came_c = swap_chip(total(*chip_shares, order.after(to_pair)))
    down.receive()
    gate.send(down.came)
    down.add().send()
    (kept, core), up = fence(lambda: (d_norm.own(), mlp_gradient(mlps, 2)))
    up = reduction(up, pair_bits, in_window)
    came_c, came_p = order.after(came_c, came_p)

    def back_mid(kept, core, chip, pair, resid, cot, gain):
        d_mid = cot + norm_back(kept + core + chip + pair, resid, rms_inverse(resid), gain)
        return d_mid, d_mid

    d_mid, d_own = order.done(
        *by_rows(
            back_mid,
            (kept, core, came_c, came_p, resid_mid, cot_own),
            (norm_mlp,),
            (jnp.float32, (jnp.bfloat16,)),
        )
    )
    d_chip = swap_chip(d_own)
    gate.receive()
    up.send(gate.came)
    down.receive().add()
    down.send()
    gate.add().send()

    @fence
    def near_back():
        d_core = order.after(swap_core(d_own))
        return d_core, order.done(
            *attend_backward(
                q_n, (*d_own, *d_core), w_out, attn_n, lse_n, k_low, v_low, cos_tab[near],
                sin_tab[near], begins, near_pos,
            )
        )

    d_core, (dq_n, dk_n, dv_n) = near_back
    d_chip = order.after(d_chip)
    down.receive().add()

    @fence
    def far_back():
        d_other = order.after(swap_core(d_chip))
        dq_f, dk_f, dv_f = order.done(
            *attend_backward(
                q_f, (*d_chip, *d_other), w_out, attn_f, lse_f, k_low, v_low, cos_tab[far],
                sin_tab[far], begins, far_pos,
            )
        )
        dkv_n, dkv_f = order.done(
            *key_value_rows(dk_n, dk_f, dv_n, dv_f, cos_tab, sin_tab, block_pos)
        )
        in_sum = chip_sum(*shares((dq_f, dkv_f), (w_query, w_kv)))
        return d_other, dq_f, dkv_n, dkv_f, in_sum

    d_other, dq_f, dkv_n, dkv_f, in_sum = far_back
    d_in_came = swap_chip(in_sum)
    gate.receive()
    up.receive()
    gate.add().send()
    up.add().send()
    to_pair = swap_pair(fence(block_sum.diag_sum), dp_size)
    qkv = fence(
        lambda: gradient([((normed_n,), (dq_n, dkv_n)), ((normed_f,), (dq_f, dkv_f))], late_bits)
    )
    gate.receive().add()
    qkv = reduction(qkv, late_bits)
    qkv.send()
    wout = fence(
        lambda: gradient([((*d_own, *d_core), (attn_n,)), ((*d_chip, *d_other), (attn_f,))], bits)
    )
    wout = reduction(wout, bits)
    wout.send()

    @fence
    def near_shares():
        kept, core = shares((dq_n, dkv_n), (w_query, w_kv))
        return kept, order.after(core)

    kept_in, core_in = near_shares
    d_in_came = order.after(d_in_came)

    def back_in(kept, core, chip, resid, d_mid, gain):
        return (d_mid + norm_back(kept + core + chip, resid, rms_inverse(resid), gain),)

    (x_grad,) = by_rows(
        back_in, (kept_in, core_in, d_in_came, x_own, d_mid), (norm_attn,), (jnp.float32,)
    )
    x_grad = order.done(x_grad)
    up.receive()
    up.add().send()
    chip_shares, pair_shares = fence(block_sum.side_shares)
    to_pair = order.after(to_pair)
    up.receive()
    block_p = swap_pair(total(*pair_shares), dp_size)
    block_c = swap_chip(total(*chip_shares, to_pair))
    up.add()
    kept, core = fence(block_sum.own)
    wout.advance()
    qkv.advance()
    wout.advance()
    block_c, block_p = order.after(block_c, block_p)
    (block_out,) = by_rows(
        lambda *items: (sum(items),),
        (resid_mid, kept, core, block_c, block_p),
        (),
        (jnp.bfloat16,),
    )
    block_out = order.done(block_out)
    qkv.advance()
    for item in (down, gate, up, wout, qkv):
        item.finish()
    grad_down, grad_gate, grad_up = down.total.T, gate.total, up.total
    grad_out, grad_qkv = wout.total.T, qkv.total
    queries = w_query.shape[1]
    grad_query = grad_qkv[:, :queries]
    grad_key = grad_qkv[:, queries : queries + HD]
    grad_value = grad_qkv[:, queries + HD :]

    share = width // dp_size

    def own_features(value):
        return lax.dynamic_slice_in_dim(value, index * share, share, 0).astype(jnp.float32)

    gain_attn = (
        jnp.sum(own_features(w_query) * grad_query, axis=1)
        + jnp.sum(own_features(w_kv) * grad_qkv[:, queries:], axis=1)
    ) / own_features(norm_attn)
    gain_mlp = jnp.sum(
        own_features(w_gate) * grad_gate + own_features(w_up) * grad_up, axis=1
    ) / own_features(norm_mlp)
    gains = jnp.stack([gain_attn, gain_mlp]).reshape(2, 4, share // 4)
    gains = jnp.stack([lax.dynamic_index_in_dim(gains, place ^ m, 1, False) for m in range(4)])
    gains = gains[:2] + lax.ppermute(gains[2:], "tensor", [(i, i ^ 2) for i in range(4)])
    gains = gains[0] + lax.ppermute(gains[1], "tensor", [(i, i ^ 1) for i in range(4)])

    return (
        block_out,
        x_grad,
        gains[0],
        grad_query,
        grad_key,
        grad_value,
        grad_out,
        gains[1],
        grad_gate,
        grad_up,
        grad_down,
    )


def solution(mesh):
    in_specs = (
        P(("dp", "tensor"), None),
        P(("dp", "tensor"), None),
        P("dp", None),
        P("dp"),
        P(),
        P(None, "tensor"),
        P(None, "tensor"),
        P(None, "tensor"),
        P("tensor", None),
        P(),
        P(None, "tensor"),
        P(None, "tensor"),
        P("tensor", None),
    )
    out_specs = (
        P(("dp", "tensor"), None),
        P(("dp", "tensor"), None),
        P(("dp", "tensor")),
        P("dp", "tensor"),
        P("dp", "tensor"),
        P("dp", "tensor"),
        P("tensor", "dp"),
        P(("dp", "tensor")),
        P("dp", "tensor"),
        P("dp", "tensor"),
        P("tensor", "dp"),
    )
    return jax.shard_map(
        functools.partial(per_device, mesh.shape["dp"]),
        mesh=mesh,
        in_specs=in_specs,
        out_specs=out_specs,
        check_vma=False,
    )
```

```python
import functools

import jax
import jax.numpy as jnp
from jax import lax
from jax.experimental import pallas as pl
from jax.experimental.pallas import tpu as pltpu
from jax.sharding import PartitionSpec as P

HD = 64
SEQ = 1024
PIECE = 256
QB = 256


EPSILON = 1e-05
ROPE_BASE = 10000.0
MASKED = -1e30
VMEM_LIMIT = 48 * 2**20
PARTS = 1
OUTER_BLOCKS = 2
PAIR = 2
NT = (((1,), (1,)), ((), ()))
TN = (((0,), (0,)), ((), ()))


def dot(left, right):
    return jnp.dot(left, right, preferred_element_type=jnp.float32)


def contract_rows(left, right):
    return lax.dot_general(left, right, TN, preferred_element_type=jnp.float32)


def contract_cols(left, right):
    return lax.dot_general(left, right, NT, preferred_element_type=jnp.float32)


def rms_inverse(resid):
    return lax.rsqrt(jnp.mean(resid * resid, axis=-1, keepdims=True) + EPSILON)


def norm_back(d_norm, resid, inverse, gain):
    scaled = d_norm * gain
    return inverse * scaled - resid * (inverse * inverse * inverse) * jnp.mean(
        scaled * resid, axis=-1, keepdims=True
    )


def rope_tables(positions):
    half_dim = HD // 2
    inverse = jnp.power(ROPE_BASE, -(jnp.arange(half_dim).astype(jnp.float32) * 2.0) / HD)
    angles = positions.astype(jnp.float32)[:, None] * inverse[None, :]
    cos, sin = jnp.cos(angles), jnp.sin(angles)
    return jnp.concatenate([cos] * 4, axis=1), jnp.concatenate([-sin, sin] * 2, axis=1)


def swap_halves(pair):
    lane = lax.broadcasted_iota(jnp.int32, pair.shape, 1)
    up = pltpu.roll(pair, 2 * HD - HD // 2, 1)
    down = pltpu.roll(pair, HD // 2, 1)
    return jnp.where(lane % HD < HD // 2, up, down)


def rotate_rows(grad, cos_tab, sin_tab):
    half = HD // 2
    swapped = jnp.concatenate([grad[:, half:], grad[:, :half]], axis=1)
    return grad * cos_tab[:, :HD] - swapped * sin_tab[:, :HD]


def either(near_refs):
    half = len(near_refs) // 2
    own, core = (
        jnp.concatenate([ref[...] for ref in refs], axis=0)
        for refs in (near_refs[:half], near_refs[half:])
    )
    return jnp.where(pl.program_id(0) == 0, own, core)


def project_kernel(*refs):
    x_refs = refs[:-9]
    gain_ref, wq_ref, wkv_ref, cos_ref, sin_ref, n_ref, q_ref, k_ref, v_ref = refs[-9:]
    resid = either(x_refs).astype(jnp.float32)
    normed = (resid * rms_inverse(resid) * gain_ref[...]).astype(jnp.bfloat16)
    n_ref[...] = normed
    cos, sin = cos_ref[...], sin_ref[...]
    query = dot(normed, wq_ref[...])
    for first in range(0, query.shape[1], 2 * HD):
        pair = query[:, first : first + 2 * HD]
        turned = (pair * cos + swap_halves(pair) * sin) * HD ** (-0.5)
        q_ref[:, first : first + 2 * HD] = turned.astype(jnp.bfloat16)
    key_value = dot(normed, wkv_ref[...])
    turned = key_value * cos + swap_halves(key_value) * sin
    k_ref[...] = turned[:, :HD].astype(jnp.bfloat16)
    v_ref[...] = key_value[:, HD:].astype(jnp.bfloat16)


def whole(array):
    return pl.BlockSpec(array.shape, lambda *_: (0,) * len(array.shape))


def params():
    return {
        "compiler_params": pltpu.CompilerParams(vmem_limit_bytes=VMEM_LIMIT),
        "cost_estimate": pl.CostEstimate(flops=1, bytes_accessed=1, transcendentals=0),
    }


def project(parts, gain, w_query, w_kv, cos_tab, sin_tab):
    rows, width = sum(part.shape[0] for part in parts) // 2, parts[0].shape[1]
    queries = w_query.shape[1]

    def tall(cols):
        return pl.BlockSpec((rows, cols), lambda i: (i, 0))

    gain = gain[None, :]
    return pl.pallas_call(
        project_kernel,
        grid=(2,),
        in_specs=[
            *(whole(item) for item in (*parts, gain, w_query, w_kv)), tall(2 * HD), tall(2 * HD)
        ],
        out_specs=[tall(width), tall(queries), tall(HD), tall(HD)],
        out_shape=[
            jax.ShapeDtypeStruct((2 * rows, width), jnp.bfloat16),
            jax.ShapeDtypeStruct((2 * rows, queries), jnp.bfloat16),
            jax.ShapeDtypeStruct((2 * rows, HD), jnp.bfloat16),
            jax.ShapeDtypeStruct((2 * rows, HD), jnp.bfloat16),
        ],
        name="project",
        **params(),
    )(*parts, gain, w_query, w_kv, cos_tab, sin_tab)


def by_rows(function, ins, consts, outs):
    flat, counts = [], []
    for item in ins:
        item = item if isinstance(item, tuple) else (item,)
        counts.append([len(flat) + sum(one is not None for one in item[:i]) if part is not None else None
                       for i, part in enumerate(item)])
        flat.extend(part for part in item if part is not None)
    rows, width = sum(flat[at].shape[0] for at in counts[0]), flat[0].shape[1]
    out_counts = [PARTS if isinstance(item, tuple) else 1 for item in outs]
    dtypes = [item[0] if isinstance(item, tuple) else item for item in outs]
    starts = [sum(out_counts[:i]) for i in range(len(outs))]
    out_places = [range(first, first + count) for first, count in zip(starts, out_counts)]
    step = 32

    def kernel(*refs):
        given = [ref[...] for ref in refs[len(flat) : len(flat) + len(consts)]]

        def views(part_refs, places, part):
            found = []
            for place in places:
                each = PARTS // len(place)
                at = place[part // each]
                ref = None if at is None else part_refs[at]
                found.append((ref, part % each * (rows // PARTS)))
            return found

        for part in range(PARTS):
            sources = views(refs, counts, part)
            targets = views(refs[len(flat) + len(consts) :], out_places, part)

            def chunk(i, _):
                def at(base):
                    return pl.ds(pl.multiple_of(base + i * step, step), step)

                values = [
                    0.0 if ref is None else ref[at(base), :].astype(jnp.float32)
                    for ref, base in sources
                ]
                for (ref, base), value in zip(targets, function(*values, *given)):
                    ref[at(base), :] = value.astype(ref.dtype)
                return 0

            lax.fori_loop(0, rows // PARTS // step, chunk, 0)

    consts = [item[None, :] for item in consts]
    shapes = []
    for count, dtype in zip(out_counts, dtypes):
        shapes.extend([jax.ShapeDtypeStruct((rows // count, width), dtype)] * count)
    results = pl.pallas_call(kernel, out_shape=shapes, name="by_rows", **params())(*flat, *consts)
    grouped, at = [], 0
    for count, item in zip(out_counts, outs):
        grouped.append(tuple(results[at : at + count]) if isinstance(item, tuple) else results[at])
        at += count
    return grouped


def see(qpos, kpos, starts_ref, pics):
    mask = kpos <= qpos
    for pic in range(pics):
        begin = starts_ref[pic]
        mask = mask | (
            (qpos >= begin) & (qpos < begin + PIECE) & (kpos >= begin) & (kpos < begin + PIECE)
        )
    return mask


def key_blocks(starts_ref, pics, first):
    edge = first + QB
    crossed = jnp.bool_(False)
    for pic in range(pics):
        begin = starts_ref[pic]
        crossed = crossed | ((begin < edge) & (begin + PIECE > edge))
    return edge // QB + jnp.where(crossed, 1, 0)


def forward_kernel(
    pos_ref, starts_ref, q_ref, k_ref, v_ref, out_ref, o_ref, lse_ref, kept_ref, *rest, heads, pics, seq
):
    *sent_refs, bias = rest
    first = pos_ref[pl.program_id(0)]
    count = key_blocks(starts_ref, pics, first)
    for blocks in range(1, seq // QB + 1):

        @pl.when(count == blocks)
        def _():
            ext = blocks * QB
            low = max(0, ext - 2 * QB)
            wide = ext - low
            qpos = lax.broadcasted_iota(jnp.int32, (QB, wide), 0) + first
            kpos = lax.broadcasted_iota(jnp.int32, (QB, wide), 1) + low
            bias[:, :wide] = jnp.where(see(qpos, kpos, starts_ref, pics), 0.0, MASKED)
            values = jnp.concatenate([v_ref[:ext, :], jnp.ones((ext, HD), jnp.bfloat16)], axis=1)
            lane = lax.broadcasted_iota(jnp.int32, (QB, heads), 1)

            def one_pair(pair, stats):
                at = pl.ds(pl.multiple_of(pair * 2 * HD, 2 * HD), 2 * HD)
                both = q_ref[:, at]
                outs = []
                for side in range(2):
                    scores = contract_cols(both[:, side * HD : (side + 1) * HD], k_ref[:ext, :])
                    if low:
                        scores = jnp.concatenate(
                            [scores[:, :low], scores[:, low:] + bias[:, :wide]], axis=1
                        )
                    else:
                        scores = scores + bias[:, :wide]
                    row_max = jnp.max(scores, axis=1, keepdims=True)
                    terms = jnp.exp(scores - row_max).astype(jnp.bfloat16)
                    summed = dot(terms, values)
                    row_sum = summed[:, HD : HD + 1]
                    outs.append(summed[:, :HD] / row_sum)
                    stats = jnp.where(lane == 2 * pair + side, row_max + jnp.log(row_sum), stats)
                o_ref[:, at] = jnp.concatenate(outs, axis=1).astype(jnp.bfloat16)
                return stats

            lse_ref[...] = lax.fori_loop(
                0, heads // 2, one_pair, jnp.zeros((QB, heads), jnp.float32), unroll=4
            )

    part = dot(o_ref[...], out_ref[...]).astype(jnp.bfloat16)

    @pl.when(pl.program_id(0) == 0)
    def _():
        kept_ref[...] = part

    @pl.when(pl.program_id(0) == 1)
    def _():
        for i, ref in enumerate(sent_refs):
            ref[...] = part[i * ref.shape[0] : (i + 1) * ref.shape[0]]


def attend_forward(q_low, k_low, v_low, w_out, starts, positions):
    rows, width = q_low.shape
    heads, seq, pics = width // HD, k_low.shape[0], starts.shape[0]
    tall = pl.BlockSpec((QB, width), lambda i, *_: (i, 0))
    parts = [(QB, w_out.shape[1])] + [(QB // PARTS, w_out.shape[1])] * PARTS
    keys = pl.BlockSpec((seq, HD), lambda i, *_: (0, 0))
    return pl.pallas_call(
        functools.partial(forward_kernel, heads=heads, pics=pics, seq=seq),
        grid_spec=pltpu.PrefetchScalarGridSpec(
            num_scalar_prefetch=2,
            grid=(rows // QB,),
            in_specs=[tall, keys, keys, whole(w_out)],
            out_specs=[
                tall,
                pl.BlockSpec((QB, heads), lambda i, *_: (i, 0)),
                *(pl.BlockSpec(part, lambda i, *_: (0, 0)) for part in parts),
            ],
            scratch_shapes=[pltpu.VMEM((QB, 2 * QB), jnp.float32)],
        ),
        out_shape=[
            jax.ShapeDtypeStruct((rows, width), jnp.bfloat16),
            jax.ShapeDtypeStruct((rows, heads), jnp.float32),
            *(jax.ShapeDtypeStruct(part, jnp.bfloat16) for part in parts),
        ],
        name="attend_forward",
        **params(),
    )(positions, starts, q_low, k_low, v_low, w_out)


def in_three(value):
    top = value.astype(jnp.bfloat16)
    rest = value - top.astype(jnp.float32)
    middle = rest.astype(jnp.bfloat16)
    last = (rest - middle.astype(jnp.float32)).astype(jnp.bfloat16)
    return [top, middle, last]


def backward_kernel(
    pos_ref, starts_ref, q_ref, out_ref, o_ref, lse_ref, k_ref, v_ref, cos_ref, sin_ref,
    *rest, heads, pics, seq
):
    *d_refs, dq_ref, dk_ref, dv_ref, bias, do_ref = rest
    first = pos_ref[pl.program_id(0)]
    count = key_blocks(starts_ref, pics, first)

    @pl.when(pl.program_id(0) == 0)
    def _():
        dk_ref[...] = jnp.zeros_like(dk_ref)
        dv_ref[...] = jnp.zeros_like(dv_ref)

    do_ref[...] = contract_cols(either(d_refs), out_ref[...]).astype(jnp.bfloat16)

    for blocks in range(1, seq // QB + 1):

        @pl.when(count == blocks)
        def _():
            ext = blocks * QB
            low = max(0, ext - 2 * QB)
            wide = ext - low
            kpos = lax.broadcasted_iota(jnp.int32, (wide, QB), 0) + low
            qpos = lax.broadcasted_iota(jnp.int32, (wide, QB), 1) + first
            bias[:wide, :] = jnp.where(see(qpos, kpos, starts_ref, pics), 0.0, MASKED)
            ones = jnp.ones((ext, HD), jnp.bfloat16)
            keys = jnp.concatenate([k_ref[:ext, :], ones], axis=1)
            values = jnp.concatenate([v_ref[:ext, :], ones], axis=1)
            zeros = jnp.zeros((QB, HD - 3), jnp.bfloat16)
            lane = lax.broadcasted_iota(jnp.int32, (QB, heads), 1)

            def one_pair(pair, _):
                at = pl.ds(pl.multiple_of(pair * 2 * HD, 2 * HD), 2 * HD)
                q_both, d_both, o_both = q_ref[:, at], do_ref[:, at], o_ref[:, at]
                stats = lse_ref[...]
                d_query, d_key, d_val = [], 0.0, 0.0
                for side in range(2):
                    cols = slice(side * HD, (side + 1) * HD)
                    queries, d_out = q_both[:, cols], d_both[:, cols]
                    delta = jnp.sum(
                        d_out.astype(jnp.float32) * o_both[:, cols].astype(jnp.float32),
                        axis=1,
                        keepdims=True,
                    )
                    lse = jnp.sum(
                        jnp.where(lane == 2 * pair + side, stats, 0.0), axis=1, keepdims=True
                    )
                    queries_ext = jnp.concatenate([queries] + in_three(-lse) + [zeros], axis=1)
                    d_out_ext = jnp.concatenate([d_out] + in_three(-delta) + [zeros], axis=1)
                    scores = contract_cols(keys, queries_ext)
                    if low:
                        scores = jnp.concatenate(
                            [scores[:low], scores[low:] + bias[:wide, :]], axis=0
                        )
                    else:
                        scores = scores + bias[:wide, :]
                    probs = jnp.exp(scores)
                    d_probs = contract_cols(values, d_out_ext)
                    d_scores = (probs * d_probs).astype(jnp.bfloat16)
                    d_val += dot(probs.astype(jnp.bfloat16), d_out)
                    d_key += dot(d_scores, queries)
                    d_query.append(contract_rows(d_scores, k_ref[:ext, :]))
                dk_ref[:ext, :] += d_key
                dv_ref[:ext, :] += d_val
                turned = jnp.concatenate(d_query, axis=1) * HD ** (-0.5)
                turned = turned * cos_ref[...] - swap_halves(turned) * sin_ref[...]
                dq_ref[:, at] = turned.astype(jnp.bfloat16)
                return 0

            lax.fori_loop(0, heads // 2, one_pair, 0, unroll=2)


def attend_backward(
    q_low, d_parts, w_out, attn_low, lse, k_low, v_low, cos_tab, sin_tab, starts, positions
):
    rows, width = q_low.shape
    heads, seq, pics = width // HD, k_low.shape[0], starts.shape[0]
    tall = pl.BlockSpec((QB, width), lambda i, *_: (i, 0))
    table = pl.BlockSpec((QB, 2 * HD), lambda i, *_: (i, 0))
    stats = pl.BlockSpec((QB, heads), lambda i, *_: (i, 0))
    keys = whole(k_low)
    return pl.pallas_call(
        functools.partial(backward_kernel, heads=heads, pics=pics, seq=seq),
        grid_spec=pltpu.PrefetchScalarGridSpec(
            num_scalar_prefetch=2,
            grid=(rows // QB,),
            in_specs=[
                tall, whole(w_out), tall, stats, keys, keys, table, table,
                *(whole(part) for part in d_parts),
            ],
            out_specs=[tall, keys, keys],
            scratch_shapes=[
                pltpu.VMEM((2 * QB, QB), jnp.float32),
                pltpu.VMEM((QB, width), jnp.bfloat16),
            ],
        ),
        out_shape=[
            jax.ShapeDtypeStruct((rows, width), jnp.bfloat16),
            jax.ShapeDtypeStruct((seq, HD), jnp.float32),
            jax.ShapeDtypeStruct((seq, HD), jnp.float32),
        ],
        name="attend_backward",
        **params(),
    )(
        positions, starts, q_low, w_out, attn_low, lse, k_low, v_low, cos_tab, sin_tab, *d_parts
    )


def feed_kernel(*refs, counts):
    gate_ref, up_ref, down_ref, hidden_ref, d_gate_ref, d_up_ref, normed, cots = refs[sum(counts) :]

    @pl.when(pl.program_id(0) == 0)
    def _():
        for target, sources in ((normed, refs[: counts[0]]), (cots, refs[counts[0] : sum(counts)])):
            at = 0
            for ref in sources:
                target[at : at + ref.shape[0], :] = ref[...]
                at += ref.shape[0]

    gate_val, up_val = dot(normed[...], gate_ref[...]), dot(normed[...], up_ref[...])
    d_hidden = contract_cols(cots[...], down_ref[...])
    gate_sig = jax.nn.sigmoid(gate_val)
    swish = gate_val * gate_sig
    hidden_ref[...] = (swish * up_val).astype(jnp.bfloat16)
    d_gate = d_hidden * up_val * (gate_sig + swish * (1.0 - gate_sig))
    d_gate_ref[...] = d_gate.astype(jnp.bfloat16)
    d_up_ref[...] = (d_hidden * swish).astype(jnp.bfloat16)


def feed_forward(normed, cots, w_gate, w_up, w_down):
    rows, width = sum(item.shape[0] for item in normed), normed[0].shape[1]
    units, tile = w_gate.shape[1], 256
    cols = pl.BlockSpec((width, tile), lambda j: (0, j))
    out = pl.BlockSpec((rows, tile), lambda j: (0, j))
    return pl.pallas_call(
        functools.partial(feed_kernel, counts=(len(normed), len(cots))),
        grid=(pl.cdiv(units, tile),),
        in_specs=[
            *(whole(item) for item in (*normed, *cots)),
            cols,
            cols,
            pl.BlockSpec((tile, width), lambda j: (j, 0)),
        ],
        out_specs=[out] * 3,
        out_shape=[jax.ShapeDtypeStruct((rows, units), jnp.bfloat16)] * 3,
        scratch_shapes=[pltpu.VMEM((rows, width), jnp.bfloat16)] * 2,
        name="feed_forward",
        **params(),
    )(*normed, *cots, w_gate, w_up, w_down)


def share_kernel(*refs, count, transposed):
    outs = refs[2 * count :]
    multiply = contract_cols if transposed else dot
    part = multiply(refs[0][...], refs[count][...])
    for left, right in zip(refs[1:count], refs[count + 1 : 2 * count]):
        part = part + multiply(left[...], right[...])
    rows = outs[0].shape[0]
    for place, ref in enumerate(outs):
        ref[...] = part[place * rows : (place + 1) * rows].astype(jnp.bfloat16)


def row_shares(lefts, rights, transposed, rows):
    blocks = lefts[0].shape[0] // rows
    width, tile = rights[0].shape[0 if transposed else 1], 512

    def right_spec(item):
        if transposed:
            return pl.BlockSpec((tile, item.shape[1]), lambda j: (j, 0))
        return pl.BlockSpec((item.shape[0], tile), lambda j: (0, j))

    return pl.pallas_call(
        functools.partial(share_kernel, count=len(lefts), transposed=transposed),
        grid=(width // tile,),
        in_specs=[*(whole(item) for item in lefts), *(right_spec(item) for item in rights)],
        out_specs=[pl.BlockSpec((rows, tile), lambda j: (0, j))] * blocks,
        out_shape=[jax.ShapeDtypeStruct((rows, width), jnp.bfloat16)] * blocks,
        name="row_shares",
        **params(),
    )(*lefts, *rights)


def outer_kernel(order_ref, *refs, shape, pieces):
    outs, refs = refs[-2 * len(pieces) :], list(refs[: -2 * len(pieces)])
    totals = None
    for lefts, rights in shape:
        rows = jnp.concatenate(
            [
                jnp.concatenate([refs.pop(0)[...] for _ in range(OUTER_BLOCKS)], axis=1)
                for _ in range(lefts)
            ],
            axis=0,
        )
        parts = [contract_rows(rows, refs.pop(0)[...]) for _ in range(rights)]
        totals = parts if totals is None else [a + b for a, b in zip(totals, parts)]
    step = pl.program_id(0)
    half = pl.num_programs(0) // 2
    for place, piece in enumerate(pieces):
        total = jnp.concatenate(totals[piece], axis=1).astype(jnp.bfloat16)

        @pl.when(step < half)
        def _():
            outs[2 * place][...] = total

        @pl.when(step >= half)
        def _():
            outs[2 * place + 1][...] = total


def outer(sections, index, bits, pieces):
    width = sections[0][0][0].shape[1]
    share = width // (1 << len(bits))
    tile = 256
    if share == tile:
        blocks = jnp.stack([index ^ item for item in block_order(bits)]).astype(jnp.int32)
    else:
        blocks = jnp.arange(width // tile, dtype=jnp.int32)
        sections = [
            ([permuted_features(item, index, bits) for item in lefts], rights)
            for lefts, rights in sections
        ]
    count = width // tile // OUTER_BLOCKS
    sizes = [sum(item.shape[1] for item in sections[0][1][piece]) for piece in pieces]
    specs, arrays = [], []
    for lefts, rights in sections:
        for item in lefts:
            for i in range(OUTER_BLOCKS):
                specs.append(
                    pl.BlockSpec(
                        (item.shape[0], tile), lambda j, b, i=i: (0, b[j * OUTER_BLOCKS + i])
                    )
                )
                arrays.append(item)
        specs.extend(whole(item) for item in rights)
        arrays.extend(rights)
    return pl.pallas_call(
        functools.partial(
            outer_kernel,
            shape=[(len(lefts), len(rights)) for lefts, rights in sections],
            pieces=pieces,
        ),
        grid_spec=pltpu.PrefetchScalarGridSpec(
            num_scalar_prefetch=1,
            grid=(count,),
            in_specs=specs,
            out_specs=[
                pl.BlockSpec((tile * OUTER_BLOCKS, size), at)
                for size in sizes
                for at in (
                    lambda j, _: (jnp.minimum(j, count // 2 - 1), 0),
                    lambda j, _: (jnp.maximum(j - count // 2, 0), 0),
                )
            ],
        ),
        out_shape=[
            jax.ShapeDtypeStruct((width // 2, size), jnp.bfloat16) for size in sizes for _ in range(2)
        ],
        name="outer",
        **params(),
    )(blocks, *arrays)


def halves_kernel(kept_a, kept_b, came_a, came_b, sent_ref, kept_ref):
    sent_ref[...] = added(kept_a[...], came_a[...])
    kept_ref[...] = added(kept_b[...], came_b[...])


def add_halves(kept, came):
    half, columns = kept.shape[0] // 2, kept.shape[1]
    block = min(256, half)
    first = pl.BlockSpec((block, columns), lambda i: (i, 0))
    second = pl.BlockSpec((block, columns), lambda i: (i + half // block, 0))
    return pl.pallas_call(
        halves_kernel,
        grid=(half // block,),
        in_specs=[first, second, first, second],
        out_specs=[first, first],
        out_shape=[jax.ShapeDtypeStruct((half, columns), jnp.bfloat16)] * 2,
        name="add_halves",
        **params(),
    )(kept, kept, came, came)


def total_kernel(kept_ref, came_ref, out_ref):
    out_ref[...] = kept_ref[...].astype(jnp.float32) + came_ref[...].astype(jnp.float32)


def add_total(kept, came):
    return pl.pallas_call(
        total_kernel,
        out_shape=jax.ShapeDtypeStruct(kept.shape, jnp.float32),
        name="add_total",
        **params(),
    )(kept, came)


def key_value_kernel(
    at_ref, dkn_ref, dkf_ref, dvn_ref, dvf_ref, cosn_ref, sinn_ref, cosf_ref, sinf_ref, near_ref, far_ref
):
    rows = dkn_ref.shape[0] // 4
    for m in range(4):
        at = pl.ds(pl.multiple_of(at_ref[m], rows), rows)
        mine = slice(m % 2 * rows, (m % 2 + 1) * rows)
        cos_ref, sin_ref = (cosn_ref, sinn_ref) if m < 2 else (cosf_ref, sinf_ref)
        d_key = dkn_ref[at, :] + dkf_ref[at, :]
        d_val = dvn_ref[at, :] + dvf_ref[at, :]
        both = jnp.concatenate([d_key, d_val], axis=1)
        turned = both * cos_ref[mine, :] - swap_halves(both) * sin_ref[mine, :]
        both = jnp.concatenate([turned[:, :HD], d_val], axis=1).astype(jnp.bfloat16)
        target = near_ref if m < 2 else far_ref
        target[mine, :] = both


def key_value_rows(dk_n, dk_f, dv_n, dv_f, tables, block_pos):
    shape = jax.ShapeDtypeStruct((dk_n.shape[0] // 2, 2 * HD), jnp.bfloat16)
    arrays = (dk_n, dk_f, dv_n, dv_f, *tables)
    return pl.pallas_call(
        key_value_kernel,
        grid_spec=pltpu.PrefetchScalarGridSpec(
            num_scalar_prefetch=1,
            grid=(1,),
            in_specs=[whole(item) for item in arrays],
            out_specs=[whole(shape), whole(shape)],
        ),
        out_shape=[shape, shape],
        name="key_value_rows",
        **params(),
    )(block_pos, *arrays)


def swapped(parts, flip):
    pairs = [(i, i ^ flip) for i in range(4)]
    return tuple(lax.ppermute(part, "tensor", pairs) for part in parts)


def swap_core(parts):
    return swapped(parts, 1)


def swap_chip(parts):
    return swapped(parts, 2)


def swap_pair(parts, size):
    return tuple(exchange(part, PAIR, size) for part in parts)


class Order:
    def __init__(self):
        self.last = ()

    def after(self, *values):
        tied = lax.optimization_barrier(values + (self.last,))[: len(values)]
        self.last = tied
        return tied if len(values) > 1 else tied[0]

    def done(self, *values):
        values = lax.optimization_barrier(values + (self.last,))[: len(values)]
        self.last = values
        return values if len(values) > 1 else values[0]


def wait_for(value, *others):
    return lax.optimization_barrier((value,) + others)[0]


def rows_of(one, two):
    return jnp.concatenate([one, two], axis=0)


def block_order(bits):
    order = [0]
    for bit in reversed(bits):
        order = [item ^ bit for item in order] + order
    return order


def permuted_features(value, index, bits):
    order = block_order(bits)
    width = value.shape[1] // len(order)
    return jnp.concatenate(
        [lax.dynamic_slice_in_dim(value, (index ^ item) * width, width, 1) for item in order], axis=1
    )


def rows_and_cols(one, two):
    return jnp.concatenate([one, two], axis=1)


def exchange(value, bit, size):
    return lax.ppermute(value, "dp", [(i, i ^ bit) for i in range(size)])


class Reduction:
    def __init__(self, order, sent, kept, bits, size, assemble=None):
        self.order, self.sent, self.kept, self.assemble = order, sent, kept, assemble
        self.bits, self.size, self.step = bits, size, 0
        self.total = None

    def send(self, *others):
        sent = wait_for(self.sent, *others) if others else self.sent
        self.came = exchange(sent, self.bits[self.step], self.size)
        return self

    def receive(self):
        self.came = self.order.after(self.came)
        return self

    def add(self):
        kept, came = self.kept, self.came
        self.step += 1
        if self.step == len(self.bits):
            self.total = self.order.done((self.assemble or add_total)(kept, came))
        else:
            self.sent, self.kept = self.order.done(*add_halves(kept, came))
        return self

    def advance(self):
        self.receive().add()
        if self.total is None:
            self.send()

    def finish(self):
        while self.total is None:
            self.advance()
        return self.total


def added(one, two):
    return (one.astype(jnp.float32) + two.astype(jnp.float32)).astype(jnp.bfloat16)


def per_device(
    dp_size,
    layer_input,
    cotangent,
    starts,
    pieces,
    norm_attn,
    w_query,
    w_key,
    w_value,
    w_out,
    norm_mlp,
    w_gate,
    w_up,
    w_down,
):
    rows = layer_input.shape[0]
    width = layer_input.shape[1]
    place = lax.axis_index("tensor")
    index = lax.axis_index("dp")
    bits = [1 << i for i in range(dp_size.bit_length() - 1)]
    late_bits = bits[1:] + bits[:1]
    begins = starts[0]

    block_pos = jnp.stack([(place ^ m) * rows for m in range(4)]).astype(jnp.int32)
    near_pos, far_pos = block_pos[:2], block_pos[2:]
    row_pos = (block_pos[:, None] + jnp.arange(rows, dtype=jnp.int32)[None, :]).reshape(-1)
    (cos_n, sin_n), (cos_f, sin_f) = (
        rope_tables(half) for half in (row_pos[: 2 * rows], row_pos[2 * rows :])
    )
    w_kv = jnp.concatenate([w_key, w_value], axis=1)

    def in_sequence(value):
        return jnp.concatenate(
            [lax.dynamic_slice_in_dim(value, (place ^ b) * rows, rows, 0) for b in range(4)], axis=0
        )

    def in_two(value):
        return tuple(jnp.split(value, PARTS, axis=0))

    order = Order()
    near, far = slice(0, 2 * rows), slice(2 * rows, 4 * rows)

    def chip_sum(kept, came):
        came = order.after(came)
        return order.done(*by_rows(lambda a, b: (a + b,), (kept, came), (), ((jnp.bfloat16,),)))

    x_own, cot_own = in_two(layer_input), in_two(cotangent)
    x_chip, x_core = swap_chip(x_own), swap_core(x_own)

    side = index // PAIR % 2
    units, queries = w_gate.shape[1], w_query.shape[1]
    window = -(-units // 256) * 128
    overlap = 2 * window - units
    mine = (jnp.arange(window) >= overlap) | (side == 0)
    gate_half = lax.dynamic_slice_in_dim(w_gate, side * (units - window), window, 1)
    up_half = lax.dynamic_slice_in_dim(w_up, side * (units - window), window, 1)
    up_half = jnp.where(mine[None, :], up_half, 0).astype(jnp.bfloat16)
    down_half = lax.dynamic_slice_in_dim(w_down, side * (units - window), window, 0)
    down_half = jnp.where(mine[:, None], down_half, 0).astype(jnp.bfloat16)
    gate_half, up_half, down_half, w_kv, cos_n, sin_n, cos_f, sin_f = order.done(
        gate_half, up_half, down_half, w_kv, cos_n, sin_n, cos_f, sin_f
    )
    normed_n, q_n, k_n, v_n = order.done(
        *project((*x_own, *x_core), norm_attn, w_query, w_kv, cos_n, sin_n)
    )
    x_chip = order.after(x_chip)
    cot_own_ = wait_for(cot_own, x_chip)
    cot_chip, cot_core, cot_pair = (
        swap_chip(cot_own_), swap_core(cot_own_), swap_pair(cot_own_, dp_size)
    )
    normed_f, q_f, k_f, v_f = order.done(
        *project((*x_chip, *swap_core(x_chip)), norm_attn, w_query, w_kv, cos_f, sin_f)
    )
    k_low = in_sequence(rows_of(k_n, k_f))
    v_low = in_sequence(rows_of(v_n, v_f))
    attn_f, lse_f, kept, *sent = order.done(
        *attend_forward(q_f, k_low, v_low, w_out, begins, far_pos)
    )
    came = swap_core(sent)
    cot_chip, cot_pair = order.after(cot_chip, cot_pair)
    cot_diag, cot_other, cot_pcore = (
        swap_pair(cot_chip, dp_size), swap_core(cot_chip), swap_core(cot_pair)
    )
    attn_came = swap_chip(chip_sum(kept, came))
    cot_core, cot_other, cot_pcore, q_n = order.after(cot_core, cot_other, cot_pcore, q_n)
    attn_n, lse_n, kept, *sent = order.done(
        *attend_forward(q_n, k_low, v_low, w_out, begins, near_pos)
    )
    sum_came = swap_core(sent)
    cot_diag = order.after(cot_diag)
    cot_dcore = swap_core(cot_diag)
    attn_came = order.after(attn_came)
    sum_came, cot_dcore = order.after(sum_came, cot_dcore)

    def norm_mid(x, kept, core, chip, gain):
        resid = x + (kept + core + chip)
        return resid, resid * rms_inverse(resid) * gain

    resid_mid, mlp_own = order.done(
        *by_rows(
            norm_mid, (x_own, kept, sum_came, attn_came), (norm_mlp,), (jnp.float32, (jnp.bfloat16,))
        )
    )
    mlp_core, mlp_chip, mlp_pair = swap_core(mlp_own), swap_chip(mlp_own), swap_pair(mlp_own, dp_size)
    mlp_core = order.after(mlp_core)

    def feed(normed, cots):
        return order.done(*feed_forward(normed, cots, gate_half, up_half, down_half))

    near_hidden = feed((*mlp_own, *mlp_core), (*cot_own, *cot_core))
    mlp_chip, mlp_pair = order.after(mlp_chip, mlp_pair)
    half = rows // 2
    mlp_diag = (
        *swap_chip((mlp_pair[0][:half],)), *swap_pair((mlp_chip[0][half:],), dp_size)
    )
    mlp_other, mlp_pcore = order.after(swap_core(mlp_chip), swap_core(mlp_pair))
    side_hidden = feed(
        (*mlp_chip, *mlp_other, *mlp_pair, *mlp_pcore),
        (*cot_chip, *cot_other, *cot_pair, *cot_pcore),
    )
    mlp_diag = order.after(mlp_diag)
    mlp_dcore = order.after(swap_core(mlp_diag))
    diag_hidden = feed((*mlp_diag, *mlp_dcore), (*cot_diag, *cot_dcore))
    hiddens = (near_hidden, side_hidden, diag_hidden)

    def in_window(kept, came):
        first = jnp.where(side == 0, kept, came)
        second = jnp.where(side == 0, came, kept)
        return jnp.concatenate([first, second[:, overlap:]], axis=1).astype(jnp.float32)

    pair_bits = [bit for bit in bits if bit != PAIR] + [PAIR]
    always = begins[0] >= 0

    def fence(step):
        def inside():
            outer_last, order.last = order.last, ()
            try:
                return step()
            finally:
                order.last = outer_last

        shapes = jax.eval_shape(inside)
        taken = order.after(always)
        results = lax.cond(
            taken,
            inside,
            lambda: jax.tree.map(lambda item: jnp.zeros(item.shape, item.dtype), shapes),
        )
        leaves, tree = jax.tree.flatten(results)
        return jax.tree.unflatten(tree, order.done(tuple(leaves)))

    def gradient(sections, order_bits, pieces=(slice(None),)):
        lefts, rights = order.after([item[0] for item in sections], [item[1] for item in sections])
        return order.done(*outer(list(zip(lefts, rights)), index, order_bits, pieces))

    cots = (
        (*cot_own, *cot_core),
        (*cot_chip, *cot_other, *cot_pair, *cot_pcore),
        (*cot_diag, *cot_dcore),
    )
    mlps = (
        (*mlp_own, *mlp_core),
        (*mlp_chip, *mlp_other, *mlp_pair, *mlp_pcore),
        (*mlp_diag, *mlp_dcore),
    )

    def mlp_gradients(lefts, which):
        sections = [(left, [right[i] for i in which]) for left, right in zip(lefts, hiddens)]
        return gradient(sections, pair_bits, [slice(i, i + 1) for i in range(len(which))])

    def reduction(sent_kept, order_bits, assemble=None):
        return Reduction(order, *sent_kept, order_bits, dp_size, assemble)

    def shares(lefts, rights, transposed=True):
        parts = order.done(*row_shares(order.after(lefts), rights, transposed, rows))
        return [(parts[i], swap_core((parts[i + 1],))) for i in range(0, len(parts), 2)]

    def total(*items):
        return order.done(*by_rows(lambda *values: (sum(values),), items, (), ((jnp.bfloat16,),)))

    class GroupSum:
        def __init__(self, which, rights, transposed):
            self.rest = rights, transposed
            self.near, self.sides, self.diag = (tuple(item[i] for i in which) for item in hiddens)

        def diag_shares(self):
            return shares(self.diag, *self.rest)[0]

        def side_shares(self):
            return shares(self.sides, *self.rest)

        def own_shares(self):
            return shares(self.near, *self.rest)[0]

    d_norm = GroupSum((1, 2), (gate_half, up_half), True)
    block_sum = GroupSum((0,), (down_half,), False)

    down = reduction(mlp_gradients(cots, (0,)), pair_bits, in_window)
    down.send()

    @fence
    def diag_and_gradients():
        kept, came = d_norm.diag_shares()
        made = mlp_gradients(mlps, (1, 2))
        return chip_sum(kept, came), made

    diag, made = diag_and_gradients
    to_pair = swap_pair(diag, dp_size)
    gate, up = (reduction(item, pair_bits, in_window) for item in (made[:2], made[2:]))

    @fence
    def other_shares():
        chip, pair = d_norm.side_shares()
        own = d_norm.own_shares()
        return order.after(chip), order.after(pair), order.after(own)

    chip, pair, own = other_shares
    came_p = swap_pair(total(pair[0], *pair[1]), dp_size)
    to_pair = order.after(to_pair)
    came_c = swap_chip(total(chip[0], *chip[1], to_pair))
    down.receive()
    gate.send(down.came)
    down.add()
    down.send()

    @fence
    def block_shares():
        def parts(lefts):
            return order.done(*row_shares(order.after(lefts), *block_sum.rest, rows))

        kept, sent = parts(block_sum.diag)
        came = swap_core((sent,))
        kept_c, sent_c, kept_p, sent_p = parts(block_sum.sides)
        diag = chip_sum(kept, came)
        came_c = swap_core((order.after(sent_c),))
        kept, sent = parts(block_sum.near)
        came_c = order.after(came_c)
        came_p = order.after(swap_core((order.after(sent_p),)))
        came = order.after(swap_core((order.after(sent),)))
        return diag, (kept_c, came_c), (kept_p, came_p), (kept, came)

    block_diag, block_chip, block_pair, block_own = block_shares
    came_c, came_p = order.after(came_c, came_p)
    to_pair = swap_pair(block_diag, dp_size)

    def back_mid(kept, core, chip, pair, resid, cot, gain):
        d_mid = cot + norm_back(kept + core + chip + pair, resid, rms_inverse(resid), gain)
        return d_mid, d_mid

    d_mid, d_own = order.done(
        *by_rows(
            back_mid,
            (own[0], own[1], came_c, came_p, resid_mid, cot_own),
            (norm_mlp,),
            (jnp.float32, (jnp.bfloat16,)),
        )
    )
    d_chip = swap_chip(d_own)

    gate.receive()
    up.send(gate.came)
    gate.add()

    @fence
    def near_back():
        d_core = order.after(swap_core(d_own))
        return d_core, order.done(
            *attend_backward(
                q_n, (*d_own, *d_core), w_out, attn_n, lse_n, k_low, v_low, cos_n,
                sin_n, begins, near_pos,
            )
        )

    d_core, (dq_n, dk_n, dv_n) = near_back
    d_chip = order.after(d_chip)
    @fence
    def out_gradient():
        d_other = order.after(swap_core(d_chip))
        sections = [((*d_own, *d_core), (attn_n,)), ((*d_chip, *d_other), (attn_f,))]
        return d_other, gradient(sections, bits)

    d_other, wout = out_gradient
    wout = reduction(wout, bits)
    down.receive()
    gate.send(down.came)
    down.add().send()
    up.receive()
    wout.send(up.came)
    up.add()
    to_pair = order.after(to_pair)
    block_c = total(block_chip[0], *block_chip[1], to_pair)
    block_p = total(block_pair[0], *block_pair[1])

    @fence
    def far_back():
        return order.done(
            *attend_backward(
                q_f, (*d_chip, *d_other), w_out, attn_f, lse_f, k_low, v_low, cos_f,
                sin_f, begins, far_pos,
            )
        )

    dq_f, dk_f, dv_f = far_back

    @fence
    def query_gradient():
        dkv_n, dkv_f = order.done(
            *key_value_rows(dk_n, dk_f, dv_n, dv_f, (cos_n, sin_n, cos_f, sin_f), block_pos)
        )
        sections = [((normed_n,), (dq_n, dkv_n)), ((normed_f,), (dq_f, dkv_f))]
        return dkv_n, dkv_f, gradient(sections, bits)

    dkv_n, dkv_f, qkv = query_gradient
    qkv = reduction(qkv, bits)
    qkv.send()
    wout.receive()
    wout.add().send()
    down.receive().add()
    gate.receive()
    up.send(gate.came)
    gate.add().send()
    in_sum = fence(lambda: chip_sum(*shares((dq_f, dkv_f), (w_query, w_kv))[0]))
    gate.receive().add()
    d_in_came = swap_chip(in_sum)
    own = fence(lambda: order.after(shares((dq_n, dkv_n), (w_query, w_kv))[0]))
    qkv.receive()
    qkv.add().send()
    wout.receive()
    up.receive()
    up.add().send()
    wout.add().send()
    d_in_came = order.after(d_in_came)

    def back_in(kept, core, chip, resid, d_mid, gain):
        return (d_mid + norm_back(kept + core + chip, resid, rms_inverse(resid), gain),)

    (x_grad,) = by_rows(
        back_in, (own[0], own[1], d_in_came, x_own, d_mid), (norm_attn,), (jnp.float32,)
    )
    x_grad = order.done(x_grad)
    qkv.receive()
    block_p = swap_pair(wait_for(block_p, qkv.came), dp_size)
    block_c = swap_chip(wait_for(block_c, qkv.came))
    qkv.add().send()
    up.receive().add()
    wout.receive().add()
    block_c, block_p = order.after(block_c, block_p)
    qkv.receive().add()
    (block_out,) = by_rows(
        lambda *items: (sum(items),),
        (resid_mid, block_own[0], block_own[1], block_c, block_p),
        (),
        (jnp.bfloat16,),
    )
    block_out = order.done(block_out)
    for item in (down, gate, up, wout, qkv):
        item.finish()
    grad_down, grad_gate, grad_up = down.total.T, gate.total, up.total
    grad_out, grad_qkv = wout.total.T, qkv.total
    queries = w_query.shape[1]
    grad_query = grad_qkv[:, :queries]
    grad_key = grad_qkv[:, queries : queries + HD]
    grad_value = grad_qkv[:, queries + HD :]

    share = width // dp_size

    def own_features(value):
        return lax.dynamic_slice_in_dim(value, index * share, share, 0).astype(jnp.float32)

    gain_attn = (
        jnp.sum(own_features(w_query) * grad_query, axis=1)
        + jnp.sum(own_features(w_kv) * grad_qkv[:, queries:], axis=1)
    ) / own_features(norm_attn)
    gain_mlp = jnp.sum(
        own_features(w_gate) * grad_gate + own_features(w_up) * grad_up, axis=1
    ) / own_features(norm_mlp)
    gains = jnp.stack([gain_attn, gain_mlp]).reshape(2, 4, share // 4)
    gains = jnp.stack([lax.dynamic_index_in_dim(gains, place ^ m, 1, False) for m in range(4)])
    gains = gains[:2] + lax.ppermute(gains[2:], "tensor", [(i, i ^ 2) for i in range(4)])
    gains = gains[0] + lax.ppermute(gains[1], "tensor", [(i, i ^ 1) for i in range(4)])

    return (
        block_out,
        x_grad,
        gains[0],
        grad_query,
        grad_key,
        grad_value,
        grad_out,
        gains[1],
        grad_gate,
        grad_up,
        grad_down,
    )


def solution(mesh):
    in_specs = (
        P(("dp", "tensor"), None),
        P(("dp", "tensor"), None),
        P("dp", None),
        P("dp"),
        P(),
        P(None, "tensor"),
        P(None, "tensor"),
        P(None, "tensor"),
        P("tensor", None),
        P(),
        P(None, "tensor"),
        P(None, "tensor"),
        P("tensor", None),
    )
    out_specs = (
        P(("dp", "tensor"), None),
        P(("dp", "tensor"), None),
        P(("dp", "tensor")),
        P("dp", "tensor"),
        P("dp", "tensor"),
        P("dp", "tensor"),
        P("tensor", "dp"),
        P(("dp", "tensor")),
        P("dp", "tensor"),
        P("dp", "tensor"),
        P("tensor", "dp"),
    )
    return jax.shard_map(
        functools.partial(per_device, mesh.shape["dp"]),
        mesh=mesh,
        in_specs=in_specs,
        out_specs=out_specs,
        check_vma=False,
    )
```

```python
import functools

import jax
import jax.numpy as jnp
from jax import lax
from jax.experimental import pallas as pl
from jax.experimental.pallas import tpu as pltpu
from jax.sharding import PartitionSpec as P

HD = 64
SEQ = 1024
PIECE = 256
QB = 256


EPSILON = 1e-05
ROPE_BASE = 10000.0
MASKED = -1e30
VMEM_LIMIT = 48 * 2**20
PARTS = 1
OUTER_BLOCKS = 2
PAIR = 2
NT = (((1,), (1,)), ((), ()))
TN = (((0,), (0,)), ((), ()))


def dot(left, right):
    return jnp.dot(left, right, preferred_element_type=jnp.float32)


def contract_rows(left, right):
    return lax.dot_general(left, right, TN, preferred_element_type=jnp.float32)


def contract_cols(left, right):
    return lax.dot_general(left, right, NT, preferred_element_type=jnp.float32)


def rms_inverse(resid):
    return lax.rsqrt(jnp.mean(resid * resid, axis=-1, keepdims=True) + EPSILON)


def norm_back(d_norm, resid, inverse, gain):
    scaled = d_norm * gain
    return inverse * scaled - resid * (inverse * inverse * inverse) * jnp.mean(
        scaled * resid, axis=-1, keepdims=True
    )


def rope_tables(positions):
    half_dim = HD // 2
    inverse = jnp.power(ROPE_BASE, -(jnp.arange(half_dim).astype(jnp.float32) * 2.0) / HD)
    angles = positions.astype(jnp.float32)[:, None] * inverse[None, :]
    cos, sin = jnp.cos(angles), jnp.sin(angles)
    return jnp.concatenate([cos] * 4, axis=1), jnp.concatenate([-sin, sin] * 2, axis=1)


def swap_halves(pair):
    lane = lax.broadcasted_iota(jnp.int32, pair.shape, 1)
    up = pltpu.roll(pair, 2 * HD - HD // 2, 1)
    down = pltpu.roll(pair, HD // 2, 1)
    return jnp.where(lane % HD < HD // 2, up, down)


def rotate_rows(grad, cos_tab, sin_tab):
    half = HD // 2
    swapped = jnp.concatenate([grad[:, half:], grad[:, :half]], axis=1)
    return grad * cos_tab[:, :HD] - swapped * sin_tab[:, :HD]


def either(near_refs):
    half = len(near_refs) // 2
    own, core = (
        jnp.concatenate([ref[...] for ref in refs], axis=0)
        for refs in (near_refs[:half], near_refs[half:])
    )
    return jnp.where(pl.program_id(0) == 0, own, core)


def project_kernel(*refs):
    x_refs = refs[:-9]
    gain_ref, wq_ref, wkv_ref, cos_ref, sin_ref, n_ref, q_ref, k_ref, v_ref = refs[-9:]
    resid = either(x_refs).astype(jnp.float32)
    normed = (resid * rms_inverse(resid) * gain_ref[...]).astype(jnp.bfloat16)
    n_ref[...] = normed
    cos, sin = cos_ref[...], sin_ref[...]
    query = dot(normed, wq_ref[...])
    for first in range(0, query.shape[1], 2 * HD):
        pair = query[:, first : first + 2 * HD]
        turned = (pair * cos + swap_halves(pair) * sin) * HD ** (-0.5)
        q_ref[:, first : first + 2 * HD] = turned.astype(jnp.bfloat16)
    key_value = dot(normed, wkv_ref[...])
    turned = key_value * cos + swap_halves(key_value) * sin
    k_ref[...] = turned[:, :HD].astype(jnp.bfloat16)
    v_ref[...] = key_value[:, HD:].astype(jnp.bfloat16)


def whole(array):
    return pl.BlockSpec(array.shape, lambda *_: (0,) * len(array.shape))


def params():
    return {
        "compiler_params": pltpu.CompilerParams(vmem_limit_bytes=VMEM_LIMIT),
        "cost_estimate": pl.CostEstimate(flops=1, bytes_accessed=1, transcendentals=0),
    }


def project(parts, gain, w_query, w_kv, cos_tab, sin_tab):
    rows, width = sum(part.shape[0] for part in parts) // 2, parts[0].shape[1]
    queries = w_query.shape[1]

    def tall(cols):
        return pl.BlockSpec((rows, cols), lambda i: (i, 0))

    gain = gain[None, :]
    return pl.pallas_call(
        project_kernel,
        grid=(2,),
        in_specs=[
            *(whole(item) for item in (*parts, gain, w_query, w_kv)), tall(2 * HD), tall(2 * HD)
        ],
        out_specs=[tall(width), tall(queries), tall(HD), tall(HD)],
        out_shape=[
            jax.ShapeDtypeStruct((2 * rows, width), jnp.bfloat16),
            jax.ShapeDtypeStruct((2 * rows, queries), jnp.bfloat16),
            jax.ShapeDtypeStruct((2 * rows, HD), jnp.bfloat16),
            jax.ShapeDtypeStruct((2 * rows, HD), jnp.bfloat16),
        ],
        name="project",
        **params(),
    )(*parts, gain, w_query, w_kv, cos_tab, sin_tab)


def by_rows(function, ins, consts, outs):
    flat, counts = [], []
    for item in ins:
        item = item if isinstance(item, tuple) else (item,)
        counts.append([len(flat) + sum(one is not None for one in item[:i]) if part is not None else None
                       for i, part in enumerate(item)])
        flat.extend(part for part in item if part is not None)
    rows, width = sum(flat[at].shape[0] for at in counts[0]), flat[0].shape[1]
    out_counts = [PARTS if isinstance(item, tuple) else 1 for item in outs]
    dtypes = [item[0] if isinstance(item, tuple) else item for item in outs]
    starts = [sum(out_counts[:i]) for i in range(len(outs))]
    out_places = [range(first, first + count) for first, count in zip(starts, out_counts)]
    step = 32

    def kernel(*refs):
        given = [ref[...] for ref in refs[len(flat) : len(flat) + len(consts)]]

        def views(part_refs, places, part):
            found = []
            for place in places:
                each = PARTS // len(place)
                at = place[part // each]
                ref = None if at is None else part_refs[at]
                found.append((ref, part % each * (rows // PARTS)))
            return found

        for part in range(PARTS):
            sources = views(refs, counts, part)
            targets = views(refs[len(flat) + len(consts) :], out_places, part)

            def chunk(i, _):
                def at(base):
                    return pl.ds(pl.multiple_of(base + i * step, step), step)

                values = [
                    0.0 if ref is None else ref[at(base), :].astype(jnp.float32)
                    for ref, base in sources
                ]
                for (ref, base), value in zip(targets, function(*values, *given)):
                    ref[at(base), :] = value.astype(ref.dtype)
                return 0

            lax.fori_loop(0, rows // PARTS // step, chunk, 0)

    consts = [item[None, :] for item in consts]
    shapes = []
    for count, dtype in zip(out_counts, dtypes):
        shapes.extend([jax.ShapeDtypeStruct((rows // count, width), dtype)] * count)
    results = pl.pallas_call(kernel, out_shape=shapes, name="by_rows", **params())(*flat, *consts)
    grouped, at = [], 0
    for count, item in zip(out_counts, outs):
        grouped.append(tuple(results[at : at + count]) if isinstance(item, tuple) else results[at])
        at += count
    return grouped


def see(qpos, kpos, starts_ref, pics):
    mask = kpos <= qpos
    for pic in range(pics):
        begin = starts_ref[pic]
        mask = mask | (
            (qpos >= begin) & (qpos < begin + PIECE) & (kpos >= begin) & (kpos < begin + PIECE)
        )
    return mask


def key_blocks(starts_ref, pics, first):
    edge = first + QB
    crossed = jnp.bool_(False)
    for pic in range(pics):
        begin = starts_ref[pic]
        crossed = crossed | ((begin < edge) & (begin + PIECE > edge))
    return edge // QB + jnp.where(crossed, 1, 0)


def forward_kernel(
    pos_ref, starts_ref, q_ref, k_ref, v_ref, out_ref, o_ref, lse_ref, kept_ref, *rest, heads, pics, seq
):
    *sent_refs, bias = rest
    first = pos_ref[pl.program_id(0)]
    count = key_blocks(starts_ref, pics, first)
    for blocks in range(1, seq // QB + 1):

        @pl.when(count == blocks)
        def _():
            ext = blocks * QB
            low = max(0, ext - 2 * QB)
            wide = ext - low
            qpos = lax.broadcasted_iota(jnp.int32, (QB, wide), 0) + first
            kpos = lax.broadcasted_iota(jnp.int32, (QB, wide), 1) + low
            bias[:, :wide] = jnp.where(see(qpos, kpos, starts_ref, pics), 0.0, MASKED)
            values = jnp.concatenate([v_ref[:ext, :], jnp.ones((ext, HD), jnp.bfloat16)], axis=1)
            lane = lax.broadcasted_iota(jnp.int32, (QB, heads), 1)

            def one_pair(pair, stats):
                at = pl.ds(pl.multiple_of(pair * 2 * HD, 2 * HD), 2 * HD)
                both = q_ref[:, at]
                outs = []
                for side in range(2):
                    scores = contract_cols(both[:, side * HD : (side + 1) * HD], k_ref[:ext, :])
                    if low:
                        scores = jnp.concatenate(
                            [scores[:, :low], scores[:, low:] + bias[:, :wide]], axis=1
                        )
                    else:
                        scores = scores + bias[:, :wide]
                    row_max = jnp.max(scores, axis=1, keepdims=True)
                    terms = jnp.exp(scores - row_max).astype(jnp.bfloat16)
                    summed = dot(terms, values)
                    row_sum = summed[:, HD : HD + 1]
                    outs.append(summed[:, :HD] / row_sum)
                    stats = jnp.where(lane == 2 * pair + side, row_max + jnp.log(row_sum), stats)
                o_ref[:, at] = jnp.concatenate(outs, axis=1).astype(jnp.bfloat16)
                return stats

            lse_ref[...] = lax.fori_loop(
                0, heads // 2, one_pair, jnp.zeros((QB, heads), jnp.float32), unroll=4
            )

    part = dot(o_ref[...], out_ref[...]).astype(jnp.bfloat16)

    @pl.when(pl.program_id(0) == 0)
    def _():
        kept_ref[...] = part

    @pl.when(pl.program_id(0) == 1)
    def _():
        for i, ref in enumerate(sent_refs):
            ref[...] = part[i * ref.shape[0] : (i + 1) * ref.shape[0]]


def attend_forward(q_low, k_low, v_low, w_out, starts, positions):
    rows, width = q_low.shape
    heads, seq, pics = width // HD, k_low.shape[0], starts.shape[0]
    tall = pl.BlockSpec((QB, width), lambda i, *_: (i, 0))
    parts = [(QB, w_out.shape[1])] + [(QB // PARTS, w_out.shape[1])] * PARTS
    keys = pl.BlockSpec((seq, HD), lambda i, *_: (0, 0))
    return pl.pallas_call(
        functools.partial(forward_kernel, heads=heads, pics=pics, seq=seq),
        grid_spec=pltpu.PrefetchScalarGridSpec(
            num_scalar_prefetch=2,
            grid=(rows // QB,),
            in_specs=[tall, keys, keys, whole(w_out)],
            out_specs=[
                tall,
                pl.BlockSpec((QB, heads), lambda i, *_: (i, 0)),
                *(pl.BlockSpec(part, lambda i, *_: (0, 0)) for part in parts),
            ],
            scratch_shapes=[pltpu.VMEM((QB, 2 * QB), jnp.float32)],
        ),
        out_shape=[
            jax.ShapeDtypeStruct((rows, width), jnp.bfloat16),
            jax.ShapeDtypeStruct((rows, heads), jnp.float32),
            *(jax.ShapeDtypeStruct(part, jnp.bfloat16) for part in parts),
        ],
        name="attend_forward",
        **params(),
    )(positions, starts, q_low, k_low, v_low, w_out)


def in_three(value):
    top = value.astype(jnp.bfloat16)
    rest = value - top.astype(jnp.float32)
    middle = rest.astype(jnp.bfloat16)
    last = (rest - middle.astype(jnp.float32)).astype(jnp.bfloat16)
    return [top, middle, last]


def backward_kernel(
    pos_ref, starts_ref, q_ref, out_ref, o_ref, lse_ref, k_ref, v_ref, cos_ref, sin_ref,
    *rest, heads, pics, seq
):
    *d_refs, dq_ref, dk_ref, dv_ref, bias, do_ref = rest
    first = pos_ref[pl.program_id(0)]
    count = key_blocks(starts_ref, pics, first)

    @pl.when(pl.program_id(0) == 0)
    def _():
        dk_ref[...] = jnp.zeros_like(dk_ref)
        dv_ref[...] = jnp.zeros_like(dv_ref)

    do_ref[...] = contract_cols(either(d_refs), out_ref[...]).astype(jnp.bfloat16)

    for blocks in range(1, seq // QB + 1):

        @pl.when(count == blocks)
        def _():
            ext = blocks * QB
            low = max(0, ext - 2 * QB)
            wide = ext - low
            kpos = lax.broadcasted_iota(jnp.int32, (wide, QB), 0) + low
            qpos = lax.broadcasted_iota(jnp.int32, (wide, QB), 1) + first
            bias[:wide, :] = jnp.where(see(qpos, kpos, starts_ref, pics), 0.0, MASKED)
            ones = jnp.ones((ext, HD), jnp.bfloat16)
            keys = jnp.concatenate([k_ref[:ext, :], ones], axis=1)
            values = jnp.concatenate([v_ref[:ext, :], ones], axis=1)
            zeros = jnp.zeros((QB, HD - 3), jnp.bfloat16)
            lane = lax.broadcasted_iota(jnp.int32, (QB, heads), 1)

            def one_pair(pair, _):
                at = pl.ds(pl.multiple_of(pair * 2 * HD, 2 * HD), 2 * HD)
                q_both, d_both, o_both = q_ref[:, at], do_ref[:, at], o_ref[:, at]
                stats = lse_ref[...]
                d_query, d_key, d_val = [], 0.0, 0.0
                for side in range(2):
                    cols = slice(side * HD, (side + 1) * HD)
                    queries, d_out = q_both[:, cols], d_both[:, cols]
                    delta = jnp.sum(
                        d_out.astype(jnp.float32) * o_both[:, cols].astype(jnp.float32),
                        axis=1,
                        keepdims=True,
                    )
                    lse = jnp.sum(
                        jnp.where(lane == 2 * pair + side, stats, 0.0), axis=1, keepdims=True
                    )
                    queries_ext = jnp.concatenate([queries] + in_three(-lse) + [zeros], axis=1)
                    d_out_ext = jnp.concatenate([d_out] + in_three(-delta) + [zeros], axis=1)
                    scores = contract_cols(keys, queries_ext)
                    if low:
                        scores = jnp.concatenate(
                            [scores[:low], scores[low:] + bias[:wide, :]], axis=0
                        )
                    else:
                        scores = scores + bias[:wide, :]
                    probs = jnp.exp(scores)
                    d_probs = contract_cols(values, d_out_ext)
                    d_scores = (probs * d_probs).astype(jnp.bfloat16)
                    d_val += dot(probs.astype(jnp.bfloat16), d_out)
                    d_key += dot(d_scores, queries)
                    d_query.append(contract_rows(d_scores, k_ref[:ext, :]))
                dk_ref[:ext, :] += d_key
                dv_ref[:ext, :] += d_val
                turned = jnp.concatenate(d_query, axis=1) * HD ** (-0.5)
                turned = turned * cos_ref[...] - swap_halves(turned) * sin_ref[...]
                dq_ref[:, at] = turned.astype(jnp.bfloat16)
                return 0

            lax.fori_loop(0, heads // 2, one_pair, 0, unroll=2)


def attend_backward(
    q_low, d_parts, w_out, attn_low, lse, k_low, v_low, cos_tab, sin_tab, starts, positions
):
    rows, width = q_low.shape
    heads, seq, pics = width // HD, k_low.shape[0], starts.shape[0]
    tall = pl.BlockSpec((QB, width), lambda i, *_: (i, 0))
    table = pl.BlockSpec((QB, 2 * HD), lambda i, *_: (i, 0))
    stats = pl.BlockSpec((QB, heads), lambda i, *_: (i, 0))
    keys = whole(k_low)
    return pl.pallas_call(
        functools.partial(backward_kernel, heads=heads, pics=pics, seq=seq),
        grid_spec=pltpu.PrefetchScalarGridSpec(
            num_scalar_prefetch=2,
            grid=(rows // QB,),
            in_specs=[
                tall, whole(w_out), tall, stats, keys, keys, table, table,
                *(whole(part) for part in d_parts),
            ],
            out_specs=[tall, keys, keys],
            scratch_shapes=[
                pltpu.VMEM((2 * QB, QB), jnp.float32),
                pltpu.VMEM((QB, width), jnp.bfloat16),
            ],
        ),
        out_shape=[
            jax.ShapeDtypeStruct((rows, width), jnp.bfloat16),
            jax.ShapeDtypeStruct((seq, HD), jnp.float32),
            jax.ShapeDtypeStruct((seq, HD), jnp.float32),
        ],
        name="attend_backward",
        **params(),
    )(
        positions, starts, q_low, w_out, attn_low, lse, k_low, v_low, cos_tab, sin_tab, *d_parts
    )


def hidden_kernel(*refs):
    *parts, down_ref, out_ref, cots = refs

    @pl.when(pl.program_id(0) == 0)
    def _():
        at = 0
        for ref in parts:
            cots[at : at + ref.shape[0], :] = ref[...]
            at += ref.shape[0]

    out_ref[...] = contract_cols(cots[...], down_ref[...]).astype(jnp.bfloat16)


def hidden_back(cots, w_down):
    rows, width = sum(item.shape[0] for item in cots), cots[0].shape[1]
    units, tile = w_down.shape[0], 256
    return pl.pallas_call(
        hidden_kernel,
        grid=(pl.cdiv(units, tile),),
        in_specs=[
            *(whole(item) for item in cots), pl.BlockSpec((tile, width), lambda j: (j, 0))
        ],
        out_specs=pl.BlockSpec((rows, tile), lambda j: (0, j)),
        out_shape=jax.ShapeDtypeStruct((rows, units), jnp.bfloat16),
        scratch_shapes=[pltpu.VMEM((rows, width), jnp.bfloat16)],
        name="hidden_back",
        **params(),
    )(*cots, w_down)


def feed_kernel(*refs):
    *parts, d_hidden_ref, gate_ref, up_ref, hidden_ref, d_gate_ref, d_up_ref, normed = refs

    @pl.when(pl.program_id(0) == 0)
    def _():
        at = 0
        for ref in parts:
            normed[at : at + ref.shape[0], :] = ref[...]
            at += ref.shape[0]

    gate_val, up_val = dot(normed[...], gate_ref[...]), dot(normed[...], up_ref[...])
    d_hidden = d_hidden_ref[...].astype(jnp.float32)
    gate_sig = jax.nn.sigmoid(gate_val)
    swish = gate_val * gate_sig
    hidden_ref[...] = (swish * up_val).astype(jnp.bfloat16)
    d_gate = d_hidden * up_val * (gate_sig + swish * (1.0 - gate_sig))
    d_gate_ref[...] = d_gate.astype(jnp.bfloat16)
    d_up_ref[...] = (d_hidden * swish).astype(jnp.bfloat16)


def feed_forward(normed, d_hidden, w_gate, w_up):
    rows, width = sum(item.shape[0] for item in normed), normed[0].shape[1]
    units, tile = w_gate.shape[1], 256
    cols = pl.BlockSpec((width, tile), lambda j: (0, j))
    out = pl.BlockSpec((rows, tile), lambda j: (0, j))
    return pl.pallas_call(
        feed_kernel,
        grid=(pl.cdiv(units, tile),),
        in_specs=[*(whole(item) for item in normed), out, cols, cols],
        out_specs=[out] * 3,
        out_shape=[jax.ShapeDtypeStruct((rows, units), jnp.bfloat16)] * 3,
        scratch_shapes=[pltpu.VMEM((rows, width), jnp.bfloat16)],
        name="feed_forward",
        **params(),
    )(*normed, d_hidden, w_gate, w_up)


def share_kernel(*refs, count, transposed):
    outs = refs[2 * count :]
    multiply = contract_cols if transposed else dot
    part = multiply(refs[0][...], refs[count][...])
    for left, right in zip(refs[1:count], refs[count + 1 : 2 * count]):
        part = part + multiply(left[...], right[...])
    rows = outs[0].shape[0]
    for place, ref in enumerate(outs):
        ref[...] = part[place * rows : (place + 1) * rows].astype(jnp.bfloat16)


def row_shares(lefts, rights, transposed, rows):
    blocks = lefts[0].shape[0] // rows
    width, tile = rights[0].shape[0 if transposed else 1], 512

    def right_spec(item):
        if transposed:
            return pl.BlockSpec((tile, item.shape[1]), lambda j: (j, 0))
        return pl.BlockSpec((item.shape[0], tile), lambda j: (0, j))

    return pl.pallas_call(
        functools.partial(share_kernel, count=len(lefts), transposed=transposed),
        grid=(width // tile,),
        in_specs=[*(whole(item) for item in lefts), *(right_spec(item) for item in rights)],
        out_specs=[pl.BlockSpec((rows, tile), lambda j: (0, j))] * blocks,
        out_shape=[jax.ShapeDtypeStruct((rows, width), jnp.bfloat16)] * blocks,
        name="row_shares",
        **params(),
    )(*lefts, *rights)


def outer_kernel(order_ref, *refs, shape, pieces):
    outs, refs = refs[-2 * len(pieces) :], list(refs[: -2 * len(pieces)])
    totals = None
    for lefts, rights in shape:
        rows = jnp.concatenate(
            [
                jnp.concatenate([refs.pop(0)[...] for _ in range(OUTER_BLOCKS)], axis=1)
                for _ in range(lefts)
            ],
            axis=0,
        )
        parts = [contract_rows(rows, refs.pop(0)[...]) for _ in range(rights)]
        totals = parts if totals is None else [a + b for a, b in zip(totals, parts)]
    step = pl.program_id(0)
    half = pl.num_programs(0) // 2
    for place, piece in enumerate(pieces):
        total = jnp.concatenate(totals[piece], axis=1).astype(jnp.bfloat16)

        @pl.when(step < half)
        def _():
            outs[2 * place][...] = total

        @pl.when(step >= half)
        def _():
            outs[2 * place + 1][...] = total


def outer(sections, index, bits, pieces):
    width = sections[0][0][0].shape[1]
    share = width // (1 << len(bits))
    tile = 256
    if share == tile:
        blocks = jnp.stack([index ^ item for item in block_order(bits)]).astype(jnp.int32)
    else:
        blocks = jnp.arange(width // tile, dtype=jnp.int32)
        sections = [
            ([permuted_features(item, index, bits) for item in lefts], rights)
            for lefts, rights in sections
        ]
    count = width // tile // OUTER_BLOCKS
    sizes = [sum(item.shape[1] for item in sections[0][1][piece]) for piece in pieces]
    specs, arrays = [], []
    for lefts, rights in sections:
        for item in lefts:
            for i in range(OUTER_BLOCKS):
                specs.append(
                    pl.BlockSpec(
                        (item.shape[0], tile), lambda j, b, i=i: (0, b[j * OUTER_BLOCKS + i])
                    )
                )
                arrays.append(item)
        specs.extend(whole(item) for item in rights)
        arrays.extend(rights)
    return pl.pallas_call(
        functools.partial(
            outer_kernel,
            shape=[(len(lefts), len(rights)) for lefts, rights in sections],
            pieces=pieces,
        ),
        grid_spec=pltpu.PrefetchScalarGridSpec(
            num_scalar_prefetch=1,
            grid=(count,),
            in_specs=specs,
            out_specs=[
                pl.BlockSpec((tile * OUTER_BLOCKS, size), at)
                for size in sizes
                for at in (
                    lambda j, _: (jnp.minimum(j, count // 2 - 1), 0),
                    lambda j, _: (jnp.maximum(j - count // 2, 0), 0),
                )
            ],
        ),
        out_shape=[
            jax.ShapeDtypeStruct((width // 2, size), jnp.bfloat16) for size in sizes for _ in range(2)
        ],
        name="outer",
        **params(),
    )(blocks, *arrays)


def halves_kernel(kept_a, kept_b, came_a, came_b, sent_ref, kept_ref):
    sent_ref[...] = added(kept_a[...], came_a[...])
    kept_ref[...] = added(kept_b[...], came_b[...])


def add_halves(kept, came):
    half, columns = kept.shape[0] // 2, kept.shape[1]
    block = min(256, half)
    first = pl.BlockSpec((block, columns), lambda i: (i, 0))
    second = pl.BlockSpec((block, columns), lambda i: (i + half // block, 0))
    return pl.pallas_call(
        halves_kernel,
        grid=(half // block,),
        in_specs=[first, second, first, second],
        out_specs=[first, first],
        out_shape=[jax.ShapeDtypeStruct((half, columns), jnp.bfloat16)] * 2,
        name="add_halves",
        **params(),
    )(kept, kept, came, came)


def total_kernel(kept_ref, came_ref, out_ref):
    out_ref[...] = kept_ref[...].astype(jnp.float32) + came_ref[...].astype(jnp.float32)


def add_total(kept, came):
    return pl.pallas_call(
        total_kernel,
        out_shape=jax.ShapeDtypeStruct(kept.shape, jnp.float32),
        name="add_total",
        **params(),
    )(kept, came)


def key_value_kernel(
    at_ref, dkn_ref, dkf_ref, dvn_ref, dvf_ref, cosn_ref, sinn_ref, cosf_ref, sinf_ref, near_ref, far_ref
):
    rows = dkn_ref.shape[0] // 4
    for m in range(4):
        at = pl.ds(pl.multiple_of(at_ref[m], rows), rows)
        mine = slice(m % 2 * rows, (m % 2 + 1) * rows)
        cos_ref, sin_ref = (cosn_ref, sinn_ref) if m < 2 else (cosf_ref, sinf_ref)
        d_key = dkn_ref[at, :] + dkf_ref[at, :]
        d_val = dvn_ref[at, :] + dvf_ref[at, :]
        both = jnp.concatenate([d_key, d_val], axis=1)
        turned = both * cos_ref[mine, :] - swap_halves(both) * sin_ref[mine, :]
        both = jnp.concatenate([turned[:, :HD], d_val], axis=1).astype(jnp.bfloat16)
        target = near_ref if m < 2 else far_ref
        target[mine, :] = both


def key_value_rows(dk_n, dk_f, dv_n, dv_f, tables, block_pos):
    shape = jax.ShapeDtypeStruct((dk_n.shape[0] // 2, 2 * HD), jnp.bfloat16)
    arrays = (dk_n, dk_f, dv_n, dv_f, *tables)
    return pl.pallas_call(
        key_value_kernel,
        grid_spec=pltpu.PrefetchScalarGridSpec(
            num_scalar_prefetch=1,
            grid=(1,),
            in_specs=[whole(item) for item in arrays],
            out_specs=[whole(shape), whole(shape)],
        ),
        out_shape=[shape, shape],
        name="key_value_rows",
        **params(),
    )(block_pos, *arrays)


def swapped(parts, flip):
    pairs = [(i, i ^ flip) for i in range(4)]
    return tuple(lax.ppermute(part, "tensor", pairs) for part in parts)


def swap_core(parts):
    return swapped(parts, 1)


def swap_chip(parts):
    return swapped(parts, 2)


def swap_pair(parts, size):
    return tuple(exchange(part, PAIR, size) for part in parts)


class Order:
    def __init__(self):
        self.last = ()

    def after(self, *values):
        tied = lax.optimization_barrier(values + (self.last,))[: len(values)]
        self.last = tied
        return tied if len(values) > 1 else tied[0]

    def done(self, *values):
        values = lax.optimization_barrier(values + (self.last,))[: len(values)]
        self.last = values
        return values if len(values) > 1 else values[0]


def wait_for(value, *others):
    return lax.optimization_barrier((value,) + others)[0]


def rows_of(one, two):
    return jnp.concatenate([one, two], axis=0)


def block_order(bits):
    order = [0]
    for bit in reversed(bits):
        order = [item ^ bit for item in order] + order
    return order


def permuted_features(value, index, bits):
    order = block_order(bits)
    width = value.shape[1] // len(order)
    return jnp.concatenate(
        [lax.dynamic_slice_in_dim(value, (index ^ item) * width, width, 1) for item in order], axis=1
    )


def rows_and_cols(one, two):
    return jnp.concatenate([one, two], axis=1)


def exchange(value, bit, size):
    return lax.ppermute(value, "dp", [(i, i ^ bit) for i in range(size)])


class Reduction:
    def __init__(self, order, sent, kept, bits, size, assemble=None):
        self.order, self.sent, self.kept, self.assemble = order, sent, kept, assemble
        self.bits, self.size, self.step = bits, size, 0
        self.total = None

    def send(self, *others):
        sent = wait_for(self.sent, *others) if others else self.sent
        self.came = exchange(sent, self.bits[self.step], self.size)
        return self

    def receive(self):
        self.came = self.order.after(self.came)
        return self

    def add(self):
        kept, came = self.kept, self.came
        self.step += 1
        if self.step == len(self.bits):
            self.total = self.order.done((self.assemble or add_total)(kept, came))
        else:
            self.sent, self.kept = self.order.done(*add_halves(kept, came))
        return self

    def advance(self):
        self.receive().add()
        if self.total is None:
            self.send()

    def finish(self):
        while self.total is None:
            self.advance()
        return self.total


def added(one, two):
    return (one.astype(jnp.float32) + two.astype(jnp.float32)).astype(jnp.bfloat16)


def per_device(
    dp_size,
    layer_input,
    cotangent,
    starts,
    pieces,
    norm_attn,
    w_query,
    w_key,
    w_value,
    w_out,
    norm_mlp,
    w_gate,
    w_up,
    w_down,
):
    rows = layer_input.shape[0]
    width = layer_input.shape[1]
    place = lax.axis_index("tensor")
    index = lax.axis_index("dp")
    bits = [1 << i for i in range(dp_size.bit_length() - 1)]
    late_bits = bits[1:] + bits[:1]
    begins = starts[0]

    block_pos = jnp.stack([(place ^ m) * rows for m in range(4)]).astype(jnp.int32)
    near_pos, far_pos = block_pos[:2], block_pos[2:]
    row_pos = (block_pos[:, None] + jnp.arange(rows, dtype=jnp.int32)[None, :]).reshape(-1)
    (cos_n, sin_n), (cos_f, sin_f) = (
        rope_tables(half) for half in (row_pos[: 2 * rows], row_pos[2 * rows :])
    )
    w_kv = jnp.concatenate([w_key, w_value], axis=1)

    def in_sequence(value):
        return jnp.concatenate(
            [lax.dynamic_slice_in_dim(value, (place ^ b) * rows, rows, 0) for b in range(4)], axis=0
        )

    def in_two(value):
        return tuple(jnp.split(value, PARTS, axis=0))

    order = Order()
    near, far = slice(0, 2 * rows), slice(2 * rows, 4 * rows)

    def chip_sum(kept, came):
        came = order.after(came)
        return order.done(*by_rows(lambda a, b: (a + b,), (kept, came), (), ((jnp.bfloat16,),)))

    x_own, cot_own = in_two(layer_input), in_two(cotangent)
    x_chip, x_core = swap_chip(x_own), swap_core(x_own)

    side = index // PAIR % 2
    units, queries = w_gate.shape[1], w_query.shape[1]
    window = -(-units // 256) * 128
    overlap = 2 * window - units
    mine = (jnp.arange(window) >= overlap) | (side == 0)
    gate_half = lax.dynamic_slice_in_dim(w_gate, side * (units - window), window, 1)
    up_half = lax.dynamic_slice_in_dim(w_up, side * (units - window), window, 1)
    up_half = jnp.where(mine[None, :], up_half, 0).astype(jnp.bfloat16)
    down_half = lax.dynamic_slice_in_dim(w_down, side * (units - window), window, 0)
    down_half = jnp.where(mine[:, None], down_half, 0).astype(jnp.bfloat16)
    gate_half, up_half, down_half, w_kv, cos_n, sin_n, cos_f, sin_f = order.done(
        gate_half, up_half, down_half, w_kv, cos_n, sin_n, cos_f, sin_f
    )
    normed_n, q_n, k_n, v_n = order.done(
        *project((*x_own, *x_core), norm_attn, w_query, w_kv, cos_n, sin_n)
    )
    x_chip = order.after(x_chip)
    cot_own_ = wait_for(cot_own, x_chip)
    cot_chip, cot_core, cot_pair = (
        swap_chip(cot_own_), swap_core(cot_own_), swap_pair(cot_own_, dp_size)
    )
    normed_f, q_f, k_f, v_f = order.done(
        *project((*x_chip, *swap_core(x_chip)), norm_attn, w_query, w_kv, cos_f, sin_f)
    )
    k_low = in_sequence(rows_of(k_n, k_f))
    v_low = in_sequence(rows_of(v_n, v_f))
    attn_f, lse_f, kept, *sent = order.done(
        *attend_forward(q_f, k_low, v_low, w_out, begins, far_pos)
    )
    came = swap_core(sent)
    cot_chip, cot_pair = order.after(cot_chip, cot_pair)
    cot_diag, cot_other, cot_pcore = (
        swap_pair(cot_chip, dp_size), swap_core(cot_chip), swap_core(cot_pair)
    )
    attn_came = swap_chip(chip_sum(kept, came))
    cot_core, cot_other, cot_pcore, q_n = order.after(cot_core, cot_other, cot_pcore, q_n)
    attn_n, lse_n, kept, *sent = order.done(
        *attend_forward(q_n, k_low, v_low, w_out, begins, near_pos)
    )
    sum_came = swap_core(sent)

    def cot_back(*cots):
        return order.done(hidden_back(order.after(cots), down_half))

    near_back_hidden = cot_back(*cot_own, *cot_core)
    cot_diag = order.after(cot_diag)
    cot_dcore = swap_core(cot_diag)
    attn_came = order.after(attn_came)
    sum_came, cot_dcore = order.after(sum_came, cot_dcore)

    def norm_mid(x, kept, core, chip, gain):
        resid = x + (kept + core + chip)
        return resid, resid * rms_inverse(resid) * gain

    resid_mid, mlp_own = order.done(
        *by_rows(
            norm_mid, (x_own, kept, sum_came, attn_came), (norm_mlp,), (jnp.float32, (jnp.bfloat16,))
        )
    )
    mlp_core, mlp_chip, mlp_pair = swap_core(mlp_own), swap_chip(mlp_own), swap_pair(mlp_own, dp_size)
    mlp_core = order.after(mlp_core)

    def feed(normed, d_hidden):
        return order.done(*feed_forward(normed, d_hidden, gate_half, up_half))

    near_hidden = feed((*mlp_own, *mlp_core), near_back_hidden)
    side_back_hidden = cot_back(*cot_chip, *cot_other, *cot_pair, *cot_pcore)
    diag_back_hidden = cot_back(*cot_diag, *cot_dcore)
    mlp_chip, mlp_pair = order.after(mlp_chip, mlp_pair)
    half = rows // 2
    mlp_diag = (
        *swap_chip((mlp_pair[0][:half],)), *swap_pair((mlp_chip[0][half:],), dp_size)
    )
    mlp_other, mlp_pcore = order.after(swap_core(mlp_chip), swap_core(mlp_pair))
    side_hidden = feed((*mlp_chip, *mlp_other, *mlp_pair, *mlp_pcore), side_back_hidden)
    mlp_diag = order.after(mlp_diag)
    mlp_dcore = order.after(swap_core(mlp_diag))
    diag_hidden = feed((*mlp_diag, *mlp_dcore), diag_back_hidden)
    hiddens = (near_hidden, side_hidden, diag_hidden)

    def in_window(kept, came):
        first = jnp.where(side == 0, kept, came)
        second = jnp.where(side == 0, came, kept)
        return jnp.concatenate([first, second[:, overlap:]], axis=1).astype(jnp.float32)

    pair_bits = [bit for bit in bits if bit != PAIR] + [PAIR]
    always = begins[0] >= 0

    def fence(step):
        def inside():
            outer_last, order.last = order.last, ()
            try:
                return step()
            finally:
                order.last = outer_last

        shapes = jax.eval_shape(inside)
        taken = order.after(always)
        results = lax.cond(
            taken,
            inside,
            lambda: jax.tree.map(lambda item: jnp.zeros(item.shape, item.dtype), shapes),
        )
        leaves, tree = jax.tree.flatten(results)
        return jax.tree.unflatten(tree, order.done(tuple(leaves)))

    def gradient(sections, order_bits, pieces=(slice(None),)):
        lefts, rights = order.after([item[0] for item in sections], [item[1] for item in sections])
        return order.done(*outer(list(zip(lefts, rights)), index, order_bits, pieces))

    cots = (
        (*cot_own, *cot_core),
        (*cot_chip, *cot_other, *cot_pair, *cot_pcore),
        (*cot_diag, *cot_dcore),
    )
    mlps = (
        (*mlp_own, *mlp_core),
        (*mlp_chip, *mlp_other, *mlp_pair, *mlp_pcore),
        (*mlp_diag, *mlp_dcore),
    )

    def mlp_gradients(lefts, which):
        sections = [(left, [right[i] for i in which]) for left, right in zip(lefts, hiddens)]
        return gradient(sections, pair_bits, [slice(i, i + 1) for i in range(len(which))])

    def reduction(sent_kept, order_bits, assemble=None):
        return Reduction(order, *sent_kept, order_bits, dp_size, assemble)

    def shares(lefts, rights, transposed=True):
        parts = order.done(*row_shares(order.after(lefts), rights, transposed, rows))
        return [(parts[i], swap_core((parts[i + 1],))) for i in range(0, len(parts), 2)]

    def total(*items):
        return order.done(*by_rows(lambda *values: (sum(values),), items, (), ((jnp.bfloat16,),)))

    class GroupSum:
        def __init__(self, which, rights, transposed):
            self.rest = rights, transposed
            self.near, self.sides, self.diag = (tuple(item[i] for i in which) for item in hiddens)

        def diag_shares(self):
            return shares(self.diag, *self.rest)[0]

        def side_shares(self):
            return shares(self.sides, *self.rest)

        def own_shares(self):
            return shares(self.near, *self.rest)[0]

    d_norm = GroupSum((1, 2), (gate_half, up_half), True)
    block_sum = GroupSum((0,), (down_half,), False)

    down = reduction(mlp_gradients(cots, (0,)), pair_bits, in_window)
    down.send()

    @fence
    def diag_and_gradients():
        kept, came = d_norm.diag_shares()
        made = mlp_gradients(mlps, (1, 2))
        return chip_sum(kept, came), made

    diag, made = diag_and_gradients
    to_pair = swap_pair(diag, dp_size)
    gate, up = (reduction(item, pair_bits, in_window) for item in (made[:2], made[2:]))

    @fence
    def other_shares():
        chip, pair = d_norm.side_shares()
        own = d_norm.own_shares()
        return order.after(chip), order.after(pair), order.after(own)

    chip, pair, own = other_shares
    came_p = swap_pair(total(pair[0], *pair[1]), dp_size)
    to_pair = order.after(to_pair)
    came_c = swap_chip(total(chip[0], *chip[1], to_pair))
    down.receive()
    gate.send(down.came)
    down.add()
    down.send()

    @fence
    def block_shares():
        def parts(lefts):
            return order.done(*row_shares(order.after(lefts), *block_sum.rest, rows))

        kept, sent = parts(block_sum.diag)
        came = swap_core((sent,))
        kept_c, sent_c, kept_p, sent_p = parts(block_sum.sides)
        diag = chip_sum(kept, came)
        came_c = swap_core((order.after(sent_c),))
        kept, sent = parts(block_sum.near)
        came_c = order.after(came_c)
        came_p = order.after(swap_core((order.after(sent_p),)))
        came = order.after(swap_core((order.after(sent),)))
        return diag, (kept_c, came_c), (kept_p, came_p), (kept, came)

    block_diag, block_chip, block_pair, block_own = block_shares
    came_c, came_p = order.after(came_c, came_p)
    to_pair = swap_pair(block_diag, dp_size)

    def back_mid(kept, core, chip, pair, resid, cot, gain):
        d_mid = cot + norm_back(kept + core + chip + pair, resid, rms_inverse(resid), gain)
        return d_mid, d_mid

    d_mid, d_own = order.done(
        *by_rows(
            back_mid,
            (own[0], own[1], came_c, came_p, resid_mid, cot_own),
            (norm_mlp,),
            (jnp.float32, (jnp.bfloat16,)),
        )
    )
    d_chip = swap_chip(d_own)

    gate.receive()
    up.send(gate.came)
    gate.add()

    @fence
    def near_back():
        d_core = order.after(swap_core(d_own))
        return d_core, order.done(
            *attend_backward(
                q_n, (*d_own, *d_core), w_out, attn_n, lse_n, k_low, v_low, cos_n,
                sin_n, begins, near_pos,
            )
        )

    d_core, (dq_n, dk_n, dv_n) = near_back
    d_chip = order.after(d_chip)
    @fence
    def out_gradient():
        d_other = order.after(swap_core(d_chip))
        sections = [((*d_own, *d_core), (attn_n,)), ((*d_chip, *d_other), (attn_f,))]
        return d_other, gradient(sections, bits)

    d_other, wout = out_gradient
    wout = reduction(wout, bits)
    down.receive()
    gate.send(down.came)
    down.add().send()
    up.receive()
    wout.send(up.came)
    up.add()
    to_pair = order.after(to_pair)
    block_c = total(block_chip[0], *block_chip[1], to_pair)
    block_p = total(block_pair[0], *block_pair[1])

    @fence
    def far_back():
        return order.done(
            *attend_backward(
                q_f, (*d_chip, *d_other), w_out, attn_f, lse_f, k_low, v_low, cos_f,
                sin_f, begins, far_pos,
            )
        )

    dq_f, dk_f, dv_f = far_back

    @fence
    def query_gradient():
        dkv_n, dkv_f = order.done(
            *key_value_rows(dk_n, dk_f, dv_n, dv_f, (cos_n, sin_n, cos_f, sin_f), block_pos)
        )
        sections = [((normed_n,), (dq_n, dkv_n)), ((normed_f,), (dq_f, dkv_f))]
        return dkv_n, dkv_f, gradient(sections, bits)

    dkv_n, dkv_f, qkv = query_gradient
    qkv = reduction(qkv, bits)
    qkv.send()
    wout.receive()
    wout.add().send()
    down.receive().add()
    gate.receive()
    up.send(gate.came)
    gate.add().send()
    in_sum = fence(lambda: chip_sum(*shares((dq_f, dkv_f), (w_query, w_kv))[0]))
    gate.receive().add()
    d_in_came = swap_chip(in_sum)
    own = fence(lambda: order.after(shares((dq_n, dkv_n), (w_query, w_kv))[0]))
    qkv.receive()
    qkv.add().send()
    wout.receive()
    up.receive()
    up.add().send()
    wout.add().send()
    d_in_came = order.after(d_in_came)

    def back_in(kept, core, chip, resid, d_mid, gain):
        return (d_mid + norm_back(kept + core + chip, resid, rms_inverse(resid), gain),)

    (x_grad,) = by_rows(
        back_in, (own[0], own[1], d_in_came, x_own, d_mid), (norm_attn,), (jnp.float32,)
    )
    x_grad = order.done(x_grad)
    qkv.receive()
    block_p = swap_pair(wait_for(block_p, qkv.came), dp_size)
    block_c = swap_chip(wait_for(block_c, qkv.came))
    qkv.add().send()
    up.receive().add()
    wout.receive().add()
    block_c, block_p = order.after(block_c, block_p)
    qkv.receive().add()
    (block_out,) = by_rows(
        lambda *items: (sum(items),),
        (resid_mid, block_own[0], block_own[1], block_c, block_p),
        (),
        (jnp.bfloat16,),
    )
    block_out = order.done(block_out)
    for item in (down, gate, up, wout, qkv):
        item.finish()
    grad_down, grad_gate, grad_up = down.total.T, gate.total, up.total
    grad_out, grad_qkv = wout.total.T, qkv.total
    queries = w_query.shape[1]
    grad_query = grad_qkv[:, :queries]
    grad_key = grad_qkv[:, queries : queries + HD]
    grad_value = grad_qkv[:, queries + HD :]

    share = width // dp_size

    def own_features(value):
        return lax.dynamic_slice_in_dim(value, index * share, share, 0).astype(jnp.float32)

    gain_attn = (
        jnp.sum(own_features(w_query) * grad_query, axis=1)
        + jnp.sum(own_features(w_kv) * grad_qkv[:, queries:], axis=1)
    ) / own_features(norm_attn)
    gain_mlp = jnp.sum(
        own_features(w_gate) * grad_gate + own_features(w_up) * grad_up, axis=1
    ) / own_features(norm_mlp)
    gains = jnp.stack([gain_attn, gain_mlp]).reshape(2, 4, share // 4)
    gains = jnp.stack([lax.dynamic_index_in_dim(gains, place ^ m, 1, False) for m in range(4)])
    gains = gains[:2] + lax.ppermute(gains[2:], "tensor", [(i, i ^ 2) for i in range(4)])
    gains = gains[0] + lax.ppermute(gains[1], "tensor", [(i, i ^ 1) for i in range(4)])

    return (
        block_out,
        x_grad,
        gains[0],
        grad_query,
        grad_key,
        grad_value,
        grad_out,
        gains[1],
        grad_gate,
        grad_up,
        grad_down,
    )


def solution(mesh):
    in_specs = (
        P(("dp", "tensor"), None),
        P(("dp", "tensor"), None),
        P("dp", None),
        P("dp"),
        P(),
        P(None, "tensor"),
        P(None, "tensor"),
        P(None, "tensor"),
        P("tensor", None),
        P(),
        P(None, "tensor"),
        P(None, "tensor"),
        P("tensor", None),
    )
    out_specs = (
        P(("dp", "tensor"), None),
        P(("dp", "tensor"), None),
        P(("dp", "tensor")),
        P("dp", "tensor"),
        P("dp", "tensor"),
        P("dp", "tensor"),
        P("tensor", "dp"),
        P(("dp", "tensor")),
        P("dp", "tensor"),
        P("dp", "tensor"),
        P("tensor", "dp"),
    )
    return jax.shard_map(
        functools.partial(per_device, mesh.shape["dp"]),
        mesh=mesh,
        in_specs=in_specs,
        out_specs=out_specs,
        check_vma=False,
    )
```

```python
import functools

import jax
import jax.numpy as jnp
from jax import lax
from jax.experimental import pallas as pl
from jax.experimental.pallas import tpu as pltpu
from jax.sharding import PartitionSpec as P

HD = 64
SEQ = 1024
PIECE = 256
QB = 256


EPSILON = 1e-05
ROPE_BASE = 10000.0
MASKED = -1e30
VMEM_LIMIT = 48 * 2**20
PARTS = 1
OUTER_BLOCKS = 2
PAIR = 2
NT = (((1,), (1,)), ((), ()))
TN = (((0,), (0,)), ((), ()))


def dot(left, right):
    return jnp.dot(left, right, preferred_element_type=jnp.float32)


def contract_rows(left, right):
    return lax.dot_general(left, right, TN, preferred_element_type=jnp.float32)


def contract_cols(left, right):
    return lax.dot_general(left, right, NT, preferred_element_type=jnp.float32)


def rms_inverse(resid):
    return lax.rsqrt(jnp.mean(resid * resid, axis=-1, keepdims=True) + EPSILON)


def norm_back(d_norm, resid, inverse, gain):
    scaled = d_norm * gain
    return inverse * scaled - resid * (inverse * inverse * inverse) * jnp.mean(
        scaled * resid, axis=-1, keepdims=True
    )


def rope_tables(positions):
    half_dim = HD // 2
    inverse = jnp.power(ROPE_BASE, -(jnp.arange(half_dim).astype(jnp.float32) * 2.0) / HD)
    angles = positions.astype(jnp.float32)[:, None] * inverse[None, :]
    cos, sin = jnp.cos(angles), jnp.sin(angles)
    return jnp.concatenate([cos] * 4, axis=1), jnp.concatenate([-sin, sin] * 2, axis=1)


def swap_halves(pair):
    lane = lax.broadcasted_iota(jnp.int32, pair.shape, 1)
    up = pltpu.roll(pair, 2 * HD - HD // 2, 1)
    down = pltpu.roll(pair, HD // 2, 1)
    return jnp.where(lane % HD < HD // 2, up, down)


def rotate_rows(grad, cos_tab, sin_tab):
    half = HD // 2
    swapped = jnp.concatenate([grad[:, half:], grad[:, :half]], axis=1)
    return grad * cos_tab[:, :HD] - swapped * sin_tab[:, :HD]


def either(near_refs):
    half = len(near_refs) // 2
    own, core = (
        jnp.concatenate([ref[...] for ref in refs], axis=0)
        for refs in (near_refs[:half], near_refs[half:])
    )
    return jnp.where(pl.program_id(0) == 0, own, core)


def project_kernel(*refs):
    x_refs = refs[:-9]
    gain_ref, wq_ref, wkv_ref, cos_ref, sin_ref, n_ref, q_ref, k_ref, v_ref = refs[-9:]
    resid = either(x_refs).astype(jnp.float32)
    normed = (resid * rms_inverse(resid) * gain_ref[...]).astype(jnp.bfloat16)
    n_ref[...] = normed
    cos, sin = cos_ref[...], sin_ref[...]
    query = dot(normed, wq_ref[...])
    for first in range(0, query.shape[1], 2 * HD):
        pair = query[:, first : first + 2 * HD]
        turned = (pair * cos + swap_halves(pair) * sin) * HD ** (-0.5)
        q_ref[:, first : first + 2 * HD] = turned.astype(jnp.bfloat16)
    key_value = dot(normed, wkv_ref[...])
    turned = key_value * cos + swap_halves(key_value) * sin
    k_ref[...] = turned[:, :HD].astype(jnp.bfloat16)
    v_ref[...] = key_value[:, HD:].astype(jnp.bfloat16)


def whole(array):
    return pl.BlockSpec(array.shape, lambda *_: (0,) * len(array.shape))


def params():
    return {
        "compiler_params": pltpu.CompilerParams(vmem_limit_bytes=VMEM_LIMIT),
        "cost_estimate": pl.CostEstimate(flops=1, bytes_accessed=1, transcendentals=0),
    }


def project(parts, gain, w_query, w_kv, cos_tab, sin_tab):
    rows, width = sum(part.shape[0] for part in parts) // 2, parts[0].shape[1]
    queries = w_query.shape[1]

    def tall(cols):
        return pl.BlockSpec((rows, cols), lambda i: (i, 0))

    gain = gain[None, :]
    return pl.pallas_call(
        project_kernel,
        grid=(2,),
        in_specs=[
            *(whole(item) for item in (*parts, gain, w_query, w_kv)), tall(2 * HD), tall(2 * HD)
        ],
        out_specs=[tall(width), tall(queries), tall(HD), tall(HD)],
        out_shape=[
            jax.ShapeDtypeStruct((2 * rows, width), jnp.bfloat16),
            jax.ShapeDtypeStruct((2 * rows, queries), jnp.bfloat16),
            jax.ShapeDtypeStruct((2 * rows, HD), jnp.bfloat16),
            jax.ShapeDtypeStruct((2 * rows, HD), jnp.bfloat16),
        ],
        name="project",
        **params(),
    )(*parts, gain, w_query, w_kv, cos_tab, sin_tab)


def by_rows(function, ins, consts, outs):
    flat, counts = [], []
    for item in ins:
        item = item if isinstance(item, tuple) else (item,)
        counts.append([len(flat) + sum(one is not None for one in item[:i]) if part is not None else None
                       for i, part in enumerate(item)])
        flat.extend(part for part in item if part is not None)
    rows, width = sum(flat[at].shape[0] for at in counts[0]), flat[0].shape[1]
    out_counts = [PARTS if isinstance(item, tuple) else 1 for item in outs]
    dtypes = [item[0] if isinstance(item, tuple) else item for item in outs]
    starts = [sum(out_counts[:i]) for i in range(len(outs))]
    out_places = [range(first, first + count) for first, count in zip(starts, out_counts)]
    step = 32

    def kernel(*refs):
        given = [ref[...] for ref in refs[len(flat) : len(flat) + len(consts)]]

        def views(part_refs, places, part):
            found = []
            for place in places:
                each = PARTS // len(place)
                at = place[part // each]
                ref = None if at is None else part_refs[at]
                found.append((ref, part % each * (rows // PARTS)))
            return found

        for part in range(PARTS):
            sources = views(refs, counts, part)
            targets = views(refs[len(flat) + len(consts) :], out_places, part)

            def chunk(i, _):
                def at(base):
                    return pl.ds(pl.multiple_of(base + i * step, step), step)

                values = [
                    0.0 if ref is None else ref[at(base), :].astype(jnp.float32)
                    for ref, base in sources
                ]
                for (ref, base), value in zip(targets, function(*values, *given)):
                    ref[at(base), :] = value.astype(ref.dtype)
                return 0

            lax.fori_loop(0, rows // PARTS // step, chunk, 0)

    consts = [item[None, :] for item in consts]
    shapes = []
    for count, dtype in zip(out_counts, dtypes):
        shapes.extend([jax.ShapeDtypeStruct((rows // count, width), dtype)] * count)
    results = pl.pallas_call(kernel, out_shape=shapes, name="by_rows", **params())(*flat, *consts)
    grouped, at = [], 0
    for count, item in zip(out_counts, outs):
        grouped.append(tuple(results[at : at + count]) if isinstance(item, tuple) else results[at])
        at += count
    return grouped


def see(qpos, kpos, starts_ref, pics):
    mask = kpos <= qpos
    for pic in range(pics):
        begin = starts_ref[pic]
        mask = mask | (
            (qpos >= begin) & (qpos < begin + PIECE) & (kpos >= begin) & (kpos < begin + PIECE)
        )
    return mask


def key_blocks(starts_ref, pics, first):
    edge = first + QB
    crossed = jnp.bool_(False)
    for pic in range(pics):
        begin = starts_ref[pic]
        crossed = crossed | ((begin < edge) & (begin + PIECE > edge))
    return edge // QB + jnp.where(crossed, 1, 0)


def forward_kernel(
    pos_ref, starts_ref, q_ref, k_ref, v_ref, out_ref, o_ref, lse_ref, kept_ref, *rest, heads, pics, seq
):
    *sent_refs, bias = rest
    first = pos_ref[pl.program_id(0)]
    count = key_blocks(starts_ref, pics, first)
    for blocks in range(1, seq // QB + 1):

        @pl.when(count == blocks)
        def _():
            ext = blocks * QB
            low = max(0, ext - 2 * QB)
            wide = ext - low
            qpos = lax.broadcasted_iota(jnp.int32, (QB, wide), 0) + first
            kpos = lax.broadcasted_iota(jnp.int32, (QB, wide), 1) + low
            bias[:, :wide] = jnp.where(see(qpos, kpos, starts_ref, pics), 0.0, MASKED)
            values = jnp.concatenate([v_ref[:ext, :], jnp.ones((ext, HD), jnp.bfloat16)], axis=1)
            lane = lax.broadcasted_iota(jnp.int32, (QB, heads), 1)

            def one_pair(pair, stats):
                at = pl.ds(pl.multiple_of(pair * 2 * HD, 2 * HD), 2 * HD)
                both = q_ref[:, at]
                outs = []
                for side in range(2):
                    scores = contract_cols(both[:, side * HD : (side + 1) * HD], k_ref[:ext, :])
                    if low:
                        scores = jnp.concatenate(
                            [scores[:, :low], scores[:, low:] + bias[:, :wide]], axis=1
                        )
                    else:
                        scores = scores + bias[:, :wide]
                    row_max = jnp.max(scores, axis=1, keepdims=True)
                    terms = jnp.exp(scores - row_max).astype(jnp.bfloat16)
                    summed = dot(terms, values)
                    row_sum = summed[:, HD : HD + 1]
                    outs.append(summed[:, :HD] / row_sum)
                    stats = jnp.where(lane == 2 * pair + side, row_max + jnp.log(row_sum), stats)
                o_ref[:, at] = jnp.concatenate(outs, axis=1).astype(jnp.bfloat16)
                return stats

            lse_ref[...] = lax.fori_loop(
                0, heads // 2, one_pair, jnp.zeros((QB, heads), jnp.float32), unroll=4
            )

    part = dot(o_ref[...], out_ref[...]).astype(jnp.bfloat16)

    @pl.when(pl.program_id(0) == 0)
    def _():
        kept_ref[...] = part

    @pl.when(pl.program_id(0) == 1)
    def _():
        for i, ref in enumerate(sent_refs):
            ref[...] = part[i * ref.shape[0] : (i + 1) * ref.shape[0]]


def attend_forward(q_low, k_low, v_low, w_out, starts, positions):
    rows, width = q_low.shape
    heads, seq, pics = width // HD, k_low.shape[0], starts.shape[0]
    tall = pl.BlockSpec((QB, width), lambda i, *_: (i, 0))
    parts = [(QB, w_out.shape[1])] + [(QB // PARTS, w_out.shape[1])] * PARTS
    keys = pl.BlockSpec((seq, HD), lambda i, *_: (0, 0))
    return pl.pallas_call(
        functools.partial(forward_kernel, heads=heads, pics=pics, seq=seq),
        grid_spec=pltpu.PrefetchScalarGridSpec(
            num_scalar_prefetch=2,
            grid=(rows // QB,),
            in_specs=[tall, keys, keys, whole(w_out)],
            out_specs=[
                tall,
                pl.BlockSpec((QB, heads), lambda i, *_: (i, 0)),
                *(pl.BlockSpec(part, lambda i, *_: (0, 0)) for part in parts),
            ],
            scratch_shapes=[pltpu.VMEM((QB, 2 * QB), jnp.float32)],
        ),
        out_shape=[
            jax.ShapeDtypeStruct((rows, width), jnp.bfloat16),
            jax.ShapeDtypeStruct((rows, heads), jnp.float32),
            *(jax.ShapeDtypeStruct(part, jnp.bfloat16) for part in parts),
        ],
        name="attend_forward",
        **params(),
    )(positions, starts, q_low, k_low, v_low, w_out)


def in_three(value):
    top = value.astype(jnp.bfloat16)
    rest = value - top.astype(jnp.float32)
    middle = rest.astype(jnp.bfloat16)
    last = (rest - middle.astype(jnp.float32)).astype(jnp.bfloat16)
    return [top, middle, last]


def backward_kernel(
    pos_ref, starts_ref, q_ref, out_ref, o_ref, lse_ref, k_ref, v_ref, cos_ref, sin_ref,
    *rest, heads, pics, seq
):
    *d_refs, dq_ref, dk_ref, dv_ref, bias, do_ref = rest
    first = pos_ref[pl.program_id(0)]
    count = key_blocks(starts_ref, pics, first)

    @pl.when(pl.program_id(0) == 0)
    def _():
        dk_ref[...] = jnp.zeros_like(dk_ref)
        dv_ref[...] = jnp.zeros_like(dv_ref)

    do_ref[...] = contract_cols(either(d_refs), out_ref[...]).astype(jnp.bfloat16)

    for blocks in range(1, seq // QB + 1):

        @pl.when(count == blocks)
        def _():
            ext = blocks * QB
            low = max(0, ext - 2 * QB)
            wide = ext - low
            kpos = lax.broadcasted_iota(jnp.int32, (wide, QB), 0) + low
            qpos = lax.broadcasted_iota(jnp.int32, (wide, QB), 1) + first
            bias[:wide, :] = jnp.where(see(qpos, kpos, starts_ref, pics), 0.0, MASKED)
            ones = jnp.ones((ext, HD), jnp.bfloat16)
            keys = jnp.concatenate([k_ref[:ext, :], ones], axis=1)
            values = jnp.concatenate([v_ref[:ext, :], ones], axis=1)
            zeros = jnp.zeros((QB, HD - 3), jnp.bfloat16)
            lane = lax.broadcasted_iota(jnp.int32, (QB, heads), 1)

            def one_pair(pair, _):
                at = pl.ds(pl.multiple_of(pair * 2 * HD, 2 * HD), 2 * HD)
                q_both, d_both, o_both = q_ref[:, at], do_ref[:, at], o_ref[:, at]
                stats = lse_ref[...]
                d_query, d_key, d_val = [], 0.0, 0.0
                for side in range(2):
                    cols = slice(side * HD, (side + 1) * HD)
                    queries, d_out = q_both[:, cols], d_both[:, cols]
                    delta = jnp.sum(
                        d_out.astype(jnp.float32) * o_both[:, cols].astype(jnp.float32),
                        axis=1,
                        keepdims=True,
                    )
                    lse = jnp.sum(
                        jnp.where(lane == 2 * pair + side, stats, 0.0), axis=1, keepdims=True
                    )
                    queries_ext = jnp.concatenate([queries] + in_three(-lse) + [zeros], axis=1)
                    d_out_ext = jnp.concatenate([d_out] + in_three(-delta) + [zeros], axis=1)
                    scores = contract_cols(keys, queries_ext)
                    if low:
                        scores = jnp.concatenate(
                            [scores[:low], scores[low:] + bias[:wide, :]], axis=0
                        )
                    else:
                        scores = scores + bias[:wide, :]
                    probs = jnp.exp(scores)
                    d_probs = contract_cols(values, d_out_ext)
                    d_scores = (probs * d_probs).astype(jnp.bfloat16)
                    d_val += dot(probs.astype(jnp.bfloat16), d_out)
                    d_key += dot(d_scores, queries)
                    d_query.append(contract_rows(d_scores, k_ref[:ext, :]))
                dk_ref[:ext, :] += d_key
                dv_ref[:ext, :] += d_val
                turned = jnp.concatenate(d_query, axis=1) * HD ** (-0.5)
                turned = turned * cos_ref[...] - swap_halves(turned) * sin_ref[...]
                dq_ref[:, at] = turned.astype(jnp.bfloat16)
                return 0

            lax.fori_loop(0, heads // 2, one_pair, 0, unroll=2)


def attend_backward(
    q_low, d_parts, w_out, attn_low, lse, k_low, v_low, cos_tab, sin_tab, starts, positions
):
    rows, width = q_low.shape
    heads, seq, pics = width // HD, k_low.shape[0], starts.shape[0]
    tall = pl.BlockSpec((QB, width), lambda i, *_: (i, 0))
    table = pl.BlockSpec((QB, 2 * HD), lambda i, *_: (i, 0))
    stats = pl.BlockSpec((QB, heads), lambda i, *_: (i, 0))
    keys = whole(k_low)
    return pl.pallas_call(
        functools.partial(backward_kernel, heads=heads, pics=pics, seq=seq),
        grid_spec=pltpu.PrefetchScalarGridSpec(
            num_scalar_prefetch=2,
            grid=(rows // QB,),
            in_specs=[
                tall, whole(w_out), tall, stats, keys, keys, table, table,
                *(whole(part) for part in d_parts),
            ],
            out_specs=[tall, keys, keys],
            scratch_shapes=[
                pltpu.VMEM((2 * QB, QB), jnp.float32),
                pltpu.VMEM((QB, width), jnp.bfloat16),
            ],
        ),
        out_shape=[
            jax.ShapeDtypeStruct((rows, width), jnp.bfloat16),
            jax.ShapeDtypeStruct((seq, HD), jnp.float32),
            jax.ShapeDtypeStruct((seq, HD), jnp.float32),
        ],
        name="attend_backward",
        **params(),
    )(
        positions, starts, q_low, w_out, attn_low, lse, k_low, v_low, cos_tab, sin_tab, *d_parts
    )


def hidden_kernel(*refs):
    *parts, down_ref, out_ref, cots = refs

    @pl.when(pl.program_id(0) == 0)
    def _():
        at = 0
        for ref in parts:
            cots[at : at + ref.shape[0], :] = ref[...]
            at += ref.shape[0]

    out_ref[...] = contract_cols(cots[...], down_ref[...]).astype(jnp.bfloat16)


def hidden_back(cots, w_down):
    rows, width = sum(item.shape[0] for item in cots), cots[0].shape[1]
    units, tile = w_down.shape[0], 256
    return pl.pallas_call(
        hidden_kernel,
        grid=(pl.cdiv(units, tile),),
        in_specs=[
            *(whole(item) for item in cots), pl.BlockSpec((tile, width), lambda j: (j, 0))
        ],
        out_specs=pl.BlockSpec((rows, tile), lambda j: (0, j)),
        out_shape=jax.ShapeDtypeStruct((rows, units), jnp.bfloat16),
        scratch_shapes=[pltpu.VMEM((rows, width), jnp.bfloat16)],
        name="hidden_back",
        **params(),
    )(*cots, w_down)


def feed_kernel(*refs):
    *parts, d_hidden_ref, gate_ref, up_ref, hidden_ref, d_gate_ref, d_up_ref, normed = refs

    @pl.when(pl.program_id(0) == 0)
    def _():
        at = 0
        for ref in parts:
            normed[at : at + ref.shape[0], :] = ref[...]
            at += ref.shape[0]

    gate_val, up_val = dot(normed[...], gate_ref[...]), dot(normed[...], up_ref[...])
    d_hidden = d_hidden_ref[...].astype(jnp.float32)
    gate_sig = jax.nn.sigmoid(gate_val)
    swish = gate_val * gate_sig
    hidden_ref[...] = (swish * up_val).astype(jnp.bfloat16)
    d_gate = d_hidden * up_val * (gate_sig + swish * (1.0 - gate_sig))
    d_gate_ref[...] = d_gate.astype(jnp.bfloat16)
    d_up_ref[...] = (d_hidden * swish).astype(jnp.bfloat16)


def feed_forward(normed, d_hidden, w_gate, w_up):
    rows, width = sum(item.shape[0] for item in normed), normed[0].shape[1]
    units, tile = w_gate.shape[1], 256
    cols = pl.BlockSpec((width, tile), lambda j: (0, j))
    out = pl.BlockSpec((rows, tile), lambda j: (0, j))
    return pl.pallas_call(
        feed_kernel,
        grid=(pl.cdiv(units, tile),),
        in_specs=[*(whole(item) for item in normed), out, cols, cols],
        out_specs=[out] * 3,
        out_shape=[jax.ShapeDtypeStruct((rows, units), jnp.bfloat16)] * 3,
        scratch_shapes=[pltpu.VMEM((rows, width), jnp.bfloat16)],
        name="feed_forward",
        **params(),
    )(*normed, d_hidden, w_gate, w_up)


def share_kernel(*refs, count, transposed):
    outs = refs[2 * count :]
    multiply = contract_cols if transposed else dot
    part = multiply(refs[0][...], refs[count][...])
    for left, right in zip(refs[1:count], refs[count + 1 : 2 * count]):
        part = part + multiply(left[...], right[...])
    rows = outs[0].shape[0]
    for place, ref in enumerate(outs):
        ref[...] = part[place * rows : (place + 1) * rows].astype(jnp.bfloat16)


def row_shares(lefts, rights, transposed, rows):
    blocks = lefts[0].shape[0] // rows
    width, tile = rights[0].shape[0 if transposed else 1], 512

    def right_spec(item):
        if transposed:
            return pl.BlockSpec((tile, item.shape[1]), lambda j: (j, 0))
        return pl.BlockSpec((item.shape[0], tile), lambda j: (0, j))

    return pl.pallas_call(
        functools.partial(share_kernel, count=len(lefts), transposed=transposed),
        grid=(width // tile,),
        in_specs=[*(whole(item) for item in lefts), *(right_spec(item) for item in rights)],
        out_specs=[pl.BlockSpec((rows, tile), lambda j: (0, j))] * blocks,
        out_shape=[jax.ShapeDtypeStruct((rows, width), jnp.bfloat16)] * blocks,
        name="row_shares",
        **params(),
    )(*lefts, *rights)


def outer_kernel(order_ref, *refs, shape, pieces):
    outs, refs = refs[-2 * len(pieces) :], list(refs[: -2 * len(pieces)])
    totals = None
    for lefts, rights in shape:
        rows = jnp.concatenate(
            [
                jnp.concatenate([refs.pop(0)[...] for _ in range(OUTER_BLOCKS)], axis=1)
                for _ in range(lefts)
            ],
            axis=0,
        )
        parts = [contract_rows(rows, refs.pop(0)[...]) for _ in range(rights)]
        totals = parts if totals is None else [a + b for a, b in zip(totals, parts)]
    step = pl.program_id(0)
    half = pl.num_programs(0) // 2
    for place, piece in enumerate(pieces):
        total = jnp.concatenate(totals[piece], axis=1).astype(jnp.bfloat16)

        @pl.when(step < half)
        def _():
            outs[2 * place][...] = total

        @pl.when(step >= half)
        def _():
            outs[2 * place + 1][...] = total


def outer(sections, index, bits, pieces):
    width = sections[0][0][0].shape[1]
    share = width // (1 << len(bits))
    tile = 256
    if share == tile:
        blocks = jnp.stack([index ^ item for item in block_order(bits)]).astype(jnp.int32)
    else:
        blocks = jnp.arange(width // tile, dtype=jnp.int32)
        sections = [
            ([permuted_features(item, index, bits) for item in lefts], rights)
            for lefts, rights in sections
        ]
    count = width // tile // OUTER_BLOCKS
    sizes = [sum(item.shape[1] for item in sections[0][1][piece]) for piece in pieces]
    specs, arrays = [], []
    for lefts, rights in sections:
        for item in lefts:
            for i in range(OUTER_BLOCKS):
                specs.append(
                    pl.BlockSpec(
                        (item.shape[0], tile), lambda j, b, i=i: (0, b[j * OUTER_BLOCKS + i])
                    )
                )
                arrays.append(item)
        specs.extend(whole(item) for item in rights)
        arrays.extend(rights)
    return pl.pallas_call(
        functools.partial(
            outer_kernel,
            shape=[(len(lefts), len(rights)) for lefts, rights in sections],
            pieces=pieces,
        ),
        grid_spec=pltpu.PrefetchScalarGridSpec(
            num_scalar_prefetch=1,
            grid=(count,),
            in_specs=specs,
            out_specs=[
                pl.BlockSpec((tile * OUTER_BLOCKS, size), at)
                for size in sizes
                for at in (
                    lambda j, _: (jnp.minimum(j, count // 2 - 1), 0),
                    lambda j, _: (jnp.maximum(j - count // 2, 0), 0),
                )
            ],
        ),
        out_shape=[
            jax.ShapeDtypeStruct((width // 2, size), jnp.bfloat16) for size in sizes for _ in range(2)
        ],
        name="outer",
        **params(),
    )(blocks, *arrays)


def halves_kernel(kept_a, kept_b, came_a, came_b, sent_ref, kept_ref):
    sent_ref[...] = added(kept_a[...], came_a[...])
    kept_ref[...] = added(kept_b[...], came_b[...])


def add_halves(kept, came):
    half, columns = kept.shape[0] // 2, kept.shape[1]
    block = min(256, half)
    first = pl.BlockSpec((block, columns), lambda i: (i, 0))
    second = pl.BlockSpec((block, columns), lambda i: (i + half // block, 0))
    return pl.pallas_call(
        halves_kernel,
        grid=(half // block,),
        in_specs=[first, second, first, second],
        out_specs=[first, first],
        out_shape=[jax.ShapeDtypeStruct((half, columns), jnp.bfloat16)] * 2,
        name="add_halves",
        **params(),
    )(kept, kept, came, came)


def total_kernel(kept_ref, came_ref, out_ref):
    out_ref[...] = kept_ref[...].astype(jnp.float32) + came_ref[...].astype(jnp.float32)


def add_total(kept, came):
    return pl.pallas_call(
        total_kernel,
        out_shape=jax.ShapeDtypeStruct(kept.shape, jnp.float32),
        name="add_total",
        **params(),
    )(kept, came)


def key_value_kernel(
    at_ref, dkn_ref, dkf_ref, dvn_ref, dvf_ref, cosn_ref, sinn_ref, cosf_ref, sinf_ref, near_ref, far_ref
):
    rows = dkn_ref.shape[0] // 4
    for m in range(4):
        at = pl.ds(pl.multiple_of(at_ref[m], rows), rows)
        mine = slice(m % 2 * rows, (m % 2 + 1) * rows)
        cos_ref, sin_ref = (cosn_ref, sinn_ref) if m < 2 else (cosf_ref, sinf_ref)
        d_key = dkn_ref[at, :] + dkf_ref[at, :]
        d_val = dvn_ref[at, :] + dvf_ref[at, :]
        both = jnp.concatenate([d_key, d_val], axis=1)
        turned = both * cos_ref[mine, :] - swap_halves(both) * sin_ref[mine, :]
        both = jnp.concatenate([turned[:, :HD], d_val], axis=1).astype(jnp.bfloat16)
        target = near_ref if m < 2 else far_ref
        target[mine, :] = both


def key_value_rows(dk_n, dk_f, dv_n, dv_f, tables, block_pos):
    shape = jax.ShapeDtypeStruct((dk_n.shape[0] // 2, 2 * HD), jnp.bfloat16)
    arrays = (dk_n, dk_f, dv_n, dv_f, *tables)
    return pl.pallas_call(
        key_value_kernel,
        grid_spec=pltpu.PrefetchScalarGridSpec(
            num_scalar_prefetch=1,
            grid=(1,),
            in_specs=[whole(item) for item in arrays],
            out_specs=[whole(shape), whole(shape)],
        ),
        out_shape=[shape, shape],
        name="key_value_rows",
        **params(),
    )(block_pos, *arrays)


def swapped(parts, flip):
    pairs = [(i, i ^ flip) for i in range(4)]
    return tuple(lax.ppermute(part, "tensor", pairs) for part in parts)


def swap_core(parts):
    return swapped(parts, 1)


def swap_chip(parts):
    return swapped(parts, 2)


def swap_pair(parts, size):
    return tuple(exchange(part, PAIR, size) for part in parts)


class Order:
    def __init__(self):
        self.last = ()

    def after(self, *values):
        tied = lax.optimization_barrier(values + (self.last,))[: len(values)]
        self.last = tied
        return tied if len(values) > 1 else tied[0]

    def done(self, *values):
        values = lax.optimization_barrier(values + (self.last,))[: len(values)]
        self.last = values
        return values if len(values) > 1 else values[0]


def wait_for(value, *others):
    return lax.optimization_barrier((value,) + others)[0]


def rows_of(one, two):
    return jnp.concatenate([one, two], axis=0)


def block_order(bits):
    order = [0]
    for bit in reversed(bits):
        order = [item ^ bit for item in order] + order
    return order


def permuted_features(value, index, bits):
    order = block_order(bits)
    width = value.shape[1] // len(order)
    return jnp.concatenate(
        [lax.dynamic_slice_in_dim(value, (index ^ item) * width, width, 1) for item in order], axis=1
    )


def rows_and_cols(one, two):
    return jnp.concatenate([one, two], axis=1)


def exchange(value, bit, size):
    return lax.ppermute(value, "dp", [(i, i ^ bit) for i in range(size)])


class Reduction:
    def __init__(self, order, sent, kept, bits, size, assemble=None):
        self.order, self.sent, self.kept, self.assemble = order, sent, kept, assemble
        self.bits, self.size, self.step = bits, size, 0
        self.total = None

    def send(self, *others):
        sent = wait_for(self.sent, *others) if others else self.sent
        self.came = exchange(sent, self.bits[self.step], self.size)
        return self

    def receive(self):
        self.came = self.order.after(self.came)
        return self

    def add(self):
        kept, came = self.kept, self.came
        self.step += 1
        if self.step == len(self.bits):
            self.total = self.order.done((self.assemble or add_total)(kept, came))
        else:
            self.sent, self.kept = self.order.done(*add_halves(kept, came))
        return self

    def advance(self):
        self.receive().add()
        if self.total is None:
            self.send()

    def finish(self):
        while self.total is None:
            self.advance()
        return self.total


def added(one, two):
    return (one.astype(jnp.float32) + two.astype(jnp.float32)).astype(jnp.bfloat16)


def per_device(
    dp_size,
    layer_input,
    cotangent,
    starts,
    pieces,
    norm_attn,
    w_query,
    w_key,
    w_value,
    w_out,
    norm_mlp,
    w_gate,
    w_up,
    w_down,
):
    rows = layer_input.shape[0]
    width = layer_input.shape[1]
    place = lax.axis_index("tensor")
    index = lax.axis_index("dp")
    bits = [1 << i for i in range(dp_size.bit_length() - 1)]
    late_bits = bits[1:] + bits[:1]
    begins = starts[0]

    block_pos = jnp.stack([(place ^ m) * rows for m in range(4)]).astype(jnp.int32)
    near_pos, far_pos = block_pos[:2], block_pos[2:]
    row_pos = (block_pos[:, None] + jnp.arange(rows, dtype=jnp.int32)[None, :]).reshape(-1)
    (cos_n, sin_n), (cos_f, sin_f) = (
        rope_tables(half) for half in (row_pos[: 2 * rows], row_pos[2 * rows :])
    )
    w_kv = jnp.concatenate([w_key, w_value], axis=1)

    def in_sequence(value):
        return jnp.concatenate(
            [lax.dynamic_slice_in_dim(value, (place ^ b) * rows, rows, 0) for b in range(4)], axis=0
        )

    def in_two(value):
        return tuple(jnp.split(value, PARTS, axis=0))

    order = Order()
    near, far = slice(0, 2 * rows), slice(2 * rows, 4 * rows)

    def chip_sum(kept, came):
        came = order.after(came)
        return order.done(*by_rows(lambda a, b: (a + b,), (kept, came), (), ((jnp.bfloat16,),)))

    x_own, cot_own = in_two(layer_input), in_two(cotangent)
    x_chip, x_core = swap_chip(x_own), swap_core(x_own)

    side = index // PAIR % 2
    units, queries = w_gate.shape[1], w_query.shape[1]
    window = -(-units // 256) * 128
    overlap = 2 * window - units
    mine = (jnp.arange(window) >= overlap) | (side == 0)
    gate_half = lax.dynamic_slice_in_dim(w_gate, side * (units - window), window, 1)
    up_half = lax.dynamic_slice_in_dim(w_up, side * (units - window), window, 1)
    up_half = jnp.where(mine[None, :], up_half, 0).astype(jnp.bfloat16)
    down_half = lax.dynamic_slice_in_dim(w_down, side * (units - window), window, 0)
    down_half = jnp.where(mine[:, None], down_half, 0).astype(jnp.bfloat16)
    gate_half, up_half, down_half, w_kv, cos_n, sin_n, cos_f, sin_f = order.done(
        gate_half, up_half, down_half, w_kv, cos_n, sin_n, cos_f, sin_f
    )
    normed_n, q_n, k_n, v_n = order.done(
        *project((*x_own, *x_core), norm_attn, w_query, w_kv, cos_n, sin_n)
    )
    x_chip = order.after(x_chip)
    cot_own_ = wait_for(cot_own, x_chip)
    cot_chip, cot_core, cot_pair = (
        swap_chip(cot_own_), swap_core(cot_own_), swap_pair(cot_own_, dp_size)
    )
    normed_f, q_f, k_f, v_f = order.done(
        *project((*x_chip, *swap_core(x_chip)), norm_attn, w_query, w_kv, cos_f, sin_f)
    )
    k_low = in_sequence(rows_of(k_n, k_f))
    v_low = in_sequence(rows_of(v_n, v_f))
    attn_f, lse_f, kept, *sent = order.done(
        *attend_forward(q_f, k_low, v_low, w_out, begins, far_pos)
    )
    came = swap_core(sent)
    cot_chip, cot_pair = order.after(cot_chip, cot_pair)
    cot_diag, cot_other, cot_pcore = (
        swap_pair(cot_chip, dp_size), swap_core(cot_chip), swap_core(cot_pair)
    )
    attn_came = swap_chip(chip_sum(kept, came))
    cot_core, cot_other, cot_pcore, q_n = order.after(cot_core, cot_other, cot_pcore, q_n)
    attn_n, lse_n, kept, *sent = order.done(
        *attend_forward(q_n, k_low, v_low, w_out, begins, near_pos)
    )
    sum_came = swap_core(sent)

    def cot_back(*cots):
        return order.done(hidden_back(order.after(cots), down_half))

    near_back_hidden = cot_back(*cot_own, *cot_core)
    cot_diag = order.after(cot_diag)
    cot_dcore = swap_core(cot_diag)
    attn_came = order.after(attn_came)
    sum_came, cot_dcore = order.after(sum_came, cot_dcore)

    def norm_mid(x, kept, core, chip, gain):
        resid = x + (kept + core + chip)
        return resid, resid * rms_inverse(resid) * gain

    resid_mid, mlp_own = order.done(
        *by_rows(
            norm_mid, (x_own, kept, sum_came, attn_came), (norm_mlp,), (jnp.float32, (jnp.bfloat16,))
        )
    )
    mlp_core, mlp_chip, mlp_pair = swap_core(mlp_own), swap_chip(mlp_own), swap_pair(mlp_own, dp_size)
    mlp_core = order.after(mlp_core)

    def feed(normed, d_hidden):
        return order.done(*feed_forward(normed, d_hidden, gate_half, up_half))

    near_hidden = feed((*mlp_own, *mlp_core), near_back_hidden)
    side_back_hidden = cot_back(*cot_chip, *cot_other, *cot_pair, *cot_pcore)
    diag_back_hidden = cot_back(*cot_diag, *cot_dcore)
    mlp_chip, mlp_pair = order.after(mlp_chip, mlp_pair)
    half = rows // 2
    mlp_diag = (
        *swap_chip((mlp_pair[0][:half],)), *swap_pair((mlp_chip[0][half:],), dp_size)
    )
    mlp_other, mlp_pcore = order.after(swap_core(mlp_chip), swap_core(mlp_pair))
    side_hidden = feed((*mlp_chip, *mlp_other, *mlp_pair, *mlp_pcore), side_back_hidden)
    mlp_diag = order.after(mlp_diag)
    mlp_dcore = order.after(swap_core(mlp_diag))
    diag_hidden = feed((*mlp_diag, *mlp_dcore), diag_back_hidden)
    hiddens = (near_hidden, side_hidden, diag_hidden)

    def in_window(kept, came):
        first = jnp.where(side == 0, kept, came)
        second = jnp.where(side == 0, came, kept)
        return jnp.concatenate([first, second[:, overlap:]], axis=1).astype(jnp.float32)

    pair_bits = [bit for bit in bits if bit != PAIR] + [PAIR]
    always = begins[0] >= 0

    def fence(step):
        def inside():
            outer_last, order.last = order.last, ()
            try:
                return step()
            finally:
                order.last = outer_last

        shapes = jax.eval_shape(inside)
        taken = order.after(always)
        results = lax.cond(
            taken,
            inside,
            lambda: jax.tree.map(lambda item: jnp.zeros(item.shape, item.dtype), shapes),
        )
        leaves, tree = jax.tree.flatten(results)
        return jax.tree.unflatten(tree, order.done(tuple(leaves)))

    def gradient(sections, order_bits, pieces=(slice(None),)):
        lefts, rights = order.after([item[0] for item in sections], [item[1] for item in sections])
        return order.done(*outer(list(zip(lefts, rights)), index, order_bits, pieces))

    cots = (
        (*cot_own, *cot_core),
        (*cot_chip, *cot_other, *cot_pair, *cot_pcore),
        (*cot_diag, *cot_dcore),
    )
    mlps = (
        (*mlp_own, *mlp_core),
        (*mlp_chip, *mlp_other, *mlp_pair, *mlp_pcore),
        (*mlp_diag, *mlp_dcore),
    )

    def mlp_gradients(lefts, which):
        sections = [(left, [right[i] for i in which]) for left, right in zip(lefts, hiddens)]
        return gradient(sections, pair_bits, [slice(i, i + 1) for i in range(len(which))])

    def reduction(sent_kept, order_bits, assemble=None):
        return Reduction(order, *sent_kept, order_bits, dp_size, assemble)

    def shares(lefts, rights, transposed=True):
        parts = order.done(*row_shares(order.after(lefts), rights, transposed, rows))
        return [(parts[i], swap_core((parts[i + 1],))) for i in range(0, len(parts), 2)]

    def total(*items):
        return order.done(*by_rows(lambda *values: (sum(values),), items, (), ((jnp.bfloat16,),)))

    class GroupSum:
        def __init__(self, which, rights, transposed):
            self.rest = rights, transposed
            self.near, self.sides, self.diag = (tuple(item[i] for i in which) for item in hiddens)

        def diag_shares(self):
            return shares(self.diag, *self.rest)[0]

        def side_shares(self):
            return shares(self.sides, *self.rest)

        def own_shares(self):
            return shares(self.near, *self.rest)[0]

    d_norm = GroupSum((1, 2), (gate_half, up_half), True)
    block_sum = GroupSum((0,), (down_half,), False)

    down = reduction(mlp_gradients(cots, (0,)), pair_bits, in_window)
    down.send()

    @fence
    def diag_and_gradients():
        kept, came = d_norm.diag_shares()
        made = mlp_gradients(mlps, (1, 2))
        return chip_sum(kept, came), made

    diag, made = diag_and_gradients
    to_pair = swap_pair(diag, dp_size)
    gate, up = (reduction(item, pair_bits, in_window) for item in (made[:2], made[2:]))

    @fence
    def other_shares():
        chip, pair = d_norm.side_shares()
        own = d_norm.own_shares()
        return order.after(chip), order.after(pair), order.after(own)

    chip, pair, own = other_shares
    came_p = swap_pair(total(pair[0], *pair[1]), dp_size)
    to_pair = order.after(to_pair)
    came_c = swap_chip(total(chip[0], *chip[1], to_pair))
    down.receive()
    gate.send(down.came)
    down.add()
    down.send()

    @fence
    def block_shares():
        def parts(lefts):
            return order.done(*row_shares(order.after(lefts), *block_sum.rest, rows))

        kept, sent = parts(block_sum.diag)
        came = swap_core((sent,))
        kept_c, sent_c, kept_p, sent_p = parts(block_sum.sides)
        diag = chip_sum(kept, came)
        came_c = swap_core((order.after(sent_c),))
        kept, sent = parts(block_sum.near)
        came_c = order.after(came_c)
        came_p = order.after(swap_core((order.after(sent_p),)))
        came = order.after(swap_core((order.after(sent),)))
        return diag, (kept_c, came_c), (kept_p, came_p), (kept, came)

    block_diag, block_chip, block_pair, block_own = block_shares
    came_c, came_p = order.after(came_c, came_p)
    to_pair = swap_pair(block_diag, dp_size)

    def back_mid(kept, core, chip, pair, resid, cot, gain):
        d_mid = cot + norm_back(kept + core + chip + pair, resid, rms_inverse(resid), gain)
        return d_mid, d_mid

    d_mid, d_own = order.done(
        *by_rows(
            back_mid,
            (own[0], own[1], came_c, came_p, resid_mid, cot_own),
            (norm_mlp,),
            (jnp.float32, (jnp.bfloat16,)),
        )
    )
    d_chip = swap_chip(d_own)

    gate.receive()
    up.send(gate.came)
    gate.add()

    @fence
    def near_back():
        d_core = order.after(swap_core(d_own))
        return d_core, order.done(
            *attend_backward(
                q_n, (*d_own, *d_core), w_out, attn_n, lse_n, k_low, v_low, cos_n,
                sin_n, begins, near_pos,
            )
        )

    d_core, (dq_n, dk_n, dv_n) = near_back
    d_chip = order.after(d_chip)
    @fence
    def out_gradient():
        d_other = order.after(swap_core(d_chip))
        sections = [((*d_own, *d_core), (attn_n,)), ((*d_chip, *d_other), (attn_f,))]
        return d_other, gradient(sections, bits)

    d_other, wout = out_gradient
    wout = reduction(wout, bits)
    down.receive()
    gate.send(down.came)
    down.add().send()
    up.receive()
    wout.send(up.came)
    up.add()
    to_pair = order.after(to_pair)
    block_c = total(block_chip[0], *block_chip[1], to_pair)
    block_p = total(block_pair[0], *block_pair[1])

    @fence
    def far_back():
        return order.done(
            *attend_backward(
                q_f, (*d_chip, *d_other), w_out, attn_f, lse_f, k_low, v_low, cos_f,
                sin_f, begins, far_pos,
            )
        )

    dq_f, dk_f, dv_f = far_back

    @fence
    def query_gradient():
        dkv_n, dkv_f = order.done(
            *key_value_rows(dk_n, dk_f, dv_n, dv_f, (cos_n, sin_n, cos_f, sin_f), block_pos)
        )
        sections = [((normed_n,), (dq_n, dkv_n)), ((normed_f,), (dq_f, dkv_f))]
        return dkv_n, dkv_f, gradient(sections, bits)

    dkv_n, dkv_f, qkv = query_gradient
    qkv = reduction(qkv, bits)
    qkv.send()
    wout.receive()
    wout.add().send()
    down.receive().add()
    gate.receive()
    up.send(gate.came)
    gate.add().send()
    in_sum = fence(lambda: chip_sum(*shares((dq_f, dkv_f), (w_query, w_kv))[0]))
    gate.receive().add()
    d_in_came = swap_chip(in_sum)
    own = fence(lambda: order.after(shares((dq_n, dkv_n), (w_query, w_kv))[0]))
    qkv.receive()
    qkv.add().send()
    wout.receive()
    up.receive()
    block_p = swap_pair(wait_for(block_p, up.came), dp_size)
    block_c = swap_chip(wait_for(block_c, up.came))
    up.add().send()
    wout.add().send()
    d_in_came = order.after(d_in_came)

    def back_in(kept, core, chip, resid, d_mid, gain):
        return (d_mid + norm_back(kept + core + chip, resid, rms_inverse(resid), gain),)

    (x_grad,) = by_rows(
        back_in, (own[0], own[1], d_in_came, x_own, d_mid), (norm_attn,), (jnp.float32,)
    )
    x_grad = order.done(x_grad)
    qkv.receive()
    qkv.add().send()
    up.receive().add()
    wout.receive().add()
    block_c, block_p = order.after(block_c, block_p)
    qkv.receive().add()
    (block_out,) = by_rows(
        lambda *items: (sum(items),),
        (resid_mid, block_own[0], block_own[1], block_c, block_p),
        (),
        (jnp.bfloat16,),
    )
    block_out = order.done(block_out)
    for item in (down, gate, up, wout, qkv):
        item.finish()
    grad_down, grad_gate, grad_up = down.total.T, gate.total, up.total
    grad_out, grad_qkv = wout.total.T, qkv.total
    queries = w_query.shape[1]
    grad_query = grad_qkv[:, :queries]
    grad_key = grad_qkv[:, queries : queries + HD]
    grad_value = grad_qkv[:, queries + HD :]

    share = width // dp_size

    def own_features(value):
        return lax.dynamic_slice_in_dim(value, index * share, share, 0).astype(jnp.float32)

    gain_attn = (
        jnp.sum(own_features(w_query) * grad_query, axis=1)
        + jnp.sum(own_features(w_kv) * grad_qkv[:, queries:], axis=1)
    ) / own_features(norm_attn)
    gain_mlp = jnp.sum(
        own_features(w_gate) * grad_gate + own_features(w_up) * grad_up, axis=1
    ) / own_features(norm_mlp)
    gains = jnp.stack([gain_attn, gain_mlp]).reshape(2, 4, share // 4)
    gains = jnp.stack([lax.dynamic_index_in_dim(gains, place ^ m, 1, False) for m in range(4)])
    gains = gains[:2] + lax.ppermute(gains[2:], "tensor", [(i, i ^ 2) for i in range(4)])
    gains = gains[0] + lax.ppermute(gains[1], "tensor", [(i, i ^ 1) for i in range(4)])

    return (
        block_out,
        x_grad,
        gains[0],
        grad_query,
        grad_key,
        grad_value,
        grad_out,
        gains[1],
        grad_gate,
        grad_up,
        grad_down,
    )


def solution(mesh):
    in_specs = (
        P(("dp", "tensor"), None),
        P(("dp", "tensor"), None),
        P("dp", None),
        P("dp"),
        P(),
        P(None, "tensor"),
        P(None, "tensor"),
        P(None, "tensor"),
        P("tensor", None),
        P(),
        P(None, "tensor"),
        P(None, "tensor"),
        P("tensor", None),
    )
    out_specs = (
        P(("dp", "tensor"), None),
        P(("dp", "tensor"), None),
        P(("dp", "tensor")),
        P("dp", "tensor"),
        P("dp", "tensor"),
        P("dp", "tensor"),
        P("tensor", "dp"),
        P(("dp", "tensor")),
        P("dp", "tensor"),
        P("dp", "tensor"),
        P("tensor", "dp"),
    )
    return jax.shard_map(
        functools.partial(per_device, mesh.shape["dp"]),
        mesh=mesh,
        in_specs=in_specs,
        out_specs=out_specs,
        check_vma=False,
    )
```

```python
import functools

import jax
import jax.numpy as jnp
from jax import lax
from jax.experimental import pallas as pl
from jax.experimental.pallas import tpu as pltpu
from jax.sharding import PartitionSpec as P

HD = 64
SEQ = 1024
PIECE = 256
QB = 256


EPSILON = 1e-05
ROPE_BASE = 10000.0
MASKED = -1e30
VMEM_LIMIT = 48 * 2**20
PARTS = 1
OUTER_BLOCKS = 2
PAIR = 2
NT = (((1,), (1,)), ((), ()))
TN = (((0,), (0,)), ((), ()))


def dot(left, right):
    return jnp.dot(left, right, preferred_element_type=jnp.float32)


def contract_rows(left, right):
    return lax.dot_general(left, right, TN, preferred_element_type=jnp.float32)


def contract_cols(left, right):
    return lax.dot_general(left, right, NT, preferred_element_type=jnp.float32)


def rms_inverse(resid):
    return lax.rsqrt(jnp.mean(resid * resid, axis=-1, keepdims=True) + EPSILON)


def norm_back(d_norm, resid, inverse, gain):
    scaled = d_norm * gain
    return inverse * scaled - resid * (inverse * inverse * inverse) * jnp.mean(
        scaled * resid, axis=-1, keepdims=True
    )


def rope_tables(positions):
    half_dim = HD // 2
    inverse = jnp.power(ROPE_BASE, -(jnp.arange(half_dim).astype(jnp.float32) * 2.0) / HD)
    angles = positions.astype(jnp.float32)[:, None] * inverse[None, :]
    cos, sin = jnp.cos(angles), jnp.sin(angles)
    return jnp.concatenate([cos] * 4, axis=1), jnp.concatenate([-sin, sin] * 2, axis=1)


def swap_halves(pair):
    lane = lax.broadcasted_iota(jnp.int32, pair.shape, 1)
    up = pltpu.roll(pair, 2 * HD - HD // 2, 1)
    down = pltpu.roll(pair, HD // 2, 1)
    return jnp.where(lane % HD < HD // 2, up, down)


def rotate_rows(grad, cos_tab, sin_tab):
    half = HD // 2
    swapped = jnp.concatenate([grad[:, half:], grad[:, :half]], axis=1)
    return grad * cos_tab[:, :HD] - swapped * sin_tab[:, :HD]


def either(near_refs):
    half = len(near_refs) // 2
    own, core = (
        jnp.concatenate([ref[...] for ref in refs], axis=0)
        for refs in (near_refs[:half], near_refs[half:])
    )
    return jnp.where(pl.program_id(0) == 0, own, core)


def project_kernel(*refs):
    x_refs = refs[:-9]
    gain_ref, wq_ref, wkv_ref, cos_ref, sin_ref, n_ref, q_ref, k_ref, v_ref = refs[-9:]
    resid = either(x_refs).astype(jnp.float32)
    normed = (resid * rms_inverse(resid) * gain_ref[...]).astype(jnp.bfloat16)
    n_ref[...] = normed
    cos, sin = cos_ref[...], sin_ref[...]
    query = dot(normed, wq_ref[...])
    for first in range(0, query.shape[1], 2 * HD):
        pair = query[:, first : first + 2 * HD]
        turned = (pair * cos + swap_halves(pair) * sin) * HD ** (-0.5)
        q_ref[:, first : first + 2 * HD] = turned.astype(jnp.bfloat16)
    key_value = dot(normed, wkv_ref[...])
    turned = key_value * cos + swap_halves(key_value) * sin
    k_ref[...] = turned[:, :HD].astype(jnp.bfloat16)
    v_ref[...] = key_value[:, HD:].astype(jnp.bfloat16)


def whole(array):
    return pl.BlockSpec(array.shape, lambda *_: (0,) * len(array.shape))


def params():
    return {
        "compiler_params": pltpu.CompilerParams(vmem_limit_bytes=VMEM_LIMIT),
        "cost_estimate": pl.CostEstimate(flops=1, bytes_accessed=1, transcendentals=0),
    }


def project(parts, gain, w_query, w_kv, cos_tab, sin_tab):
    rows, width = sum(part.shape[0] for part in parts) // 2, parts[0].shape[1]
    queries = w_query.shape[1]

    def tall(cols):
        return pl.BlockSpec((rows, cols), lambda i: (i, 0))

    gain = gain[None, :]
    return pl.pallas_call(
        project_kernel,
        grid=(2,),
        in_specs=[
            *(whole(item) for item in (*parts, gain, w_query, w_kv)), tall(2 * HD), tall(2 * HD)
        ],
        out_specs=[tall(width), tall(queries), tall(HD), tall(HD)],
        out_shape=[
            jax.ShapeDtypeStruct((2 * rows, width), jnp.bfloat16),
            jax.ShapeDtypeStruct((2 * rows, queries), jnp.bfloat16),
            jax.ShapeDtypeStruct((2 * rows, HD), jnp.bfloat16),
            jax.ShapeDtypeStruct((2 * rows, HD), jnp.bfloat16),
        ],
        name="project",
        **params(),
    )(*parts, gain, w_query, w_kv, cos_tab, sin_tab)


def by_rows(function, ins, consts, outs):
    flat, counts = [], []
    for item in ins:
        item = item if isinstance(item, tuple) else (item,)
        counts.append([len(flat) + sum(one is not None for one in item[:i]) if part is not None else None
                       for i, part in enumerate(item)])
        flat.extend(part for part in item if part is not None)
    rows, width = sum(flat[at].shape[0] for at in counts[0]), flat[0].shape[1]
    out_counts = [PARTS if isinstance(item, tuple) else 1 for item in outs]
    dtypes = [item[0] if isinstance(item, tuple) else item for item in outs]
    starts = [sum(out_counts[:i]) for i in range(len(outs))]
    out_places = [range(first, first + count) for first, count in zip(starts, out_counts)]
    step = 32

    def kernel(*refs):
        given = [ref[...] for ref in refs[len(flat) : len(flat) + len(consts)]]

        def views(part_refs, places, part):
            found = []
            for place in places:
                each = PARTS // len(place)
                at = place[part // each]
                ref = None if at is None else part_refs[at]
                found.append((ref, part % each * (rows // PARTS)))
            return found

        for part in range(PARTS):
            sources = views(refs, counts, part)
            targets = views(refs[len(flat) + len(consts) :], out_places, part)

            def chunk(i, _):
                def at(base):
                    return pl.ds(pl.multiple_of(base + i * step, step), step)

                values = [
                    0.0 if ref is None else ref[at(base), :].astype(jnp.float32)
                    for ref, base in sources
                ]
                for (ref, base), value in zip(targets, function(*values, *given)):
                    ref[at(base), :] = value.astype(ref.dtype)
                return 0

            lax.fori_loop(0, rows // PARTS // step, chunk, 0)

    consts = [item[None, :] for item in consts]
    shapes = []
    for count, dtype in zip(out_counts, dtypes):
        shapes.extend([jax.ShapeDtypeStruct((rows // count, width), dtype)] * count)
    results = pl.pallas_call(kernel, out_shape=shapes, name="by_rows", **params())(*flat, *consts)
    grouped, at = [], 0
    for count, item in zip(out_counts, outs):
        grouped.append(tuple(results[at : at + count]) if isinstance(item, tuple) else results[at])
        at += count
    return grouped


def see(qpos, kpos, starts_ref, pics):
    mask = kpos <= qpos
    for pic in range(pics):
        begin = starts_ref[pic]
        mask = mask | (
            (qpos >= begin) & (qpos < begin + PIECE) & (kpos >= begin) & (kpos < begin + PIECE)
        )
    return mask


def key_blocks(starts_ref, pics, first):
    edge = first + QB
    crossed = jnp.bool_(False)
    for pic in range(pics):
        begin = starts_ref[pic]
        crossed = crossed | ((begin < edge) & (begin + PIECE > edge))
    return edge // QB + jnp.where(crossed, 1, 0)


def forward_kernel(
    pos_ref, starts_ref, q_ref, k_ref, v_ref, out_ref, o_ref, lse_ref, kept_ref, *rest, heads, pics, seq
):
    *sent_refs, bias = rest
    first = pos_ref[pl.program_id(0)]
    count = key_blocks(starts_ref, pics, first)
    for blocks in range(1, seq // QB + 1):

        @pl.when(count == blocks)
        def _():
            ext = blocks * QB
            low = max(0, ext - 2 * QB)
            wide = ext - low
            qpos = lax.broadcasted_iota(jnp.int32, (QB, wide), 0) + first
            kpos = lax.broadcasted_iota(jnp.int32, (QB, wide), 1) + low
            bias[:, :wide] = jnp.where(see(qpos, kpos, starts_ref, pics), 0.0, MASKED)
            values = jnp.concatenate([v_ref[:ext, :], jnp.ones((ext, HD), jnp.bfloat16)], axis=1)
            lane = lax.broadcasted_iota(jnp.int32, (QB, heads), 1)

            def one_pair(pair, stats):
                at = pl.ds(pl.multiple_of(pair * 2 * HD, 2 * HD), 2 * HD)
                both = q_ref[:, at]
                outs = []
                for side in range(2):
                    scores = contract_cols(both[:, side * HD : (side + 1) * HD], k_ref[:ext, :])
                    if low:
                        scores = jnp.concatenate(
                            [scores[:, :low], scores[:, low:] + bias[:, :wide]], axis=1
                        )
                    else:
                        scores = scores + bias[:, :wide]
                    row_max = jnp.max(scores, axis=1, keepdims=True)
                    terms = jnp.exp(scores - row_max).astype(jnp.bfloat16)
                    summed = dot(terms, values)
                    row_sum = summed[:, HD : HD + 1]
                    outs.append(summed[:, :HD] / row_sum)
                    stats = jnp.where(lane == 2 * pair + side, row_max + jnp.log(row_sum), stats)
                o_ref[:, at] = jnp.concatenate(outs, axis=1).astype(jnp.bfloat16)
                return stats

            lse_ref[...] = lax.fori_loop(
                0, heads // 2, one_pair, jnp.zeros((QB, heads), jnp.float32), unroll=4
            )

    part = dot(o_ref[...], out_ref[...]).astype(jnp.bfloat16)

    @pl.when(pl.program_id(0) == 0)
    def _():
        kept_ref[...] = part

    @pl.when(pl.program_id(0) == 1)
    def _():
        for i, ref in enumerate(sent_refs):
            ref[...] = part[i * ref.shape[0] : (i + 1) * ref.shape[0]]


def attend_forward(q_low, k_low, v_low, w_out, starts, positions):
    rows, width = q_low.shape
    heads, seq, pics = width // HD, k_low.shape[0], starts.shape[0]
    tall = pl.BlockSpec((QB, width), lambda i, *_: (i, 0))
    parts = [(QB, w_out.shape[1])] + [(QB // PARTS, w_out.shape[1])] * PARTS
    keys = pl.BlockSpec((seq, HD), lambda i, *_: (0, 0))
    return pl.pallas_call(
        functools.partial(forward_kernel, heads=heads, pics=pics, seq=seq),
        grid_spec=pltpu.PrefetchScalarGridSpec(
            num_scalar_prefetch=2,
            grid=(rows // QB,),
            in_specs=[tall, keys, keys, whole(w_out)],
            out_specs=[
                tall,
                pl.BlockSpec((QB, heads), lambda i, *_: (i, 0)),
                *(pl.BlockSpec(part, lambda i, *_: (0, 0)) for part in parts),
            ],
            scratch_shapes=[pltpu.VMEM((QB, 2 * QB), jnp.float32)],
        ),
        out_shape=[
            jax.ShapeDtypeStruct((rows, width), jnp.bfloat16),
            jax.ShapeDtypeStruct((rows, heads), jnp.float32),
            *(jax.ShapeDtypeStruct(part, jnp.bfloat16) for part in parts),
        ],
        name="attend_forward",
        **params(),
    )(positions, starts, q_low, k_low, v_low, w_out)


def in_three(value):
    top = value.astype(jnp.bfloat16)
    rest = value - top.astype(jnp.float32)
    middle = rest.astype(jnp.bfloat16)
    last = (rest - middle.astype(jnp.float32)).astype(jnp.bfloat16)
    return [top, middle, last]


def backward_kernel(
    pos_ref, starts_ref, q_ref, out_ref, o_ref, lse_ref, k_ref, v_ref, cos_ref, sin_ref,
    *rest, heads, pics, seq
):
    *d_refs, dq_ref, dk_ref, dv_ref, bias, do_ref = rest
    first = pos_ref[pl.program_id(0)]
    count = key_blocks(starts_ref, pics, first)

    @pl.when(pl.program_id(0) == 0)
    def _():
        dk_ref[...] = jnp.zeros_like(dk_ref)
        dv_ref[...] = jnp.zeros_like(dv_ref)

    do_ref[...] = contract_cols(either(d_refs), out_ref[...]).astype(jnp.bfloat16)

    for blocks in range(1, seq // QB + 1):

        @pl.when(count == blocks)
        def _():
            ext = blocks * QB
            low = max(0, ext - 2 * QB)
            wide = ext - low
            kpos = lax.broadcasted_iota(jnp.int32, (wide, QB), 0) + low
            qpos = lax.broadcasted_iota(jnp.int32, (wide, QB), 1) + first
            bias[:wide, :] = jnp.where(see(qpos, kpos, starts_ref, pics), 0.0, MASKED)
            ones = jnp.ones((ext, HD), jnp.bfloat16)
            keys = jnp.concatenate([k_ref[:ext, :], ones], axis=1)
            values = jnp.concatenate([v_ref[:ext, :], ones], axis=1)
            zeros = jnp.zeros((QB, HD - 3), jnp.bfloat16)
            lane = lax.broadcasted_iota(jnp.int32, (QB, heads), 1)

            def one_pair(pair, _):
                at = pl.ds(pl.multiple_of(pair * 2 * HD, 2 * HD), 2 * HD)
                q_both, d_both, o_both = q_ref[:, at], do_ref[:, at], o_ref[:, at]
                stats = lse_ref[...]
                d_query, d_key, d_val = [], 0.0, 0.0
                for side in range(2):
                    cols = slice(side * HD, (side + 1) * HD)
                    queries, d_out = q_both[:, cols], d_both[:, cols]
                    delta = jnp.sum(
                        d_out.astype(jnp.float32) * o_both[:, cols].astype(jnp.float32),
                        axis=1,
                        keepdims=True,
                    )
                    lse = jnp.sum(
                        jnp.where(lane == 2 * pair + side, stats, 0.0), axis=1, keepdims=True
                    )
                    queries_ext = jnp.concatenate([queries] + in_three(-lse) + [zeros], axis=1)
                    d_out_ext = jnp.concatenate([d_out] + in_three(-delta) + [zeros], axis=1)
                    scores = contract_cols(keys, queries_ext)
                    if low:
                        scores = jnp.concatenate(
                            [scores[:low], scores[low:] + bias[:wide, :]], axis=0
                        )
                    else:
                        scores = scores + bias[:wide, :]
                    probs = jnp.exp(scores)
                    d_probs = contract_cols(values, d_out_ext)
                    d_scores = (probs * d_probs).astype(jnp.bfloat16)
                    d_val += dot(probs.astype(jnp.bfloat16), d_out)
                    d_key += dot(d_scores, queries)
                    d_query.append(contract_rows(d_scores, k_ref[:ext, :]))
                dk_ref[:ext, :] += d_key
                dv_ref[:ext, :] += d_val
                turned = jnp.concatenate(d_query, axis=1) * HD ** (-0.5)
                turned = turned * cos_ref[...] - swap_halves(turned) * sin_ref[...]
                dq_ref[:, at] = turned.astype(jnp.bfloat16)
                return 0

            lax.fori_loop(0, heads // 2, one_pair, 0, unroll=2)


def attend_backward(
    q_low, d_parts, w_out, attn_low, lse, k_low, v_low, cos_tab, sin_tab, starts, positions
):
    rows, width = q_low.shape
    heads, seq, pics = width // HD, k_low.shape[0], starts.shape[0]
    tall = pl.BlockSpec((QB, width), lambda i, *_: (i, 0))
    table = pl.BlockSpec((QB, 2 * HD), lambda i, *_: (i, 0))
    stats = pl.BlockSpec((QB, heads), lambda i, *_: (i, 0))
    keys = whole(k_low)
    return pl.pallas_call(
        functools.partial(backward_kernel, heads=heads, pics=pics, seq=seq),
        grid_spec=pltpu.PrefetchScalarGridSpec(
            num_scalar_prefetch=2,
            grid=(rows // QB,),
            in_specs=[
                tall, whole(w_out), tall, stats, keys, keys, table, table,
                *(whole(part) for part in d_parts),
            ],
            out_specs=[tall, keys, keys],
            scratch_shapes=[
                pltpu.VMEM((2 * QB, QB), jnp.float32),
                pltpu.VMEM((QB, width), jnp.bfloat16),
            ],
        ),
        out_shape=[
            jax.ShapeDtypeStruct((rows, width), jnp.bfloat16),
            jax.ShapeDtypeStruct((seq, HD), jnp.float32),
            jax.ShapeDtypeStruct((seq, HD), jnp.float32),
        ],
        name="attend_backward",
        **params(),
    )(
        positions, starts, q_low, w_out, attn_low, lse, k_low, v_low, cos_tab, sin_tab, *d_parts
    )


def hidden_kernel(*refs):
    *parts, down_ref, out_ref, cots = refs

    @pl.when(pl.program_id(0) == 0)
    def _():
        at = 0
        for ref in parts:
            cots[at : at + ref.shape[0], :] = ref[...]
            at += ref.shape[0]

    out_ref[...] = contract_cols(cots[...], down_ref[...]).astype(jnp.bfloat16)


def hidden_back(cots, w_down):
    rows, width = sum(item.shape[0] for item in cots), cots[0].shape[1]
    units, tile = w_down.shape[0], 256
    return pl.pallas_call(
        hidden_kernel,
        grid=(pl.cdiv(units, tile),),
        in_specs=[
            *(whole(item) for item in cots), pl.BlockSpec((tile, width), lambda j: (j, 0))
        ],
        out_specs=pl.BlockSpec((rows, tile), lambda j: (0, j)),
        out_shape=jax.ShapeDtypeStruct((rows, units), jnp.bfloat16),
        scratch_shapes=[pltpu.VMEM((rows, width), jnp.bfloat16)],
        name="hidden_back",
        **params(),
    )(*cots, w_down)


def feed_kernel(*refs):
    *parts, d_hidden_ref, gate_ref, up_ref, hidden_ref, d_gate_ref, d_up_ref, normed = refs

    @pl.when(pl.program_id(0) == 0)
    def _():
        at = 0
        for ref in parts:
            normed[at : at + ref.shape[0], :] = ref[...]
            at += ref.shape[0]

    gate_val, up_val = dot(normed[...], gate_ref[...]), dot(normed[...], up_ref[...])
    d_hidden = d_hidden_ref[...].astype(jnp.float32)
    gate_sig = jax.nn.sigmoid(gate_val)
    swish = gate_val * gate_sig
    hidden_ref[...] = (swish * up_val).astype(jnp.bfloat16)
    d_gate = d_hidden * up_val * (gate_sig + swish * (1.0 - gate_sig))
    d_gate_ref[...] = d_gate.astype(jnp.bfloat16)
    d_up_ref[...] = (d_hidden * swish).astype(jnp.bfloat16)


def feed_forward(normed, d_hidden, w_gate, w_up):
    rows, width = sum(item.shape[0] for item in normed), normed[0].shape[1]
    units, tile = w_gate.shape[1], 256
    cols = pl.BlockSpec((width, tile), lambda j: (0, j))
    out = pl.BlockSpec((rows, tile), lambda j: (0, j))
    return pl.pallas_call(
        feed_kernel,
        grid=(pl.cdiv(units, tile),),
        in_specs=[*(whole(item) for item in normed), out, cols, cols],
        out_specs=[out] * 3,
        out_shape=[jax.ShapeDtypeStruct((rows, units), jnp.bfloat16)] * 3,
        scratch_shapes=[pltpu.VMEM((rows, width), jnp.bfloat16)],
        name="feed_forward",
        **params(),
    )(*normed, d_hidden, w_gate, w_up)


def share_kernel(*refs, count, transposed):
    outs = refs[2 * count :]
    multiply = contract_cols if transposed else dot
    part = multiply(refs[0][...], refs[count][...])
    for left, right in zip(refs[1:count], refs[count + 1 : 2 * count]):
        part = part + multiply(left[...], right[...])
    rows = outs[0].shape[0]
    for place, ref in enumerate(outs):
        ref[...] = part[place * rows : (place + 1) * rows].astype(jnp.bfloat16)


def row_shares(lefts, rights, transposed, rows):
    blocks = lefts[0].shape[0] // rows
    width, tile = rights[0].shape[0 if transposed else 1], 512

    def right_spec(item):
        if transposed:
            return pl.BlockSpec((tile, item.shape[1]), lambda j: (j, 0))
        return pl.BlockSpec((item.shape[0], tile), lambda j: (0, j))

    return pl.pallas_call(
        functools.partial(share_kernel, count=len(lefts), transposed=transposed),
        grid=(width // tile,),
        in_specs=[*(whole(item) for item in lefts), *(right_spec(item) for item in rights)],
        out_specs=[pl.BlockSpec((rows, tile), lambda j: (0, j))] * blocks,
        out_shape=[jax.ShapeDtypeStruct((rows, width), jnp.bfloat16)] * blocks,
        name="row_shares",
        **params(),
    )(*lefts, *rights)


def outer_kernel(order_ref, *refs, shape, pieces):
    outs, refs = refs[-2 * len(pieces) :], list(refs[: -2 * len(pieces)])
    totals = None
    for lefts, rights in shape:
        rows = jnp.concatenate(
            [
                jnp.concatenate([refs.pop(0)[...] for _ in range(OUTER_BLOCKS)], axis=1)
                for _ in range(lefts)
            ],
            axis=0,
        )
        parts = [contract_rows(rows, refs.pop(0)[...]) for _ in range(rights)]
        totals = parts if totals is None else [a + b for a, b in zip(totals, parts)]
    step = pl.program_id(0)
    half = pl.num_programs(0) // 2
    for place, piece in enumerate(pieces):
        total = jnp.concatenate(totals[piece], axis=1).astype(jnp.bfloat16)

        @pl.when(step < half)
        def _():
            outs[2 * place][...] = total

        @pl.when(step >= half)
        def _():
            outs[2 * place + 1][...] = total


def outer(sections, index, bits, pieces):
    width = sections[0][0][0].shape[1]
    share = width // (1 << len(bits))
    tile = 256
    if share == tile:
        blocks = jnp.stack([index ^ item for item in block_order(bits)]).astype(jnp.int32)
    else:
        blocks = jnp.arange(width // tile, dtype=jnp.int32)
        sections = [
            ([permuted_features(item, index, bits) for item in lefts], rights)
            for lefts, rights in sections
        ]
    count = width // tile // OUTER_BLOCKS
    sizes = [sum(item.shape[1] for item in sections[0][1][piece]) for piece in pieces]
    specs, arrays = [], []
    for lefts, rights in sections:
        for item in lefts:
            for i in range(OUTER_BLOCKS):
                specs.append(
                    pl.BlockSpec(
                        (item.shape[0], tile), lambda j, b, i=i: (0, b[j * OUTER_BLOCKS + i])
                    )
                )
                arrays.append(item)
        specs.extend(whole(item) for item in rights)
        arrays.extend(rights)
    return pl.pallas_call(
        functools.partial(
            outer_kernel,
            shape=[(len(lefts), len(rights)) for lefts, rights in sections],
            pieces=pieces,
        ),
        grid_spec=pltpu.PrefetchScalarGridSpec(
            num_scalar_prefetch=1,
            grid=(count,),
            in_specs=specs,
            out_specs=[
                pl.BlockSpec((tile * OUTER_BLOCKS, size), at)
                for size in sizes
                for at in (
                    lambda j, _: (jnp.minimum(j, count // 2 - 1), 0),
                    lambda j, _: (jnp.maximum(j - count // 2, 0), 0),
                )
            ],
        ),
        out_shape=[
            jax.ShapeDtypeStruct((width // 2, size), jnp.bfloat16) for size in sizes for _ in range(2)
        ],
        name="outer",
        **params(),
    )(blocks, *arrays)


def halves_kernel(kept_a, kept_b, came_a, came_b, sent_ref, kept_ref):
    sent_ref[...] = added(kept_a[...], came_a[...])
    kept_ref[...] = added(kept_b[...], came_b[...])


def add_halves(kept, came):
    half, columns = kept.shape[0] // 2, kept.shape[1]
    block = min(256, half)
    first = pl.BlockSpec((block, columns), lambda i: (i, 0))
    second = pl.BlockSpec((block, columns), lambda i: (i + half // block, 0))
    return pl.pallas_call(
        halves_kernel,
        grid=(half // block,),
        in_specs=[first, second, first, second],
        out_specs=[first, first],
        out_shape=[jax.ShapeDtypeStruct((half, columns), jnp.bfloat16)] * 2,
        name="add_halves",
        **params(),
    )(kept, kept, came, came)


def total_kernel(kept_ref, came_ref, out_ref):
    out_ref[...] = kept_ref[...].astype(jnp.float32) + came_ref[...].astype(jnp.float32)


def add_total(kept, came):
    return pl.pallas_call(
        total_kernel,
        out_shape=jax.ShapeDtypeStruct(kept.shape, jnp.float32),
        name="add_total",
        **params(),
    )(kept, came)


def key_value_kernel(
    at_ref, dkn_ref, dkf_ref, dvn_ref, dvf_ref, cosn_ref, sinn_ref, cosf_ref, sinf_ref, near_ref, far_ref
):
    rows = dkn_ref.shape[0] // 4
    for m in range(4):
        at = pl.ds(pl.multiple_of(at_ref[m], rows), rows)
        mine = slice(m % 2 * rows, (m % 2 + 1) * rows)
        cos_ref, sin_ref = (cosn_ref, sinn_ref) if m < 2 else (cosf_ref, sinf_ref)
        d_key = dkn_ref[at, :] + dkf_ref[at, :]
        d_val = dvn_ref[at, :] + dvf_ref[at, :]
        both = jnp.concatenate([d_key, d_val], axis=1)
        turned = both * cos_ref[mine, :] - swap_halves(both) * sin_ref[mine, :]
        both = jnp.concatenate([turned[:, :HD], d_val], axis=1).astype(jnp.bfloat16)
        target = near_ref if m < 2 else far_ref
        target[mine, :] = both


def key_value_rows(dk_n, dk_f, dv_n, dv_f, tables, block_pos):
    shape = jax.ShapeDtypeStruct((dk_n.shape[0] // 2, 2 * HD), jnp.bfloat16)
    arrays = (dk_n, dk_f, dv_n, dv_f, *tables)
    return pl.pallas_call(
        key_value_kernel,
        grid_spec=pltpu.PrefetchScalarGridSpec(
            num_scalar_prefetch=1,
            grid=(1,),
            in_specs=[whole(item) for item in arrays],
            out_specs=[whole(shape), whole(shape)],
        ),
        out_shape=[shape, shape],
        name="key_value_rows",
        **params(),
    )(block_pos, *arrays)


def swapped(parts, flip):
    pairs = [(i, i ^ flip) for i in range(4)]
    return tuple(lax.ppermute(part, "tensor", pairs) for part in parts)


def swap_core(parts):
    return swapped(parts, 1)


def swap_chip(parts):
    return swapped(parts, 2)


def swap_pair(parts, size):
    return tuple(exchange(part, PAIR, size) for part in parts)


class Order:
    def __init__(self):
        self.last = ()

    def after(self, *values):
        tied = lax.optimization_barrier(values + (self.last,))[: len(values)]
        self.last = tied
        return tied if len(values) > 1 else tied[0]

    def done(self, *values):
        values = lax.optimization_barrier(values + (self.last,))[: len(values)]
        self.last = values
        return values if len(values) > 1 else values[0]


def wait_for(value, *others):
    return lax.optimization_barrier((value,) + others)[0]


def rows_of(one, two):
    return jnp.concatenate([one, two], axis=0)


def block_order(bits):
    order = [0]
    for bit in reversed(bits):
        order = [item ^ bit for item in order] + order
    return order


def permuted_features(value, index, bits):
    order = block_order(bits)
    width = value.shape[1] // len(order)
    return jnp.concatenate(
        [lax.dynamic_slice_in_dim(value, (index ^ item) * width, width, 1) for item in order], axis=1
    )


def rows_and_cols(one, two):
    return jnp.concatenate([one, two], axis=1)


def exchange(value, bit, size):
    return lax.ppermute(value, "dp", [(i, i ^ bit) for i in range(size)])


class Reduction:
    def __init__(self, order, sent, kept, bits, size, assemble=None):
        self.order, self.sent, self.kept, self.assemble = order, sent, kept, assemble
        self.bits, self.size, self.step = bits, size, 0
        self.total = None

    def send(self, *others):
        sent = wait_for(self.sent, *others) if others else self.sent
        self.came = exchange(sent, self.bits[self.step], self.size)
        return self

    def receive(self):
        self.came = self.order.after(self.came)
        return self

    def add(self):
        kept, came = self.kept, self.came
        self.step += 1
        if self.step == len(self.bits):
            self.total = self.order.done((self.assemble or add_total)(kept, came))
        else:
            self.sent, self.kept = self.order.done(*add_halves(kept, came))
        return self

    def advance(self):
        self.receive().add()
        if self.total is None:
            self.send()

    def finish(self):
        while self.total is None:
            self.advance()
        return self.total


def added(one, two):
    return (one.astype(jnp.float32) + two.astype(jnp.float32)).astype(jnp.bfloat16)


def per_device(
    dp_size,
    layer_input,
    cotangent,
    starts,
    pieces,
    norm_attn,
    w_query,
    w_key,
    w_value,
    w_out,
    norm_mlp,
    w_gate,
    w_up,
    w_down,
):
    rows = layer_input.shape[0]
    width = layer_input.shape[1]
    place = lax.axis_index("tensor")
    index = lax.axis_index("dp")
    bits = [1 << i for i in range(dp_size.bit_length() - 1)]
    late_bits = bits[1:] + bits[:1]
    begins = starts[0]

    block_pos = jnp.stack([(place ^ m) * rows for m in range(4)]).astype(jnp.int32)
    near_pos, far_pos = block_pos[:2], block_pos[2:]
    row_pos = (block_pos[:, None] + jnp.arange(rows, dtype=jnp.int32)[None, :]).reshape(-1)
    (cos_n, sin_n), (cos_f, sin_f) = (
        rope_tables(half) for half in (row_pos[: 2 * rows], row_pos[2 * rows :])
    )
    w_kv = jnp.concatenate([w_key, w_value], axis=1)

    def in_sequence(value):
        return jnp.concatenate(
            [lax.dynamic_slice_in_dim(value, (place ^ b) * rows, rows, 0) for b in range(4)], axis=0
        )

    def in_two(value):
        return tuple(jnp.split(value, PARTS, axis=0))

    order = Order()
    near, far = slice(0, 2 * rows), slice(2 * rows, 4 * rows)

    def chip_sum(kept, came):
        came = order.after(came)
        return order.done(*by_rows(lambda a, b: (a + b,), (kept, came), (), ((jnp.bfloat16,),)))

    x_own, cot_own = in_two(layer_input), in_two(cotangent)
    x_chip, x_core = swap_chip(x_own), swap_core(x_own)

    side = index // PAIR % 2
    units, queries = w_gate.shape[1], w_query.shape[1]
    window = -(-units // 256) * 128
    overlap = 2 * window - units
    mine = (jnp.arange(window) >= overlap) | (side == 0)
    gate_half = lax.dynamic_slice_in_dim(w_gate, side * (units - window), window, 1)
    up_half = lax.dynamic_slice_in_dim(w_up, side * (units - window), window, 1)
    up_half = jnp.where(mine[None, :], up_half, 0).astype(jnp.bfloat16)
    down_half = lax.dynamic_slice_in_dim(w_down, side * (units - window), window, 0)
    down_half = jnp.where(mine[:, None], down_half, 0).astype(jnp.bfloat16)
    gate_half, up_half, down_half, w_kv, cos_n, sin_n, cos_f, sin_f = order.done(
        gate_half, up_half, down_half, w_kv, cos_n, sin_n, cos_f, sin_f
    )
    normed_n, q_n, k_n, v_n = order.done(
        *project((*x_own, *x_core), norm_attn, w_query, w_kv, cos_n, sin_n)
    )
    x_chip = order.after(x_chip)
    cot_own_ = wait_for(cot_own, x_chip)
    cot_chip, cot_core, cot_pair = (
        swap_chip(cot_own_), swap_core(cot_own_), swap_pair(cot_own_, dp_size)
    )
    normed_f, q_f, k_f, v_f = order.done(
        *project((*x_chip, *swap_core(x_chip)), norm_attn, w_query, w_kv, cos_f, sin_f)
    )
    k_low = in_sequence(rows_of(k_n, k_f))
    v_low = in_sequence(rows_of(v_n, v_f))
    attn_f, lse_f, kept, *sent = order.done(
        *attend_forward(q_f, k_low, v_low, w_out, begins, far_pos)
    )
    came = swap_core(sent)
    cot_chip, cot_pair = order.after(cot_chip, cot_pair)
    cot_diag, cot_other, cot_pcore = (
        swap_pair(cot_chip, dp_size), swap_core(cot_chip), swap_core(cot_pair)
    )
    attn_came = swap_chip(chip_sum(kept, came))
    cot_core, cot_other, cot_pcore, q_n = order.after(cot_core, cot_other, cot_pcore, q_n)
    attn_n, lse_n, kept, *sent = order.done(
        *attend_forward(q_n, k_low, v_low, w_out, begins, near_pos)
    )
    sum_came = swap_core(sent)

    def cot_back(*cots):
        return order.done(hidden_back(order.after(cots), down_half))

    near_back_hidden = cot_back(*cot_own, *cot_core)
    cot_diag = order.after(cot_diag)
    cot_dcore = swap_core(cot_diag)
    attn_came = order.after(attn_came)
    sum_came, cot_dcore = order.after(sum_came, cot_dcore)

    def norm_mid(x, kept, core, chip, gain):
        resid = x + (kept + core + chip)
        return resid, resid * rms_inverse(resid) * gain

    resid_mid, mlp_own = order.done(
        *by_rows(
            norm_mid, (x_own, kept, sum_came, attn_came), (norm_mlp,), (jnp.float32, (jnp.bfloat16,))
        )
    )
    mlp_core, mlp_chip, mlp_pair = swap_core(mlp_own), swap_chip(mlp_own), swap_pair(mlp_own, dp_size)
    mlp_core = order.after(mlp_core)

    def feed(normed, d_hidden):
        return order.done(*feed_forward(normed, d_hidden, gate_half, up_half))

    near_hidden = feed((*mlp_own, *mlp_core), near_back_hidden)
    side_back_hidden = cot_back(*cot_chip, *cot_other, *cot_pair, *cot_pcore)
    diag_back_hidden = cot_back(*cot_diag, *cot_dcore)
    mlp_chip, mlp_pair = order.after(mlp_chip, mlp_pair)
    half = rows // 2
    mlp_diag = (
        *swap_chip((mlp_pair[0][:half],)), *swap_pair((mlp_chip[0][half:],), dp_size)
    )
    mlp_other, mlp_pcore = order.after(swap_core(mlp_chip), swap_core(mlp_pair))
    side_hidden = feed((*mlp_chip, *mlp_other, *mlp_pair, *mlp_pcore), side_back_hidden)
    mlp_diag = order.after(mlp_diag)
    mlp_dcore = order.after(swap_core(mlp_diag))
    diag_hidden = feed((*mlp_diag, *mlp_dcore), diag_back_hidden)
    hiddens = (near_hidden, side_hidden, diag_hidden)

    def in_window(kept, came):
        first = jnp.where(side == 0, kept, came)
        second = jnp.where(side == 0, came, kept)
        return jnp.concatenate([first, second[:, overlap:]], axis=1).astype(jnp.float32)

    pair_bits = [bit for bit in bits if bit != PAIR] + [PAIR]
    always = begins[0] >= 0

    def fence(step):
        def inside():
            outer_last, order.last = order.last, ()
            try:
                return step()
            finally:
                order.last = outer_last

        shapes = jax.eval_shape(inside)
        taken = order.after(always)
        results = lax.cond(
            taken,
            inside,
            lambda: jax.tree.map(lambda item: jnp.zeros(item.shape, item.dtype), shapes),
        )
        leaves, tree = jax.tree.flatten(results)
        return jax.tree.unflatten(tree, order.done(tuple(leaves)))

    def gradient(sections, order_bits, pieces=(slice(None),)):
        lefts, rights = order.after([item[0] for item in sections], [item[1] for item in sections])
        return order.done(*outer(list(zip(lefts, rights)), index, order_bits, pieces))

    cots = (
        (*cot_own, *cot_core),
        (*cot_chip, *cot_other, *cot_pair, *cot_pcore),
        (*cot_diag, *cot_dcore),
    )
    mlps = (
        (*mlp_own, *mlp_core),
        (*mlp_chip, *mlp_other, *mlp_pair, *mlp_pcore),
        (*mlp_diag, *mlp_dcore),
    )

    def mlp_gradients(lefts, which):
        sections = [(left, [right[i] for i in which]) for left, right in zip(lefts, hiddens)]
        return gradient(sections, pair_bits, [slice(i, i + 1) for i in range(len(which))])

    def reduction(sent_kept, order_bits, assemble=None):
        return Reduction(order, *sent_kept, order_bits, dp_size, assemble)

    def shares(lefts, rights, transposed=True):
        parts = order.done(*row_shares(order.after(lefts), rights, transposed, rows))
        return [(parts[i], swap_core((parts[i + 1],))) for i in range(0, len(parts), 2)]

    def total(*items):
        return order.done(*by_rows(lambda *values: (sum(values),), items, (), ((jnp.bfloat16,),)))

    class GroupSum:
        def __init__(self, which, rights, transposed):
            self.rest = rights, transposed
            self.near, self.sides, self.diag = (tuple(item[i] for i in which) for item in hiddens)

        def diag_shares(self):
            return shares(self.diag, *self.rest)[0]

        def side_shares(self):
            return shares(self.sides, *self.rest)

        def own_shares(self):
            return shares(self.near, *self.rest)[0]

    d_norm = GroupSum((1, 2), (gate_half, up_half), True)
    block_sum = GroupSum((0,), (down_half,), False)

    down = reduction(mlp_gradients(cots, (0,)), pair_bits, in_window)
    down.send()

    @fence
    def diag_and_gradients():
        kept, came = d_norm.diag_shares()
        made = mlp_gradients(mlps, (1, 2))
        return chip_sum(kept, came), made

    diag, made = diag_and_gradients
    to_pair = swap_pair(diag, dp_size)
    gate, up = (reduction(item, pair_bits, in_window) for item in (made[:2], made[2:]))

    @fence
    def other_shares():
        chip, pair = d_norm.side_shares()
        own = d_norm.own_shares()
        return order.after(chip), order.after(pair), order.after(own)

    chip, pair, own = other_shares
    came_p = swap_pair(total(pair[0], *pair[1]), dp_size)
    to_pair = order.after(to_pair)
    came_c = swap_chip(total(chip[0], *chip[1], to_pair))
    down.receive()
    gate.send(down.came)
    down.add()
    down.send()

    @fence
    def block_shares():
        def parts(lefts):
            return order.done(*row_shares(order.after(lefts), *block_sum.rest, rows))

        kept, sent = parts(block_sum.diag)
        came = swap_core((sent,))
        kept_c, sent_c, kept_p, sent_p = parts(block_sum.sides)
        diag = chip_sum(kept, came)
        came_c = swap_core((order.after(sent_c),))
        kept, sent = parts(block_sum.near)
        came_c = order.after(came_c)
        came_p = order.after(swap_core((order.after(sent_p),)))
        came = order.after(swap_core((order.after(sent),)))
        return diag, (kept_c, came_c), (kept_p, came_p), (kept, came)

    block_diag, block_chip, block_pair, block_own = block_shares
    came_c, came_p = order.after(came_c, came_p)
    to_pair = swap_pair(block_diag, dp_size)

    def back_mid(kept, core, chip, pair, resid, cot, gain):
        d_mid = cot + norm_back(kept + core + chip + pair, resid, rms_inverse(resid), gain)
        return d_mid, d_mid

    d_mid, d_own = order.done(
        *by_rows(
            back_mid,
            (own[0], own[1], came_c, came_p, resid_mid, cot_own),
            (norm_mlp,),
            (jnp.float32, (jnp.bfloat16,)),
        )
    )
    d_chip = swap_chip(d_own)

    gate.receive()
    up.send(gate.came)
    gate.add()

    @fence
    def near_back():
        d_core = order.after(swap_core(d_own))
        return d_core, order.done(
            *attend_backward(
                q_n, (*d_own, *d_core), w_out, attn_n, lse_n, k_low, v_low, cos_n,
                sin_n, begins, near_pos,
            )
        )

    d_core, (dq_n, dk_n, dv_n) = near_back
    d_chip = order.after(d_chip)
    @fence
    def out_gradient():
        d_other = order.after(swap_core(d_chip))
        sections = [((*d_own, *d_core), (attn_n,)), ((*d_chip, *d_other), (attn_f,))]
        return d_other, gradient(sections, bits)

    d_other, wout = out_gradient
    wout = reduction(wout, bits)
    down.receive()
    gate.send(down.came)
    down.add().send()
    up.receive()
    wout.send(up.came)
    up.add()
    to_pair = order.after(to_pair)
    block_c = total(block_chip[0], *block_chip[1], to_pair)
    block_p = total(block_pair[0], *block_pair[1])

    @fence
    def far_back():
        return order.done(
            *attend_backward(
                q_f, (*d_chip, *d_other), w_out, attn_f, lse_f, k_low, v_low, cos_f,
                sin_f, begins, far_pos,
            )
        )

    dq_f, dk_f, dv_f = far_back

    @fence
    def query_gradient():
        dkv_n, dkv_f = order.done(
            *key_value_rows(dk_n, dk_f, dv_n, dv_f, (cos_n, sin_n, cos_f, sin_f), block_pos)
        )
        sections = [((normed_n,), (dq_n, dkv_n)), ((normed_f,), (dq_f, dkv_f))]
        return dkv_n, dkv_f, gradient(sections, bits)

    dkv_n, dkv_f, qkv = query_gradient
    qkv = reduction(qkv, bits)
    qkv.send()
    wout.receive()
    wout.add().send()
    down.receive().add()
    gate.receive()
    up.send(gate.came)
    gate.add().send()
    in_sum = fence(lambda: chip_sum(*shares((dq_f, dkv_f), (w_query, w_kv))[0]))
    gate.receive().add()
    d_in_came = swap_chip(in_sum)
    own = fence(lambda: order.after(shares((dq_n, dkv_n), (w_query, w_kv))[0]))
    qkv.receive()
    qkv.add().send()
    wout.receive()
    up.receive()
    up.add().send()
    wout.add().send()
    d_in_came = order.after(d_in_came)

    def back_in(kept, core, chip, resid, d_mid, gain):
        return (d_mid + norm_back(kept + core + chip, resid, rms_inverse(resid), gain),)

    (x_grad,) = by_rows(
        back_in, (own[0], own[1], d_in_came, x_own, d_mid), (norm_attn,), (jnp.float32,)
    )
    x_grad = order.done(x_grad)
    qkv.receive()
    block_p = swap_pair(wait_for(block_p, qkv.came), dp_size)
    block_c = swap_chip(wait_for(block_c, qkv.came))
    qkv.add().send()
    up.receive().add()
    wout.receive().add()
    block_c, block_p = order.after(block_c, block_p)
    qkv.receive().add()
    (block_out,) = by_rows(
        lambda *items: (sum(items),),
        (resid_mid, block_own[0], block_own[1], block_c, block_p),
        (),
        (jnp.bfloat16,),
    )
    block_out = order.done(block_out)
    for item in (down, gate, up, wout, qkv):
        item.finish()
    grad_down, grad_gate, grad_up = down.total.T, gate.total, up.total
    grad_out, grad_qkv = wout.total.T, qkv.total
    queries = w_query.shape[1]
    grad_query = grad_qkv[:, :queries]
    grad_key = grad_qkv[:, queries : queries + HD]
    grad_value = grad_qkv[:, queries + HD :]

    share = width // dp_size

    def own_features(value):
        return lax.dynamic_slice_in_dim(value, index * share, share, 0).astype(jnp.float32)

    gain_attn = (
        jnp.sum(own_features(w_query) * grad_query, axis=1)
        + jnp.sum(own_features(w_kv) * grad_qkv[:, queries:], axis=1)
    ) / own_features(norm_attn)
    gain_mlp = jnp.sum(
        own_features(w_gate) * grad_gate + own_features(w_up) * grad_up, axis=1
    ) / own_features(norm_mlp)
    gains = jnp.stack([gain_attn, gain_mlp]).reshape(2, 4, share // 4)
    gains = jnp.stack([lax.dynamic_index_in_dim(gains, place ^ m, 1, False) for m in range(4)])
    came = lax.ppermute(gains[2:], "tensor", [(i, i ^ 2) for i in range(4)])
    gains = gains[:2] + wait_for(came, block_out)
    gains = gains[0] + lax.ppermute(gains[1], "tensor", [(i, i ^ 1) for i in range(4)])

    return (
        block_out,
        x_grad,
        gains[0],
        grad_query,
        grad_key,
        grad_value,
        grad_out,
        gains[1],
        grad_gate,
        grad_up,
        grad_down,
    )


def solution(mesh):
    in_specs = (
        P(("dp", "tensor"), None),
        P(("dp", "tensor"), None),
        P("dp", None),
        P("dp"),
        P(),
        P(None, "tensor"),
        P(None, "tensor"),
        P(None, "tensor"),
        P("tensor", None),
        P(),
        P(None, "tensor"),
        P(None, "tensor"),
        P("tensor", None),
    )
    out_specs = (
        P(("dp", "tensor"), None),
        P(("dp", "tensor"), None),
        P(("dp", "tensor")),
        P("dp", "tensor"),
        P("dp", "tensor"),
        P("dp", "tensor"),
        P("tensor", "dp"),
        P(("dp", "tensor")),
        P("dp", "tensor"),
        P("dp", "tensor"),
        P("tensor", "dp"),
    )
    return jax.shard_map(
        functools.partial(per_device, mesh.shape["dp"]),
        mesh=mesh,
        in_specs=in_specs,
        out_specs=out_specs,
        check_vma=False,
    )
```

```python
import functools

import jax
import jax.numpy as jnp
from jax import lax
from jax.experimental import pallas as pl
from jax.experimental.pallas import tpu as pltpu
from jax.sharding import PartitionSpec as P

HD = 64
SEQ = 1024
PIECE = 256
QB = 256


EPSILON = 1e-05
ROPE_BASE = 10000.0
MASKED = -1e30
VMEM_LIMIT = 48 * 2**20
PARTS = 1
OUTER_BLOCKS = 2
PAIR = 2
NT = (((1,), (1,)), ((), ()))
TN = (((0,), (0,)), ((), ()))


def dot(left, right):
    return jnp.dot(left, right, preferred_element_type=jnp.float32)


def contract_rows(left, right):
    return lax.dot_general(left, right, TN, preferred_element_type=jnp.float32)


def contract_cols(left, right):
    return lax.dot_general(left, right, NT, preferred_element_type=jnp.float32)


def rms_inverse(resid):
    return lax.rsqrt(jnp.mean(resid * resid, axis=-1, keepdims=True) + EPSILON)


def norm_back(d_norm, resid, inverse, gain):
    scaled = d_norm * gain
    return inverse * scaled - resid * (inverse * inverse * inverse) * jnp.mean(
        scaled * resid, axis=-1, keepdims=True
    )


def rope_tables(positions):
    half_dim = HD // 2
    inverse = jnp.power(ROPE_BASE, -(jnp.arange(half_dim).astype(jnp.float32) * 2.0) / HD)
    angles = positions.astype(jnp.float32)[:, None] * inverse[None, :]
    cos, sin = jnp.cos(angles), jnp.sin(angles)
    return jnp.concatenate([cos] * 4, axis=1), jnp.concatenate([-sin, sin] * 2, axis=1)


def swap_halves(pair):
    lane = lax.broadcasted_iota(jnp.int32, pair.shape, 1)
    up = pltpu.roll(pair, 2 * HD - HD // 2, 1)
    down = pltpu.roll(pair, HD // 2, 1)
    return jnp.where(lane % HD < HD // 2, up, down)


def rotate_rows(grad, cos_tab, sin_tab):
    half = HD // 2
    swapped = jnp.concatenate([grad[:, half:], grad[:, :half]], axis=1)
    return grad * cos_tab[:, :HD] - swapped * sin_tab[:, :HD]


def either(near_refs):
    half = len(near_refs) // 2
    own, core = (
        jnp.concatenate([ref[...] for ref in refs], axis=0)
        for refs in (near_refs[:half], near_refs[half:])
    )
    return jnp.where(pl.program_id(0) == 0, own, core)


def project_kernel(*refs):
    x_refs = refs[:-9]
    gain_ref, wq_ref, wkv_ref, cos_ref, sin_ref, n_ref, q_ref, k_ref, v_ref = refs[-9:]
    resid = either(x_refs).astype(jnp.float32)
    normed = (resid * rms_inverse(resid) * gain_ref[...]).astype(jnp.bfloat16)
    n_ref[...] = normed
    cos, sin = cos_ref[...], sin_ref[...]
    query = dot(normed, wq_ref[...])
    for first in range(0, query.shape[1], 2 * HD):
        pair = query[:, first : first + 2 * HD]
        turned = (pair * cos + swap_halves(pair) * sin) * HD ** (-0.5)
        q_ref[:, first : first + 2 * HD] = turned.astype(jnp.bfloat16)
    key_value = dot(normed, wkv_ref[...])
    turned = key_value * cos + swap_halves(key_value) * sin
    k_ref[...] = turned[:, :HD].astype(jnp.bfloat16)
    v_ref[...] = key_value[:, HD:].astype(jnp.bfloat16)


def whole(array):
    return pl.BlockSpec(array.shape, lambda *_: (0,) * len(array.shape))


def params():
    return {
        "compiler_params": pltpu.CompilerParams(vmem_limit_bytes=VMEM_LIMIT),
        "cost_estimate": pl.CostEstimate(flops=1, bytes_accessed=1, transcendentals=0),
    }


def project(parts, gain, w_query, w_kv, cos_tab, sin_tab):
    rows, width = sum(part.shape[0] for part in parts) // 2, parts[0].shape[1]
    queries = w_query.shape[1]

    def tall(cols):
        return pl.BlockSpec((rows, cols), lambda i: (i, 0))

    gain = gain[None, :]
    return pl.pallas_call(
        project_kernel,
        grid=(2,),
        in_specs=[
            *(whole(item) for item in (*parts, gain, w_query, w_kv)), tall(2 * HD), tall(2 * HD)
        ],
        out_specs=[tall(width), tall(queries), tall(HD), tall(HD)],
        out_shape=[
            jax.ShapeDtypeStruct((2 * rows, width), jnp.bfloat16),
            jax.ShapeDtypeStruct((2 * rows, queries), jnp.bfloat16),
            jax.ShapeDtypeStruct((2 * rows, HD), jnp.bfloat16),
            jax.ShapeDtypeStruct((2 * rows, HD), jnp.bfloat16),
        ],
        name="project",
        **params(),
    )(*parts, gain, w_query, w_kv, cos_tab, sin_tab)


def by_rows(function, ins, consts, outs):
    flat = [item[0] if isinstance(item, tuple) else item for item in ins]
    dtypes = [item[0] if isinstance(item, tuple) else item for item in outs]
    consts = [item[None, :] for item in consts]
    rows, width = flat[0].shape
    block, step = rows // 2, 32

    def kernel(*refs):
        given = [ref[...] for ref in refs[len(flat) : len(flat) + len(consts)]]
        targets = refs[len(flat) + len(consts) :]

        def chunk(i, _):
            at = pl.ds(pl.multiple_of(i * step, step), step)
            values = [ref[at, :].astype(jnp.float32) for ref in refs[: len(flat)]]
            for ref, value in zip(targets, function(*values, *given)):
                ref[at, :] = value.astype(ref.dtype)
            return 0

        lax.fori_loop(0, block // step, chunk, 0)

    tall = pl.BlockSpec((block, width), lambda i: (i, 0))
    results = pl.pallas_call(
        kernel,
        grid=(2,),
        in_specs=[tall] * len(flat) + [whole(item) for item in consts],
        out_specs=[tall] * len(dtypes),
        out_shape=[jax.ShapeDtypeStruct((rows, width), dtype) for dtype in dtypes],
        name="by_rows",
        **params(),
    )(*flat, *consts)
    return [
        (result,) if isinstance(item, tuple) else result for result, item in zip(results, outs)
    ]


def see(qpos, kpos, starts_ref, pics):
    mask = kpos <= qpos
    for pic in range(pics):
        begin = starts_ref[pic]
        mask = mask | (
            (qpos >= begin) & (qpos < begin + PIECE) & (kpos >= begin) & (kpos < begin + PIECE)
        )
    return mask


def key_blocks(starts_ref, pics, first):
    edge = first + QB
    crossed = jnp.bool_(False)
    for pic in range(pics):
        begin = starts_ref[pic]
        crossed = crossed | ((begin < edge) & (begin + PIECE > edge))
    return edge // QB + jnp.where(crossed, 1, 0)


def forward_kernel(
    pos_ref, starts_ref, q_ref, k_ref, v_ref, out_ref, o_ref, lse_ref, kept_ref, *rest, heads, pics, seq
):
    *sent_refs, bias = rest
    first = pos_ref[pl.program_id(0)]
    count = key_blocks(starts_ref, pics, first)
    for blocks in range(1, seq // QB + 1):

        @pl.when(count == blocks)
        def _():
            ext = blocks * QB
            low = max(0, ext - 2 * QB)
            wide = ext - low
            qpos = lax.broadcasted_iota(jnp.int32, (QB, wide), 0) + first
            kpos = lax.broadcasted_iota(jnp.int32, (QB, wide), 1) + low
            bias[:, :wide] = jnp.where(see(qpos, kpos, starts_ref, pics), 0.0, MASKED)
            values = jnp.concatenate([v_ref[:ext, :], jnp.ones((ext, HD), jnp.bfloat16)], axis=1)
            lane = lax.broadcasted_iota(jnp.int32, (QB, heads), 1)

            def one_pair(pair, stats):
                at = pl.ds(pl.multiple_of(pair * 2 * HD, 2 * HD), 2 * HD)
                both = q_ref[:, at]
                outs = []
                for side in range(2):
                    scores = contract_cols(both[:, side * HD : (side + 1) * HD], k_ref[:ext, :])
                    if low:
                        scores = jnp.concatenate(
                            [scores[:, :low], scores[:, low:] + bias[:, :wide]], axis=1
                        )
                    else:
                        scores = scores + bias[:, :wide]
                    row_max = jnp.max(scores, axis=1, keepdims=True)
                    terms = jnp.exp(scores - row_max).astype(jnp.bfloat16)
                    summed = dot(terms, values)
                    row_sum = summed[:, HD : HD + 1]
                    outs.append(summed[:, :HD] / row_sum)
                    stats = jnp.where(lane == 2 * pair + side, row_max + jnp.log(row_sum), stats)
                o_ref[:, at] = jnp.concatenate(outs, axis=1).astype(jnp.bfloat16)
                return stats

            lse_ref[...] = lax.fori_loop(
                0, heads // 2, one_pair, jnp.zeros((QB, heads), jnp.float32), unroll=4
            )

    part = dot(o_ref[...], out_ref[...]).astype(jnp.bfloat16)

    @pl.when(pl.program_id(0) == 0)
    def _():
        kept_ref[...] = part

    @pl.when(pl.program_id(0) == 1)
    def _():
        for i, ref in enumerate(sent_refs):
            ref[...] = part[i * ref.shape[0] : (i + 1) * ref.shape[0]]


def attend_forward(q_low, k_low, v_low, w_out, starts, positions):
    rows, width = q_low.shape
    heads, seq, pics = width // HD, k_low.shape[0], starts.shape[0]
    tall = pl.BlockSpec((QB, width), lambda i, *_: (i, 0))
    parts = [(QB, w_out.shape[1])] + [(QB // PARTS, w_out.shape[1])] * PARTS
    keys = pl.BlockSpec((seq, HD), lambda i, *_: (0, 0))
    return pl.pallas_call(
        functools.partial(forward_kernel, heads=heads, pics=pics, seq=seq),
        grid_spec=pltpu.PrefetchScalarGridSpec(
            num_scalar_prefetch=2,
            grid=(rows // QB,),
            in_specs=[tall, keys, keys, whole(w_out)],
            out_specs=[
                tall,
                pl.BlockSpec((QB, heads), lambda i, *_: (i, 0)),
                *(pl.BlockSpec(part, lambda i, *_: (0, 0)) for part in parts),
            ],
            scratch_shapes=[pltpu.VMEM((QB, 2 * QB), jnp.float32)],
        ),
        out_shape=[
            jax.ShapeDtypeStruct((rows, width), jnp.bfloat16),
            jax.ShapeDtypeStruct((rows, heads), jnp.float32),
            *(jax.ShapeDtypeStruct(part, jnp.bfloat16) for part in parts),
        ],
        name="attend_forward",
        **params(),
    )(positions, starts, q_low, k_low, v_low, w_out)


def in_three(value):
    top = value.astype(jnp.bfloat16)
    rest = value - top.astype(jnp.float32)
    middle = rest.astype(jnp.bfloat16)
    last = (rest - middle.astype(jnp.float32)).astype(jnp.bfloat16)
    return [top, middle, last]


def backward_kernel(
    pos_ref, starts_ref, q_ref, out_ref, o_ref, lse_ref, k_ref, v_ref, cos_ref, sin_ref,
    *rest, heads, pics, seq
):
    *d_refs, dq_ref, dk_ref, dv_ref, bias, do_ref = rest
    first = pos_ref[pl.program_id(0)]
    count = key_blocks(starts_ref, pics, first)

    @pl.when(pl.program_id(0) == 0)
    def _():
        dk_ref[...] = jnp.zeros_like(dk_ref)
        dv_ref[...] = jnp.zeros_like(dv_ref)

    do_ref[...] = contract_cols(either(d_refs), out_ref[...]).astype(jnp.bfloat16)

    for blocks in range(1, seq // QB + 1):

        @pl.when(count == blocks)
        def _():
            ext = blocks * QB
            low = max(0, ext - 2 * QB)
            wide = ext - low
            kpos = lax.broadcasted_iota(jnp.int32, (wide, QB), 0) + low
            qpos = lax.broadcasted_iota(jnp.int32, (wide, QB), 1) + first
            bias[:wide, :] = jnp.where(see(qpos, kpos, starts_ref, pics), 0.0, MASKED)
            ones = jnp.ones((ext, HD), jnp.bfloat16)
            keys = jnp.concatenate([k_ref[:ext, :], ones], axis=1)
            values = jnp.concatenate([v_ref[:ext, :], ones], axis=1)
            zeros = jnp.zeros((QB, HD - 3), jnp.bfloat16)
            lane = lax.broadcasted_iota(jnp.int32, (QB, heads), 1)

            def one_pair(pair, _):
                at = pl.ds(pl.multiple_of(pair * 2 * HD, 2 * HD), 2 * HD)
                q_both, d_both, o_both = q_ref[:, at], do_ref[:, at], o_ref[:, at]
                stats = lse_ref[...]
                d_query, d_key, d_val = [], 0.0, 0.0
                for side in range(2):
                    cols = slice(side * HD, (side + 1) * HD)
                    queries, d_out = q_both[:, cols], d_both[:, cols]
                    delta = jnp.sum(
                        d_out.astype(jnp.float32) * o_both[:, cols].astype(jnp.float32),
                        axis=1,
                        keepdims=True,
                    )
                    lse = jnp.sum(
                        jnp.where(lane == 2 * pair + side, stats, 0.0), axis=1, keepdims=True
                    )
                    queries_ext = jnp.concatenate([queries] + in_three(-lse) + [zeros], axis=1)
                    d_out_ext = jnp.concatenate([d_out] + in_three(-delta) + [zeros], axis=1)
                    scores = contract_cols(keys, queries_ext)
                    if low:
                        scores = jnp.concatenate(
                            [scores[:low], scores[low:] + bias[:wide, :]], axis=0
                        )
                    else:
                        scores = scores + bias[:wide, :]
                    probs = jnp.exp(scores)
                    d_probs = contract_cols(values, d_out_ext)
                    d_scores = (probs * d_probs).astype(jnp.bfloat16)
                    d_val += dot(probs.astype(jnp.bfloat16), d_out)
                    d_key += dot(d_scores, queries)
                    d_query.append(contract_rows(d_scores, k_ref[:ext, :]))
                dk_ref[:ext, :] += d_key
                dv_ref[:ext, :] += d_val
                turned = jnp.concatenate(d_query, axis=1) * HD ** (-0.5)
                turned = turned * cos_ref[...] - swap_halves(turned) * sin_ref[...]
                dq_ref[:, at] = turned.astype(jnp.bfloat16)
                return 0

            lax.fori_loop(0, heads // 2, one_pair, 0, unroll=2)


def attend_backward(
    q_low, d_parts, w_out, attn_low, lse, k_low, v_low, cos_tab, sin_tab, starts, positions
):
    rows, width = q_low.shape
    heads, seq, pics = width // HD, k_low.shape[0], starts.shape[0]
    tall = pl.BlockSpec((QB, width), lambda i, *_: (i, 0))
    table = pl.BlockSpec((QB, 2 * HD), lambda i, *_: (i, 0))
    stats = pl.BlockSpec((QB, heads), lambda i, *_: (i, 0))
    keys = whole(k_low)
    return pl.pallas_call(
        functools.partial(backward_kernel, heads=heads, pics=pics, seq=seq),
        grid_spec=pltpu.PrefetchScalarGridSpec(
            num_scalar_prefetch=2,
            grid=(rows // QB,),
            in_specs=[
                tall, whole(w_out), tall, stats, keys, keys, table, table,
                *(whole(part) for part in d_parts),
            ],
            out_specs=[tall, keys, keys],
            scratch_shapes=[
                pltpu.VMEM((2 * QB, QB), jnp.float32),
                pltpu.VMEM((QB, width), jnp.bfloat16),
            ],
        ),
        out_shape=[
            jax.ShapeDtypeStruct((rows, width), jnp.bfloat16),
            jax.ShapeDtypeStruct((seq, HD), jnp.float32),
            jax.ShapeDtypeStruct((seq, HD), jnp.float32),
        ],
        name="attend_backward",
        **params(),
    )(
        positions, starts, q_low, w_out, attn_low, lse, k_low, v_low, cos_tab, sin_tab, *d_parts
    )


def hidden_kernel(*refs):
    *parts, down_ref, out_ref, cots = refs

    @pl.when(pl.program_id(0) == 0)
    def _():
        at = 0
        for ref in parts:
            cots[at : at + ref.shape[0], :] = ref[...]
            at += ref.shape[0]

    out_ref[...] = contract_cols(cots[...], down_ref[...]).astype(jnp.bfloat16)


def hidden_back(cots, w_down):
    rows, width = sum(item.shape[0] for item in cots), cots[0].shape[1]
    units, tile = w_down.shape[0], 256
    return pl.pallas_call(
        hidden_kernel,
        grid=(pl.cdiv(units, tile),),
        in_specs=[
            *(whole(item) for item in cots), pl.BlockSpec((tile, width), lambda j: (j, 0))
        ],
        out_specs=pl.BlockSpec((rows, tile), lambda j: (0, j)),
        out_shape=jax.ShapeDtypeStruct((rows, units), jnp.bfloat16),
        scratch_shapes=[pltpu.VMEM((rows, width), jnp.bfloat16)],
        name="hidden_back",
        **params(),
    )(*cots, w_down)


def feed_kernel(*refs):
    *parts, d_hidden_ref, gate_ref, up_ref, hidden_ref, d_gate_ref, d_up_ref, normed = refs

    @pl.when(pl.program_id(0) == 0)
    def _():
        at = 0
        for ref in parts:
            normed[at : at + ref.shape[0], :] = ref[...]
            at += ref.shape[0]

    gate_val, up_val = dot(normed[...], gate_ref[...]), dot(normed[...], up_ref[...])
    d_hidden = d_hidden_ref[...].astype(jnp.float32)
    gate_sig = jax.nn.sigmoid(gate_val)
    swish = gate_val * gate_sig
    hidden_ref[...] = (swish * up_val).astype(jnp.bfloat16)
    d_gate = d_hidden * up_val * (gate_sig + swish * (1.0 - gate_sig))
    d_gate_ref[...] = d_gate.astype(jnp.bfloat16)
    d_up_ref[...] = (d_hidden * swish).astype(jnp.bfloat16)


def feed_forward(normed, d_hidden, w_gate, w_up):
    rows, width = sum(item.shape[0] for item in normed), normed[0].shape[1]
    units, tile = w_gate.shape[1], 256
    cols = pl.BlockSpec((width, tile), lambda j: (0, j))
    out = pl.BlockSpec((rows, tile), lambda j: (0, j))
    return pl.pallas_call(
        feed_kernel,
        grid=(pl.cdiv(units, tile),),
        in_specs=[*(whole(item) for item in normed), out, cols, cols],
        out_specs=[out] * 3,
        out_shape=[jax.ShapeDtypeStruct((rows, units), jnp.bfloat16)] * 3,
        scratch_shapes=[pltpu.VMEM((rows, width), jnp.bfloat16)],
        name="feed_forward",
        **params(),
    )(*normed, d_hidden, w_gate, w_up)


def share_kernel(*refs, count, transposed):
    outs = refs[2 * count :]
    multiply = contract_cols if transposed else dot
    part = multiply(refs[0][...], refs[count][...])
    for left, right in zip(refs[1:count], refs[count + 1 : 2 * count]):
        part = part + multiply(left[...], right[...])
    rows = outs[0].shape[0]
    for place, ref in enumerate(outs):
        ref[...] = part[place * rows : (place + 1) * rows].astype(jnp.bfloat16)


def row_shares(lefts, rights, transposed, rows):
    blocks = lefts[0].shape[0] // rows
    width, tile = rights[0].shape[0 if transposed else 1], 512

    def right_spec(item):
        if transposed:
            return pl.BlockSpec((tile, item.shape[1]), lambda j: (j, 0))
        return pl.BlockSpec((item.shape[0], tile), lambda j: (0, j))

    return pl.pallas_call(
        functools.partial(share_kernel, count=len(lefts), transposed=transposed),
        grid=(width // tile,),
        in_specs=[*(whole(item) for item in lefts), *(right_spec(item) for item in rights)],
        out_specs=[pl.BlockSpec((rows, tile), lambda j: (0, j))] * blocks,
        out_shape=[jax.ShapeDtypeStruct((rows, width), jnp.bfloat16)] * blocks,
        name="row_shares",
        **params(),
    )(*lefts, *rights)


def outer_kernel(order_ref, *refs, shape, pieces):
    outs, refs = refs[-2 * len(pieces) :], list(refs[: -2 * len(pieces)])
    totals = None
    for lefts, rights in shape:
        rows = jnp.concatenate(
            [
                jnp.concatenate([refs.pop(0)[...] for _ in range(OUTER_BLOCKS)], axis=1)
                for _ in range(lefts)
            ],
            axis=0,
        )
        parts = [contract_rows(rows, refs.pop(0)[...]) for _ in range(rights)]
        totals = parts if totals is None else [a + b for a, b in zip(totals, parts)]
    step = pl.program_id(0)
    half = pl.num_programs(0) // 2
    for place, piece in enumerate(pieces):
        total = jnp.concatenate(totals[piece], axis=1).astype(jnp.bfloat16)

        @pl.when(step < half)
        def _():
            outs[2 * place][...] = total

        @pl.when(step >= half)
        def _():
            outs[2 * place + 1][...] = total


def outer(sections, index, bits, pieces):
    width = sections[0][0][0].shape[1]
    share = width // (1 << len(bits))
    tile = 256
    if share == tile:
        blocks = jnp.stack([index ^ item for item in block_order(bits)]).astype(jnp.int32)
    else:
        blocks = jnp.arange(width // tile, dtype=jnp.int32)
        sections = [
            ([permuted_features(item, index, bits) for item in lefts], rights)
            for lefts, rights in sections
        ]
    count = width // tile // OUTER_BLOCKS
    sizes = [sum(item.shape[1] for item in sections[0][1][piece]) for piece in pieces]
    specs, arrays = [], []
    for lefts, rights in sections:
        for item in lefts:
            for i in range(OUTER_BLOCKS):
                specs.append(
                    pl.BlockSpec(
                        (item.shape[0], tile), lambda j, b, i=i: (0, b[j * OUTER_BLOCKS + i])
                    )
                )
                arrays.append(item)
        specs.extend(whole(item) for item in rights)
        arrays.extend(rights)
    return pl.pallas_call(
        functools.partial(
            outer_kernel,
            shape=[(len(lefts), len(rights)) for lefts, rights in sections],
            pieces=pieces,
        ),
        grid_spec=pltpu.PrefetchScalarGridSpec(
            num_scalar_prefetch=1,
            grid=(count,),
            in_specs=specs,
            out_specs=[
                pl.BlockSpec((tile * OUTER_BLOCKS, size), at)
                for size in sizes
                for at in (
                    lambda j, _: (jnp.minimum(j, count // 2 - 1), 0),
                    lambda j, _: (jnp.maximum(j - count // 2, 0), 0),
                )
            ],
        ),
        out_shape=[
            jax.ShapeDtypeStruct((width // 2, size), jnp.bfloat16) for size in sizes for _ in range(2)
        ],
        name="outer",
        **params(),
    )(blocks, *arrays)


def halves_kernel(kept_a, kept_b, came_a, came_b, sent_ref, kept_ref):
    sent_ref[...] = added(kept_a[...], came_a[...])
    kept_ref[...] = added(kept_b[...], came_b[...])


def add_halves(kept, came):
    half, columns = kept.shape[0] // 2, kept.shape[1]
    block = min(256, half)
    first = pl.BlockSpec((block, columns), lambda i: (i, 0))
    second = pl.BlockSpec((block, columns), lambda i: (i + half // block, 0))
    return pl.pallas_call(
        halves_kernel,
        grid=(half // block,),
        in_specs=[first, second, first, second],
        out_specs=[first, first],
        out_shape=[jax.ShapeDtypeStruct((half, columns), jnp.bfloat16)] * 2,
        name="add_halves",
        **params(),
    )(kept, kept, came, came)


def total_kernel(kept_ref, came_ref, out_ref):
    out_ref[...] = kept_ref[...].astype(jnp.float32) + came_ref[...].astype(jnp.float32)


def add_total(kept, came):
    return pl.pallas_call(
        total_kernel,
        out_shape=jax.ShapeDtypeStruct(kept.shape, jnp.float32),
        name="add_total",
        **params(),
    )(kept, came)


def key_value_kernel(
    at_ref, dkn_ref, dkf_ref, dvn_ref, dvf_ref, cosn_ref, sinn_ref, cosf_ref, sinf_ref, near_ref, far_ref
):
    rows = dkn_ref.shape[0] // 4
    for m in range(4):
        at = pl.ds(pl.multiple_of(at_ref[m], rows), rows)
        mine = slice(m % 2 * rows, (m % 2 + 1) * rows)
        cos_ref, sin_ref = (cosn_ref, sinn_ref) if m < 2 else (cosf_ref, sinf_ref)
        d_key = dkn_ref[at, :] + dkf_ref[at, :]
        d_val = dvn_ref[at, :] + dvf_ref[at, :]
        both = jnp.concatenate([d_key, d_val], axis=1)
        turned = both * cos_ref[mine, :] - swap_halves(both) * sin_ref[mine, :]
        both = jnp.concatenate([turned[:, :HD], d_val], axis=1).astype(jnp.bfloat16)
        target = near_ref if m < 2 else far_ref
        target[mine, :] = both


def key_value_rows(dk_n, dk_f, dv_n, dv_f, tables, block_pos):
    shape = jax.ShapeDtypeStruct((dk_n.shape[0] // 2, 2 * HD), jnp.bfloat16)
    arrays = (dk_n, dk_f, dv_n, dv_f, *tables)
    return pl.pallas_call(
        key_value_kernel,
        grid_spec=pltpu.PrefetchScalarGridSpec(
            num_scalar_prefetch=1,
            grid=(1,),
            in_specs=[whole(item) for item in arrays],
            out_specs=[whole(shape), whole(shape)],
        ),
        out_shape=[shape, shape],
        name="key_value_rows",
        **params(),
    )(block_pos, *arrays)


def swapped(parts, flip):
    pairs = [(i, i ^ flip) for i in range(4)]
    return tuple(lax.ppermute(part, "tensor", pairs) for part in parts)


def swap_core(parts):
    return swapped(parts, 1)


def swap_chip(parts):
    return swapped(parts, 2)


def swap_pair(parts, size):
    return tuple(exchange(part, PAIR, size) for part in parts)


class Order:
    def __init__(self):
        self.last = ()

    def after(self, *values):
        tied = lax.optimization_barrier(values + (self.last,))[: len(values)]
        self.last = tied
        return tied if len(values) > 1 else tied[0]

    def done(self, *values):
        values = lax.optimization_barrier(values + (self.last,))[: len(values)]
        self.last = values
        return values if len(values) > 1 else values[0]


def wait_for(value, *others):
    return lax.optimization_barrier((value,) + others)[0]


def rows_of(one, two):
    return jnp.concatenate([one, two], axis=0)


def block_order(bits):
    order = [0]
    for bit in reversed(bits):
        order = [item ^ bit for item in order] + order
    return order


def permuted_features(value, index, bits):
    order = block_order(bits)
    width = value.shape[1] // len(order)
    return jnp.concatenate(
        [lax.dynamic_slice_in_dim(value, (index ^ item) * width, width, 1) for item in order], axis=1
    )


def rows_and_cols(one, two):
    return jnp.concatenate([one, two], axis=1)


def exchange(value, bit, size):
    return lax.ppermute(value, "dp", [(i, i ^ bit) for i in range(size)])


class Reduction:
    def __init__(self, order, sent, kept, bits, size, assemble=None):
        self.order, self.sent, self.kept, self.assemble = order, sent, kept, assemble
        self.bits, self.size, self.step = bits, size, 0
        self.total = None

    def send(self, *others):
        sent = wait_for(self.sent, *others) if others else self.sent
        self.came = exchange(sent, self.bits[self.step], self.size)
        return self

    def receive(self):
        self.came = self.order.after(self.came)
        return self

    def add(self):
        kept, came = self.kept, self.came
        self.step += 1
        if self.step == len(self.bits):
            self.total = self.order.done((self.assemble or add_total)(kept, came))
        else:
            self.sent, self.kept = self.order.done(*add_halves(kept, came))
        return self

    def advance(self):
        self.receive().add()
        if self.total is None:
            self.send()

    def finish(self):
        while self.total is None:
            self.advance()
        return self.total


def added(one, two):
    return (one.astype(jnp.float32) + two.astype(jnp.float32)).astype(jnp.bfloat16)


def per_device(
    dp_size,
    layer_input,
    cotangent,
    starts,
    pieces,
    norm_attn,
    w_query,
    w_key,
    w_value,
    w_out,
    norm_mlp,
    w_gate,
    w_up,
    w_down,
):
    rows = layer_input.shape[0]
    width = layer_input.shape[1]
    place = lax.axis_index("tensor")
    index = lax.axis_index("dp")
    bits = [1 << i for i in range(dp_size.bit_length() - 1)]
    late_bits = bits[1:] + bits[:1]
    begins = starts[0]

    block_pos = jnp.stack([(place ^ m) * rows for m in range(4)]).astype(jnp.int32)
    near_pos, far_pos = block_pos[:2], block_pos[2:]
    row_pos = (block_pos[:, None] + jnp.arange(rows, dtype=jnp.int32)[None, :]).reshape(-1)
    (cos_n, sin_n), (cos_f, sin_f) = (
        rope_tables(half) for half in (row_pos[: 2 * rows], row_pos[2 * rows :])
    )
    w_kv = jnp.concatenate([w_key, w_value], axis=1)

    def in_sequence(value):
        return jnp.concatenate(
            [lax.dynamic_slice_in_dim(value, (place ^ b) * rows, rows, 0) for b in range(4)], axis=0
        )

    def in_two(value):
        return tuple(jnp.split(value, PARTS, axis=0))

    order = Order()
    near, far = slice(0, 2 * rows), slice(2 * rows, 4 * rows)

    def chip_sum(kept, came):
        came = order.after(came)
        return order.done(*by_rows(lambda a, b: (a + b,), (kept, came), (), ((jnp.bfloat16,),)))

    x_own, cot_own = in_two(layer_input), in_two(cotangent)
    x_chip, x_core = swap_chip(x_own), swap_core(x_own)

    side = index // PAIR % 2
    units, queries = w_gate.shape[1], w_query.shape[1]
    window = -(-units // 256) * 128
    overlap = 2 * window - units
    mine = (jnp.arange(window) >= overlap) | (side == 0)
    gate_half = lax.dynamic_slice_in_dim(w_gate, side * (units - window), window, 1)
    up_half = lax.dynamic_slice_in_dim(w_up, side * (units - window), window, 1)
    up_half = jnp.where(mine[None, :], up_half, 0).astype(jnp.bfloat16)
    down_half = lax.dynamic_slice_in_dim(w_down, side * (units - window), window, 0)
    down_half = jnp.where(mine[:, None], down_half, 0).astype(jnp.bfloat16)
    gate_half, up_half, down_half, w_kv, cos_n, sin_n, cos_f, sin_f = order.done(
        gate_half, up_half, down_half, w_kv, cos_n, sin_n, cos_f, sin_f
    )
    normed_n, q_n, k_n, v_n = order.done(
        *project((*x_own, *x_core), norm_attn, w_query, w_kv, cos_n, sin_n)
    )
    x_chip = order.after(x_chip)
    cot_own_ = wait_for(cot_own, x_chip)
    cot_chip, cot_core, cot_pair = (
        swap_chip(cot_own_), swap_core(cot_own_), swap_pair(cot_own_, dp_size)
    )
    normed_f, q_f, k_f, v_f = order.done(
        *project((*x_chip, *swap_core(x_chip)), norm_attn, w_query, w_kv, cos_f, sin_f)
    )
    k_low = in_sequence(rows_of(k_n, k_f))
    v_low = in_sequence(rows_of(v_n, v_f))
    attn_f, lse_f, kept, *sent = order.done(
        *attend_forward(q_f, k_low, v_low, w_out, begins, far_pos)
    )
    came = swap_core(sent)
    cot_chip, cot_pair = order.after(cot_chip, cot_pair)
    cot_diag, cot_other, cot_pcore = (
        swap_pair(cot_chip, dp_size), swap_core(cot_chip), swap_core(cot_pair)
    )
    attn_came = swap_chip(chip_sum(kept, came))
    cot_core, cot_other, cot_pcore, q_n = order.after(cot_core, cot_other, cot_pcore, q_n)
    attn_n, lse_n, kept, *sent = order.done(
        *attend_forward(q_n, k_low, v_low, w_out, begins, near_pos)
    )
    sum_came = swap_core(sent)

    def cot_back(*cots):
        return order.done(hidden_back(order.after(cots), down_half))

    near_back_hidden = cot_back(*cot_own, *cot_core)
    cot_diag = order.after(cot_diag)
    cot_dcore = swap_core(cot_diag)
    attn_came = order.after(attn_came)
    sum_came, cot_dcore = order.after(sum_came, cot_dcore)

    def norm_mid(x, kept, core, chip, gain):
        resid = x + (kept + core + chip)
        return resid, resid * rms_inverse(resid) * gain

    resid_mid, mlp_own = order.done(
        *by_rows(
            norm_mid, (x_own, kept, sum_came, attn_came), (norm_mlp,), (jnp.float32, (jnp.bfloat16,))
        )
    )
    mlp_core, mlp_chip, mlp_pair = swap_core(mlp_own), swap_chip(mlp_own), swap_pair(mlp_own, dp_size)
    mlp_core = order.after(mlp_core)

    def feed(normed, d_hidden):
        return order.done(*feed_forward(normed, d_hidden, gate_half, up_half))

    near_hidden = feed((*mlp_own, *mlp_core), near_back_hidden)
    side_back_hidden = cot_back(*cot_chip, *cot_other, *cot_pair, *cot_pcore)
    diag_back_hidden = cot_back(*cot_diag, *cot_dcore)
    mlp_chip, mlp_pair = order.after(mlp_chip, mlp_pair)
    half = rows // 2
    mlp_diag = (
        *swap_chip((mlp_pair[0][:half],)), *swap_pair((mlp_chip[0][half:],), dp_size)
    )
    mlp_other, mlp_pcore = order.after(swap_core(mlp_chip), swap_core(mlp_pair))
    side_hidden = feed((*mlp_chip, *mlp_other, *mlp_pair, *mlp_pcore), side_back_hidden)
    mlp_diag = order.after(mlp_diag)
    mlp_dcore = order.after(swap_core(mlp_diag))
    diag_hidden = feed((*mlp_diag, *mlp_dcore), diag_back_hidden)
    hiddens = (near_hidden, side_hidden, diag_hidden)

    def in_window(kept, came):
        first = jnp.where(side == 0, kept, came)
        second = jnp.where(side == 0, came, kept)
        return jnp.concatenate([first, second[:, overlap:]], axis=1).astype(jnp.float32)

    pair_bits = [bit for bit in bits if bit != PAIR] + [PAIR]
    always = begins[0] >= 0

    def fence(step):
        def inside():
            outer_last, order.last = order.last, ()
            try:
                return step()
            finally:
                order.last = outer_last

        shapes = jax.eval_shape(inside)
        taken = order.after(always)
        results = lax.cond(
            taken,
            inside,
            lambda: jax.tree.map(lambda item: jnp.zeros(item.shape, item.dtype), shapes),
        )
        leaves, tree = jax.tree.flatten(results)
        return jax.tree.unflatten(tree, order.done(tuple(leaves)))

    def gradient(sections, order_bits, pieces=(slice(None),)):
        lefts, rights = order.after([item[0] for item in sections], [item[1] for item in sections])
        return order.done(*outer(list(zip(lefts, rights)), index, order_bits, pieces))

    cots = (
        (*cot_own, *cot_core),
        (*cot_chip, *cot_other, *cot_pair, *cot_pcore),
        (*cot_diag, *cot_dcore),
    )
    mlps = (
        (*mlp_own, *mlp_core),
        (*mlp_chip, *mlp_other, *mlp_pair, *mlp_pcore),
        (*mlp_diag, *mlp_dcore),
    )

    def mlp_gradients(lefts, which):
        sections = [(left, [right[i] for i in which]) for left, right in zip(lefts, hiddens)]
        return gradient(sections, pair_bits, [slice(i, i + 1) for i in range(len(which))])

    def reduction(sent_kept, order_bits, assemble=None):
        return Reduction(order, *sent_kept, order_bits, dp_size, assemble)

    def shares(lefts, rights, transposed=True):
        parts = order.done(*row_shares(order.after(lefts), rights, transposed, rows))
        return [(parts[i], swap_core((parts[i + 1],))) for i in range(0, len(parts), 2)]

    def total(*items):
        return order.done(*by_rows(lambda *values: (sum(values),), items, (), ((jnp.bfloat16,),)))

    class GroupSum:
        def __init__(self, which, rights, transposed):
            self.rest = rights, transposed
            self.near, self.sides, self.diag = (tuple(item[i] for i in which) for item in hiddens)

        def diag_shares(self):
            return shares(self.diag, *self.rest)[0]

        def side_shares(self):
            return shares(self.sides, *self.rest)

        def own_shares(self):
            return shares(self.near, *self.rest)[0]

    d_norm = GroupSum((1, 2), (gate_half, up_half), True)
    block_sum = GroupSum((0,), (down_half,), False)

    down = reduction(mlp_gradients(cots, (0,)), pair_bits, in_window)
    down.send()

    @fence
    def diag_and_gradients():
        kept, came = d_norm.diag_shares()
        made = mlp_gradients(mlps, (1, 2))
        return chip_sum(kept, came), made

    diag, made = diag_and_gradients
    to_pair = swap_pair(diag, dp_size)
    gate, up = (reduction(item, pair_bits, in_window) for item in (made[:2], made[2:]))

    @fence
    def other_shares():
        chip, pair = d_norm.side_shares()
        own = d_norm.own_shares()
        return order.after(chip), order.after(pair), order.after(own)

    chip, pair, own = other_shares
    came_p = swap_pair(total(pair[0], *pair[1]), dp_size)
    to_pair = order.after(to_pair)
    came_c = swap_chip(total(chip[0], *chip[1], to_pair))
    down.receive()
    gate.send(down.came)
    down.add()
    down.send()

    @fence
    def block_shares():
        def parts(lefts):
            return order.done(*row_shares(order.after(lefts), *block_sum.rest, rows))

        kept, sent = parts(block_sum.diag)
        came = swap_core((sent,))
        kept_c, sent_c, kept_p, sent_p = parts(block_sum.sides)
        diag = chip_sum(kept, came)
        came_c = swap_core((order.after(sent_c),))
        kept, sent = parts(block_sum.near)
        came_c = order.after(came_c)
        came_p = order.after(swap_core((order.after(sent_p),)))
        came = order.after(swap_core((order.after(sent),)))
        return diag, (kept_c, came_c), (kept_p, came_p), (kept, came)

    block_diag, block_chip, block_pair, block_own = block_shares
    came_c, came_p = order.after(came_c, came_p)
    to_pair = swap_pair(block_diag, dp_size)

    def back_mid(kept, core, chip, pair, resid, cot, gain):
        d_mid = cot + norm_back(kept + core + chip + pair, resid, rms_inverse(resid), gain)
        return d_mid, d_mid

    d_mid, d_own = order.done(
        *by_rows(
            back_mid,
            (own[0], own[1], came_c, came_p, resid_mid, cot_own),
            (norm_mlp,),
            (jnp.float32, (jnp.bfloat16,)),
        )
    )
    d_chip = swap_chip(d_own)

    gate.receive()
    up.send(gate.came)
    gate.add()

    @fence
    def near_back():
        d_core = order.after(swap_core(d_own))
        return d_core, order.done(
            *attend_backward(
                q_n, (*d_own, *d_core), w_out, attn_n, lse_n, k_low, v_low, cos_n,
                sin_n, begins, near_pos,
            )
        )

    d_core, (dq_n, dk_n, dv_n) = near_back
    d_chip = order.after(d_chip)
    @fence
    def out_gradient():
        d_other = order.after(swap_core(d_chip))
        sections = [((*d_own, *d_core), (attn_n,)), ((*d_chip, *d_other), (attn_f,))]
        return d_other, gradient(sections, bits)

    d_other, wout = out_gradient
    wout = reduction(wout, bits)
    down.receive()
    gate.send(down.came)
    down.add().send()
    up.receive()
    wout.send(up.came)
    up.add()
    to_pair = order.after(to_pair)
    block_c = total(block_chip[0], *block_chip[1], to_pair)
    block_p = total(block_pair[0], *block_pair[1])

    @fence
    def far_back():
        return order.done(
            *attend_backward(
                q_f, (*d_chip, *d_other), w_out, attn_f, lse_f, k_low, v_low, cos_f,
                sin_f, begins, far_pos,
            )
        )

    dq_f, dk_f, dv_f = far_back

    @fence
    def query_gradient():
        dkv_n, dkv_f = order.done(
            *key_value_rows(dk_n, dk_f, dv_n, dv_f, (cos_n, sin_n, cos_f, sin_f), block_pos)
        )
        sections = [((normed_n,), (dq_n, dkv_n)), ((normed_f,), (dq_f, dkv_f))]
        return dkv_n, dkv_f, gradient(sections, bits)

    dkv_n, dkv_f, qkv = query_gradient
    qkv = reduction(qkv, bits)
    qkv.send()
    wout.receive()
    wout.add().send()
    down.receive().add()
    gate.receive()
    up.send(gate.came)
    gate.add().send()
    in_sum = fence(lambda: chip_sum(*shares((dq_f, dkv_f), (w_query, w_kv))[0]))
    gate.receive().add()
    d_in_came = swap_chip(in_sum)
    own = fence(lambda: order.after(shares((dq_n, dkv_n), (w_query, w_kv))[0]))
    qkv.receive()
    qkv.add().send()
    wout.receive()
    up.receive()
    up.add().send()
    wout.add().send()
    d_in_came = order.after(d_in_came)

    def back_in(kept, core, chip, resid, d_mid, gain):
        return (d_mid + norm_back(kept + core + chip, resid, rms_inverse(resid), gain),)

    (x_grad,) = by_rows(
        back_in, (own[0], own[1], d_in_came, x_own, d_mid), (norm_attn,), (jnp.float32,)
    )
    x_grad = order.done(x_grad)
    qkv.receive()
    block_p = swap_pair(wait_for(block_p, qkv.came), dp_size)
    block_c = swap_chip(wait_for(block_c, qkv.came))
    qkv.add().send()
    up.receive().add()
    wout.receive().add()
    block_c, block_p = order.after(block_c, block_p)
    qkv.receive().add()
    (block_out,) = by_rows(
        lambda *items: (sum(items),),
        (resid_mid, block_own[0], block_own[1], block_c, block_p),
        (),
        (jnp.bfloat16,),
    )
    block_out = order.done(block_out)
    for item in (down, gate, up, wout, qkv):
        item.finish()
    grad_down, grad_gate, grad_up = down.total.T, gate.total, up.total
    grad_out, grad_qkv = wout.total.T, qkv.total
    queries = w_query.shape[1]
    grad_query = grad_qkv[:, :queries]
    grad_key = grad_qkv[:, queries : queries + HD]
    grad_value = grad_qkv[:, queries + HD :]

    share = width // dp_size

    def own_features(value):
        return lax.dynamic_slice_in_dim(value, index * share, share, 0).astype(jnp.float32)

    gain_attn = (
        jnp.sum(own_features(w_query) * grad_query, axis=1)
        + jnp.sum(own_features(w_kv) * grad_qkv[:, queries:], axis=1)
    ) / own_features(norm_attn)
    gain_mlp = jnp.sum(
        own_features(w_gate) * grad_gate + own_features(w_up) * grad_up, axis=1
    ) / own_features(norm_mlp)
    gains = jnp.stack([gain_attn, gain_mlp]).reshape(2, 4, share // 4)
    gains = jnp.stack([lax.dynamic_index_in_dim(gains, place ^ m, 1, False) for m in range(4)])
    gains = gains[:2] + lax.ppermute(gains[2:], "tensor", [(i, i ^ 2) for i in range(4)])
    gains = gains[0] + lax.ppermute(gains[1], "tensor", [(i, i ^ 1) for i in range(4)])

    return (
        block_out,
        x_grad,
        gains[0],
        grad_query,
        grad_key,
        grad_value,
        grad_out,
        gains[1],
        grad_gate,
        grad_up,
        grad_down,
    )


def solution(mesh):
    in_specs = (
        P(("dp", "tensor"), None),
        P(("dp", "tensor"), None),
        P("dp", None),
        P("dp"),
        P(),
        P(None, "tensor"),
        P(None, "tensor"),
        P(None, "tensor"),
        P("tensor", None),
        P(),
        P(None, "tensor"),
        P(None, "tensor"),
        P("tensor", None),
    )
    out_specs = (
        P(("dp", "tensor"), None),
        P(("dp", "tensor"), None),
        P(("dp", "tensor")),
        P("dp", "tensor"),
        P("dp", "tensor"),
        P("dp", "tensor"),
        P("tensor", "dp"),
        P(("dp", "tensor")),
        P("dp", "tensor"),
        P("dp", "tensor"),
        P("tensor", "dp"),
    )
    return jax.shard_map(
        functools.partial(per_device, mesh.shape["dp"]),
        mesh=mesh,
        in_specs=in_specs,
        out_specs=out_specs,
        check_vma=False,
    )
```
